32 devices in a mesh: frame: 8 (over z, x), patch: 4 (over y, core).
Axes of the slice: x: 2, y: 2, z: 4, core: 2. Of those that a mesh axis runs over, the one named last changes fastest.
Arguments:
- tokens: bfloat16 [8, 512, 1152], P('frame', 'patch'), may hold values from -5 to 5
- modulation: float32 [6, 1152], replicated, may hold values from -4 to 4
- spatial_qkv: bfloat16 [3456, 1152], P('patch'), may hold values from -4 to 4
- spatial_out: bfloat16 [1152, 1152], P('patch'), may hold values from -0.1875 to 0.1875
- temporal_qkv: bfloat16 [3456, 1152], P('patch'), may hold values from -4 to 4
- temporal_out: bfloat16 [1152, 1152], P('patch'), may hold values from -0.1875 to 0.1875
Outputs:
- result: bfloat16 [8, 512, 1152], P('frame', 'patch')
The draws below stay inside these ranges and needn't reach their ends.
All inputs are finite; a program needn't handle non-finite values.
Results may differ from the reference program's by a relative error of at most 0.022.
The reference program's roundings to bfloat16 on the way count: a program that leaves them out, or rounds other values in their place, can miss the bound.
Values may be sent and summed in bfloat16 or wider, within the bound.
No kernel may reach another device: no remote copies, remote signals or barrier semaphores. Data moves between devices by JAX's collectives and lax.ppermute only.
A program may use at most 64 MiB of HBM per device.

```python
import jax
import jax.numpy as jnp
from jax import lax

D = 1152
HEADS = 16
HD = 72
PT_DEV = 128
FRAMES = 8
PATCHES = 512


def projection_weights(key, spread, share_percent):
    key_query, key_key, key_value, key_factor, key_pick = jax.random.split(key, 5)
    width_scale = D ** (-0.5)
    query_cols = jax.random.normal(key_query, (D, HEADS, HD), jnp.float32) * (spread * width_scale)
    key_cols = jax.random.normal(key_key, (D, HEADS, HD), jnp.float32) * (spread * width_scale)
    value_cols = jax.random.normal(key_value, (D, HEADS, HD), jnp.float32) * width_scale
    factor = 2.0 ** jax.random.randint(key_factor, (HEADS,), 1, 4).astype(jnp.float32)
    picked = jax.random.randint(key_pick, (HEADS,), 0, 100) < share_percent
    key_cols = jnp.where(picked[None, :, None], factor[None, :, None] * query_cols, key_cols)
    stacked = jnp.stack([query_cols, key_cols, value_cols], axis=2).reshape(D, 3 * D)
    return jnp.clip(stacked, -4.0, 4.0).T.astype(jnp.bfloat16)


def draw_tokens(key, part):
    key = jax.random.fold_in(key, 11)
    values = jax.random.normal(key, (FRAMES, PATCHES, D), jnp.float32)
    return jnp.clip(values, -5.0, 5.0).astype(jnp.bfloat16)


def draw_spatial_qkv(key, part):
    key = jax.random.fold_in(key, 21)
    return projection_weights(key, 2.0, 0)


def draw_temporal_qkv(key, part):
    key = jax.random.fold_in(key, 31)
    return projection_weights(key, 2.0, 0)


def block_scale(stream_key, shape, shards, smallest, largest):
    gain = 1.0
    for axis_at, shards_of in shards:
        heights = jax.random.uniform(jax.random.fold_in(jax.random.fold_in(stream_key, 6), axis_at), (shards_of,), jnp.float32, smallest / len(shards), largest / len(shards))
        gain = gain * jnp.repeat(jnp.exp(heights), shape[axis_at] // shards_of).reshape((-1,) + (1,) * (len(shape) - 1 - axis_at))
    return gain


def normal_values(key, dims, scale, bound, cuts=(), held_as=jnp.bfloat16):
    drawn = scale * jax.random.normal(key, dims, jnp.float32)
    if cuts:
        drawn = drawn * block_scale(key, dims, cuts, -0.22, 0.18)
    return jnp.clip(drawn, -bound, bound).astype(held_as)


def setup_inputs(seed: int = 0) -> dict:
    splits = jax.random.split(jax.random.key(seed), 7)
    tokens = draw_tokens(jax.random.fold_in(splits[6], 71), 0)
    modulation = normal_values(splits[1], (6, D), 1.0, 4.0, (), jnp.float32)
    spatial_qkv = draw_spatial_qkv(jax.random.fold_in(splits[6], 71), 0)
    spatial_out = normal_values(splits[3], (D, D), D ** -0.5, 0.1875, ((0, 4),))
    temporal_qkv = draw_temporal_qkv(jax.random.fold_in(splits[6], 71), 0)
    temporal_out = normal_values(splits[5], (D, D), D ** -0.5, 0.1875, ((0, 4),))
    return {"tokens": tokens, "modulation": modulation, "spatial_qkv": spatial_qkv, "spatial_out": spatial_out, "temporal_qkv": temporal_qkv, "temporal_out": temporal_out}


def modulate(rows, shift, scale):
    values = rows.astype(jnp.float32)
    average = lax.optimization_barrier(jnp.mean(values, axis=-1, keepdims=True))
    centred = values - average
    variance = lax.optimization_barrier(jnp.mean(centred * centred, axis=-1, keepdims=True))
    normed = centred * lax.rsqrt(variance + 1e-06)
    return (normed * (1.0 + shift * 0.0 + scale) + shift).astype(jnp.bfloat16)

def attend(projected):
    query_part = projected[:, :, :, 0].astype(jnp.float32)
    key_part = projected[:, :, :, 1].astype(jnp.float32)
    value_part = projected[:, :, :, 2].astype(jnp.float32)
    scores = jnp.einsum('nqhd,nkhd->nhqk', query_part, key_part) * projected.shape[-1] ** (-0.5)
    probs = lax.optimization_barrier(jax.nn.softmax(scores, axis=-1).astype(jnp.bfloat16))
    mixed = jnp.einsum('nhqk,nkhd->nqhd', probs.astype(jnp.float32), value_part)
    return mixed.astype(jnp.bfloat16)

def reference(tokens, modulation, spatial_qkv, spatial_out, temporal_qkv, temporal_out):

    def spatial_frame(frame_rows):
        normed = modulate(frame_rows, modulation[0], modulation[1])
        projected = jnp.dot(normed, spatial_qkv.T, preferred_element_type=jnp.float32).astype(jnp.bfloat16)
        heads = attend(projected.reshape(1, PATCHES, HEADS, 3, HD)).reshape(PATCHES, D)
        update = jnp.dot(heads, spatial_out, preferred_element_type=jnp.float32)
        return (frame_rows.astype(jnp.float32) + modulation[2] * update).astype(jnp.bfloat16)
    middle = lax.map(spatial_frame, tokens)
    blocks = middle.transpose(1, 0, 2).reshape(PATCHES // PT_DEV, PT_DEV, FRAMES, D)

    def temporal_block(block_rows):
        flat_rows = block_rows.reshape(PT_DEV * FRAMES, D)
        normed = modulate(flat_rows, modulation[3], modulation[4])
        projected = jnp.dot(normed, temporal_qkv.T, preferred_element_type=jnp.float32).astype(jnp.bfloat16)
        heads = attend(projected.reshape(PT_DEV, FRAMES, HEADS, 3, HD)).reshape(PT_DEV * FRAMES, D)
        update = jnp.dot(heads, temporal_out, preferred_element_type=jnp.float32)
        summed = (flat_rows.astype(jnp.float32) + modulation[5] * update).astype(jnp.bfloat16)
        return summed.reshape(PT_DEV, FRAMES, D)
    result = lax.map(temporal_block, blocks).reshape(PATCHES, FRAMES, D)
    return result.transpose(1, 0, 2)
```

```python
import functools

import jax
import jax.numpy as jnp
from jax import lax
from jax.experimental import pallas as pl
from jax.experimental.pallas import tpu as pltpu
from jax.sharding import PartitionSpec as P

HD = 72
MIB = 1 << 20
LOG2E = 1.4426950408889634
F32 = jnp.float32
BF16 = jnp.bfloat16


def norm_rows(values, shift, scale):
    average = jnp.mean(values, axis=-1, keepdims=True)
    centred = values - average
    variance = jnp.mean(centred * centred, axis=-1, keepdims=True)
    normed = centred * lax.rsqrt(variance + 1e-06)
    return (normed * (1.0 + scale) + shift).astype(BF16)


def dot(left, right, left_dim=1, right_dim=0):
    return lax.dot_general(
        left, right, (((left_dim,), (right_dim,)), ((), ())), preferred_element_type=F32
    )


def softmax_over_rows(scores, mask=None):
    if mask is not None:
        scores = jnp.where(mask, scores, -1e30)
    top = jnp.max(scores, axis=0, keepdims=True)
    grown = jnp.exp2((scores - top) * (HD**-0.5 * LOG2E))
    total = jnp.sum(grown, axis=0, keepdims=True)
    return (grown * (1.0 / total)).astype(BF16)


def spatial_kernel(count, mod_ref, weight_ref, *refs):
    token_refs, out_refs = refs[:count], refs[count : 2 * count]
    proj_ref, heads_ref = refs[2 * count :]
    shift, scale = mod_ref[0:1, :], mod_ref[1:2, :]
    block = token_refs[0].shape[1]
    heads = weight_ref.shape[0] // (3 * HD)
    step = 2 if count % 2 == 0 else 1
    for at in range(0, count, step):
        rows = [
            norm_rows(token_refs[at + i][0].astype(F32), shift, scale) for i in range(step)
        ]
        rows = jnp.concatenate(rows, axis=0)
        proj_ref[:, at * block : (at + step) * block] = dot(weight_ref[...], rows, 1, 1)
    for head in range(heads):
        base = head * 3 * HD
        keys = proj_ref[base + HD : base + 2 * HD, :].astype(BF16).T
        values = proj_ref[base + 2 * HD : base + 3 * HD, :].astype(BF16)
        for at in range(0, count, step):
            cols = slice(at * block, (at + step) * block)
            query = proj_ref[base : base + HD, cols].astype(BF16)
            probs = softmax_over_rows(dot(keys, query))
            heads_ref[head * HD : (head + 1) * HD, cols] = dot(values, probs)
    for at in range(count):
        out_refs[at][...] = heads_ref[:, at * block : (at + 1) * block].astype(BF16)


def middle_kernel(count, pieces, mod_ref, token_ref, *refs):
    head_refs, weight_refs = refs[:count], refs[count : 2 * count]
    middle_ref, piece_refs, scratch = refs[2 * count], refs[2 * count + 1 : -1], refs[-1]
    heads = jnp.concatenate([ref[...] for ref in head_refs], axis=0)
    weights = jnp.concatenate([ref[...] for ref in weight_refs], axis=0)
    update = dot(heads.T, weights)
    middle = (token_ref[0].astype(F32) + mod_ref[2:3, :] * update).astype(BF16)
    middle_ref[...] = middle
    normed = norm_rows(middle.astype(F32), mod_ref[3:4, :], mod_ref[4:5, :])
    if pieces == 1:
        piece_refs[0][...] = normed
        return
    scratch[...] = normed
    here = lax.axis_index("frame")
    size = normed.shape[0] // pieces
    for at in range(pieces):
        start = pl.multiple_of((here ^ at) * size, size)
        piece_refs[at][...] = scratch[pl.ds(start, size), :]


def temporal_kernel(groups, pieces, cores, period, *refs):
    weight_refs = refs[:cores]
    piece_refs = refs[cores : cores + groups * pieces]
    out_refs = refs[cores + groups * pieces : -2]
    proj_ref, heads_ref = refs[-2:]
    rows = jnp.concatenate([ref[...] for ref in piece_refs], axis=0)
    block = rows.shape[0] // groups
    depth = weight_refs[0].shape[0]
    for core in range(cores):
        proj_ref[core * depth : (core + 1) * depth, :] = dot(weight_refs[core][...], rows, 1, 1)
    heads = cores * depth // (3 * HD)
    key_patch = lax.broadcasted_iota(jnp.int32, (block, block), 0) % period
    query_patch = lax.broadcasted_iota(jnp.int32, (block, block), 1) % period
    mask = key_patch == query_patch
    for head in range(heads):
        base = head * 3 * HD
        for group in range(groups):
            cols = slice(group * block, (group + 1) * block)
            query = proj_ref[base : base + HD, cols].astype(BF16)
            keys = proj_ref[base + HD : base + 2 * HD, cols].astype(BF16)
            values = proj_ref[base + 2 * HD : base + 3 * HD, cols].astype(BF16)
            probs = softmax_over_rows(dot(keys.T, query), mask)
            heads_ref[head * HD : (head + 1) * HD, cols] = dot(values, probs)
    for group in range(groups):
        out_refs[group][...] = heads_ref[:, group * block : (group + 1) * block].astype(BF16)


def update_kernel(groups, pieces, *refs):
    count = len(refs) - groups - pieces
    head_refs, weight_refs, piece_refs = refs[:groups], refs[groups:-pieces], refs[-pieces:]
    heads = jnp.concatenate([ref[...] for ref in head_refs], axis=0)
    weights = jnp.concatenate([ref[...] for ref in weight_refs], axis=0)
    update = dot(heads.T, weights).astype(BF16)
    size = update.shape[0] // pieces
    for at in range(pieces):
        piece_refs[at][...] = update[at * size : (at + 1) * size]


def result_kernel(pieces, mod_ref, middle_ref, *refs):
    piece_refs, out_ref = refs[:-1], refs[-1]
    gate = mod_ref[5:6, :]
    here = lax.axis_index("frame")
    size = middle_ref.shape[0] // pieces
    for at in range(pieces):
        start = pl.multiple_of((here ^ at) * size, size) if pieces > 1 else 0
        rows = pl.ds(start, size)
        update = piece_refs[at][...].astype(F32)
        out_ref[0, rows, :] = (middle_ref[rows, :].astype(F32) + gate * update).astype(BF16)


def call(body, operands, outs, scratch=(), flops=0, limit=24):
    moved = sum(x.size * x.dtype.itemsize for x in (*operands, *outs))
    return pl.pallas_call(
        body,
        out_shape=outs,
        in_specs=[pl.BlockSpec(memory_space=pltpu.VMEM)] * len(operands),
        out_specs=[pl.BlockSpec(memory_space=pltpu.VMEM)] * len(outs),
        scratch_shapes=list(scratch),
        compiler_params=pltpu.CompilerParams(vmem_limit_bytes=limit * MIB),
        cost_estimate=pl.CostEstimate(flops=flops, bytes_accessed=moved, transcendentals=0),
    )(*operands)


def swap(value, axis, offset):
    size = lax.axis_size(axis)
    return lax.ppermute(value, axis, [(at, at ^ offset) for at in range(size)])


def gather_patch(value):
    size = lax.axis_size("patch")
    blocks = [value] + [None] * (size - 1)
    for offset in range(2, size, 2):
        blocks[offset] = swap(value, "patch", offset)
    for offset in range(0, size, 2):
        blocks[offset + 1] = swap(blocks[offset], "patch", 1)
    return blocks


def per_device(tokens, modulation, spatial_qkv, spatial_out, temporal_qkv, temporal_out):
    _, rows, width = tokens.shape
    shard = spatial_out.shape[0]
    count, frames = lax.axis_size("patch"), lax.axis_size("frame")
    period = rows // frames
    pieces = frames if period % 16 == 0 else 1
    groups = count // 2
    shape = jax.ShapeDtypeStruct

    blocks = gather_patch(tokens)
    spatial_weights = gather_patch(spatial_out)
    temporal_pair = [temporal_qkv, swap(temporal_qkv, "patch", 1)]
    temporal_weights = gather_patch(temporal_out)

    mixed = call(
        functools.partial(spatial_kernel, count),
        (modulation, spatial_qkv, *blocks),
        [shape((shard, rows), BF16)] * count,
        [pltpu.VMEM((3 * shard, count * rows), F32), pltpu.VMEM((shard, count * rows), F32)],
        flops=2 * count * rows * 3 * shard * width,
    )
    returned = [swap(mixed[at], "patch", at) if at else mixed[0] for at in range(count)]
    middle, *parts = call(
        functools.partial(middle_kernel, count, pieces),
        (modulation, tokens, *returned, *spatial_weights),
        [shape((rows, width), BF16)] + [shape((rows // pieces, width), BF16)] * pieces,
        [pltpu.VMEM((rows, width), BF16)],
        flops=2 * rows * width * width,
    )

    def exchange_frames(parts):
        if pieces > 1:
            return [swap(parts[at], "frame", at) if at else parts[0] for at in range(pieces)]
        return [lax.all_to_all(parts[0], "frame", split_axis=0, concat_axis=0, tiled=True)]

    parts = exchange_frames(parts)
    segments = list(parts)
    for group in range(1, groups):
        segments += [swap(part, "patch", 2 * group) for part in parts]
    mixed = call(
        functools.partial(temporal_kernel, groups, pieces, 2, period),
        (*temporal_pair, *segments),
        [shape((2 * shard, rows), BF16)] * groups,
        [pltpu.VMEM((6 * shard, groups * rows), F32), pltpu.VMEM((2 * shard, groups * rows), F32)],
        flops=2 * groups * rows * 6 * shard * width,
    )
    returned = [swap(mixed[at], "patch", 2 * at) if at else mixed[0] for at in range(groups)]
    parts = call(
        functools.partial(update_kernel, groups, pieces),
        (*returned, *temporal_weights),
        [shape((rows // pieces, width), BF16)] * pieces,
        flops=2 * rows * width * width,
    )
    parts = exchange_frames(parts)
    (result,) = call(
        functools.partial(result_kernel, pieces),
        (modulation, middle, *parts),
        [shape((1, rows, width), BF16)],
    )
    return result


def solution(mesh):
    in_specs = (
        P("frame", "patch", None),
        P(),
        P("patch", None),
        P("patch", None),
        P("patch", None),
        P("patch", None),
    )
    out_specs = P("frame", "patch", None)
    return jax.shard_map(
        per_device, mesh=mesh, in_specs=in_specs, out_specs=out_specs, check_vma=False
    )
```

```python
import functools

import jax
import jax.numpy as jnp
from jax import lax
from jax.experimental import pallas as pl
from jax.experimental.pallas import tpu as pltpu
from jax.sharding import PartitionSpec as P

HD = 72
MIB = 1 << 20
LOG2E = 1.4426950408889634
F32 = jnp.float32
BF16 = jnp.bfloat16


def norm_rows(values, shift, scale):
    average = jnp.mean(values, axis=-1, keepdims=True)
    centred = values - average
    variance = jnp.mean(centred * centred, axis=-1, keepdims=True)
    normed = centred * lax.rsqrt(variance + 1e-06)
    return (normed * (1.0 + scale) + shift).astype(BF16)


def dot(left, right, left_dim=1, right_dim=0):
    return lax.dot_general(
        left, right, (((left_dim,), (right_dim,)), ((), ())), preferred_element_type=F32
    )


def softmax_over_rows(scores, mask=None):
    if mask is not None:
        scores = jnp.where(mask, scores, -1e30)
    top = jnp.max(scores, axis=0, keepdims=True)
    grown = jnp.exp2((scores - top) * (HD**-0.5 * LOG2E))
    total = jnp.sum(grown, axis=0, keepdims=True)
    return (grown * (1.0 / total)).astype(BF16)


def spatial_kernel(count, mod_ref, weight_ref, *refs):
    token_refs, out_refs = refs[:count], refs[count : 2 * count]
    proj_ref, heads_ref = refs[2 * count :]
    shift, scale = mod_ref[0:1, :], mod_ref[1:2, :]
    block = token_refs[0].shape[1]
    heads = weight_ref.shape[0] // (3 * HD)
    step = 2 if count % 2 == 0 else 1
    for at in range(0, count, step):
        rows = [
            norm_rows(token_refs[at + i][0].astype(F32), shift, scale) for i in range(step)
        ]
        rows = jnp.concatenate(rows, axis=0)
        proj_ref[:, at * block : (at + step) * block] = dot(weight_ref[...], rows, 1, 1)
    for head in range(heads):
        base = head * 3 * HD
        keys = proj_ref[base + HD : base + 2 * HD, :].astype(BF16).T
        values = proj_ref[base + 2 * HD : base + 3 * HD, :].astype(BF16)
        for at in range(0, count, step):
            cols = slice(at * block, (at + step) * block)
            query = proj_ref[base : base + HD, cols].astype(BF16)
            probs = softmax_over_rows(dot(keys, query))
            heads_ref[head * HD : (head + 1) * HD, cols] = dot(values, probs)
    for at in range(count):
        out_refs[at][...] = heads_ref[:, at * block : (at + 1) * block].astype(BF16)


def middle_kernel(count, mod_ref, token_ref, *refs):
    head_refs, weight_refs = refs[:count], refs[count : 2 * count]
    middle_ref, normed_ref = refs[2 * count :]
    heads = jnp.concatenate([ref[...] for ref in head_refs], axis=0)
    weights = jnp.concatenate([ref[...] for ref in weight_refs], axis=0)
    update = dot(heads.T, weights)
    middle = (token_ref[0].astype(F32) + mod_ref[2:3, :] * update).astype(BF16)
    middle_ref[...] = middle
    normed_ref[...] = norm_rows(middle.astype(F32), mod_ref[3:4, :], mod_ref[4:5, :])


def temporal_kernel(groups, pieces, cores, period, *refs):
    weight_refs = refs[:cores]
    piece_refs = refs[cores : cores + groups * pieces]
    out_refs = refs[cores + groups * pieces : -2]
    proj_ref, heads_ref = refs[-2:]
    rows = jnp.concatenate([ref[...] for ref in piece_refs], axis=0)
    block = rows.shape[0] // groups
    depth = weight_refs[0].shape[0]
    for core in range(cores):
        proj_ref[core * depth : (core + 1) * depth, :] = dot(weight_refs[core][...], rows, 1, 1)
    heads = cores * depth // (3 * HD)
    key_patch = lax.broadcasted_iota(jnp.int32, (block, block), 0) % period
    query_patch = lax.broadcasted_iota(jnp.int32, (block, block), 1) % period
    mask = key_patch == query_patch
    for head in range(heads):
        base = head * 3 * HD
        for group in range(groups):
            cols = slice(group * block, (group + 1) * block)
            query = proj_ref[base : base + HD, cols].astype(BF16)
            keys = proj_ref[base + HD : base + 2 * HD, cols].astype(BF16)
            values = proj_ref[base + 2 * HD : base + 3 * HD, cols].astype(BF16)
            probs = softmax_over_rows(dot(keys.T, query), mask)
            heads_ref[head * HD : (head + 1) * HD, cols] = dot(values, probs)
    for group in range(groups):
        out_refs[group][...] = heads_ref[:, group * block : (group + 1) * block].astype(BF16)


def update_kernel(groups, *refs):
    heads = jnp.concatenate([ref[...] for ref in refs[:groups]], axis=0)
    weights = jnp.concatenate([ref[...] for ref in refs[groups:-1]], axis=0)
    refs[-1][...] = dot(heads.T, weights).astype(BF16)


def result_kernel(mod_ref, middle_ref, update_ref, out_ref):
    update = update_ref[...].astype(F32)
    out_ref[0] = (middle_ref[...].astype(F32) + mod_ref[5:6, :] * update).astype(BF16)


def call(body, operands, outs, scratch=(), flops=0, limit=24):
    moved = sum(x.size * x.dtype.itemsize for x in (*operands, *outs))
    return pl.pallas_call(
        body,
        out_shape=outs,
        in_specs=[pl.BlockSpec(memory_space=pltpu.VMEM)] * len(operands),
        out_specs=[pl.BlockSpec(memory_space=pltpu.VMEM)] * len(outs),
        scratch_shapes=list(scratch),
        compiler_params=pltpu.CompilerParams(vmem_limit_bytes=limit * MIB),
        cost_estimate=pl.CostEstimate(flops=flops, bytes_accessed=moved, transcendentals=0),
    )(*operands)


def swap(value, axis, offset):
    size = lax.axis_size(axis)
    return lax.ppermute(value, axis, [(at, at ^ offset) for at in range(size)])


def after(value, *others):
    return lax.optimization_barrier((value, *others))[0]


def across(value):
    size = lax.axis_size("patch")
    return [swap(value, "patch", at) if at else value for at in range(0, size, 2)]


def both_cores(blocks):
    return [part for block in blocks for part in (block, swap(block, "patch", 1))]


def per_device(tokens, modulation, spatial_qkv, spatial_out, temporal_qkv, temporal_out):
    _, rows, width = tokens.shape
    shard = spatial_out.shape[0]
    count, frames = lax.axis_size("patch"), lax.axis_size("frame")
    period = rows // frames
    groups = count // 2
    shape = jax.ShapeDtypeStruct

    def exchange_frames(value):
        blocks = value.reshape(frames, period, width)
        blocks = lax.all_to_all(blocks, "frame", split_axis=0, concat_axis=0, tiled=True)
        return blocks.reshape(rows, width)

    sister = swap(tokens, "patch", 1)
    far = across(tokens)[1:]
    early_out = after(spatial_out, sister)
    near_weights = [spatial_out, swap(early_out, "patch", 1)]
    far_weights = across(early_out)[1:]
    blocks = [tokens, sister] + both_cores([after(block, near_weights[1]) for block in far])

    mixed = call(
        functools.partial(spatial_kernel, count),
        (modulation, spatial_qkv, *blocks),
        [shape((shard, rows), BF16)] * count,
        [pltpu.VMEM((3 * shard, count * rows), F32), pltpu.VMEM((shard, count * rows), F32)],
        flops=2 * count * rows * 3 * shard * width,
    )
    returned = list(mixed)
    for at in reversed(range(1, count)):
        returned[at] = swap(mixed[at], "patch", at)
    far_weights = both_cores([after(block, *returned) for block in far_weights])
    temporal_pair = [temporal_qkv, swap(after(temporal_qkv, returned[1]), "patch", 1)]
    temporal_weights = across(after(temporal_out, returned[1]))
    middle, part = call(
        functools.partial(middle_kernel, count),
        (modulation, tokens, *returned, *near_weights, *far_weights),
        [shape((rows, width), BF16)] * 2,
        flops=2 * rows * width * width,
    )
    part = exchange_frames(part)
    segments = across(part)
    temporal_weights = both_cores([after(block, *segments) for block in temporal_weights])
    mixed = call(
        functools.partial(temporal_kernel, groups, 1, 2, period),
        (*temporal_pair, *segments),
        [shape((2 * shard, rows), BF16)] * groups,
        [pltpu.VMEM((6 * shard, groups * rows), F32), pltpu.VMEM((2 * shard, groups * rows), F32)],
        flops=2 * groups * rows * 6 * shard * width,
    )
    returned = [swap(mixed[at], "patch", 2 * at) if at else mixed[0] for at in range(groups)]
    (update,) = call(
        functools.partial(update_kernel, groups),
        (*returned, *temporal_weights),
        [shape((rows, width), BF16)],
        flops=2 * rows * width * width,
    )
    update = exchange_frames(update)
    (result,) = call(
        result_kernel,
        (modulation, middle, update),
        [shape((1, rows, width), BF16)],
    )
    return result


def solution(mesh):
    in_specs = (
        P("frame", "patch", None),
        P(),
        P("patch", None),
        P("patch", None),
        P("patch", None),
        P("patch", None),
    )
    out_specs = P("frame", "patch", None)
    return jax.shard_map(
        per_device, mesh=mesh, in_specs=in_specs, out_specs=out_specs, check_vma=False
    )
```

```python
import functools

import jax
import jax.numpy as jnp
from jax import lax
from jax.experimental import pallas as pl
from jax.experimental.pallas import tpu as pltpu
from jax.sharding import PartitionSpec as P

HD = 72
MIB = 1 << 20
LOG2E = 1.4426950408889634
F32 = jnp.float32
BF16 = jnp.bfloat16


def norm_rows(values, shift, scale):
    average = jnp.mean(values, axis=-1, keepdims=True)
    centred = values - average
    variance = jnp.mean(centred * centred, axis=-1, keepdims=True)
    normed = centred * lax.rsqrt(variance + 1e-06)
    return (normed * (1.0 + scale) + shift).astype(BF16)


def dot(left, right, left_dim=1, right_dim=0):
    return lax.dot_general(
        left, right, (((left_dim,), (right_dim,)), ((), ())), preferred_element_type=F32
    )


def softmax_over_rows(scores, mask=None):
    if mask is not None:
        scores = jnp.where(mask, scores, -1e30)
    top = jnp.max(scores, axis=0, keepdims=True)
    grown = jnp.exp2((scores - top) * (HD**-0.5 * LOG2E))
    total = jnp.sum(grown, axis=0, keepdims=True)
    return (grown * (1.0 / total)).astype(BF16)


def project(mod_ref, weight_ref, token_refs, proj_ref):
    shift, scale = mod_ref[0:1, :], mod_ref[1:2, :]
    block = token_refs[0].shape[1]
    for at in range(0, len(token_refs), 2):
        rows = [norm_rows(ref[0].astype(F32), shift, scale) for ref in token_refs[at : at + 2]]
        rows = jnp.concatenate(rows, axis=0)
        proj_ref[:, at * block : (at + 2) * block] = dot(weight_ref[...], rows, 1, 1)


def near_kernel(mod_ref, weight_ref, own_ref, sister_ref, proj_ref):
    project(mod_ref, weight_ref, (own_ref, sister_ref), proj_ref)


def spatial_kernel(count, mod_ref, weight_ref, near_ref, *refs):
    token_refs, out_refs = refs[: count - 2], refs[count - 2 : -2]
    far_ref, heads_ref = refs[-2:]
    block = token_refs[0].shape[1]
    heads = weight_ref.shape[0] // (3 * HD)
    project(mod_ref, weight_ref, token_refs, far_ref)

    def whole(start):
        parts = [ref[start : start + HD, :].astype(BF16) for ref in (near_ref, far_ref)]
        return jnp.concatenate(parts, axis=1)

    for head in range(heads):
        base = head * 3 * HD
        queries, keys, values = (whole(base + part * HD) for part in range(3))
        keys = keys.T
        for at in range(0, count, 2):
            cols = slice(at * block, (at + 2) * block)
            probs = softmax_over_rows(dot(keys, queries[:, cols]))
            heads_ref[head * HD : (head + 1) * HD, cols] = dot(values, probs)
    for at in range(count):
        out_refs[at][...] = heads_ref[:, at * block : (at + 1) * block].astype(BF16)


def ordered(*weight_refs):
    here = lax.axis_index("patch") // 2
    parts = [ref[here ^ at] for at in range(weight_refs[0].shape[0]) for ref in weight_refs]
    return jnp.concatenate(parts, axis=0)


def middle_kernel(count, pieces, mod_ref, token_ref, own_ref, sister_ref, *refs):
    head_refs, middle_ref = refs[:count], refs[count]
    piece_refs, scratch = refs[count + 1 : -1], refs[-1]
    heads = jnp.concatenate([ref[...] for ref in head_refs], axis=0)
    weights = ordered(own_ref, sister_ref)
    update = dot(heads.T, weights)
    middle = (token_ref[0].astype(F32) + mod_ref[2:3, :] * update).astype(BF16)
    middle_ref[...] = middle
    normed = norm_rows(middle.astype(F32), mod_ref[3:4, :], mod_ref[4:5, :])
    if pieces == 1:
        piece_refs[0][...] = normed
        return
    scratch[...] = normed
    here = lax.axis_index("frame")
    size = normed.shape[0] // pieces
    for at in range(pieces):
        start = pl.multiple_of((here ^ at) * size, size)
        piece_refs[at][...] = scratch[pl.ds(start, size), :]


def join_kernel(*refs):
    size = refs[0].shape[0]
    for at, ref in enumerate(refs[:-1]):
        refs[-1][at * size : (at + 1) * size, :] = ref[...]


def temporal_kernel(groups, cores, period, *refs):
    weight_refs = refs[:cores]
    row_refs = refs[cores : cores + groups]
    out_refs = refs[cores + groups : -2]
    proj_ref, heads_ref = refs[-2:]
    rows = jnp.concatenate([ref[...] for ref in row_refs], axis=0)
    block = rows.shape[0] // groups
    depth = weight_refs[0].shape[0]
    for core in range(cores):
        proj_ref[core * depth : (core + 1) * depth, :] = dot(weight_refs[core][...], rows, 1, 1)
    heads = cores * depth // (3 * HD)
    key_patch = lax.broadcasted_iota(jnp.int32, (block, block), 0) % period
    query_patch = lax.broadcasted_iota(jnp.int32, (block, block), 1) % period
    mask = key_patch == query_patch
    for head in range(heads):
        base = head * 3 * HD
        for group in range(groups):
            cols = slice(group * block, (group + 1) * block)
            query = proj_ref[base : base + HD, cols].astype(BF16)
            keys = proj_ref[base + HD : base + 2 * HD, cols].astype(BF16)
            values = proj_ref[base + 2 * HD : base + 3 * HD, cols].astype(BF16)
            probs = softmax_over_rows(dot(keys.T, query), mask)
            heads_ref[head * HD : (head + 1) * HD, cols] = dot(values, probs)
    for group in range(groups):
        out_refs[group][...] = heads_ref[:, group * block : (group + 1) * block].astype(BF16)


def turn_kernel(pieces, *refs):
    heads = jnp.concatenate([ref[...] for ref in refs[:-pieces]], axis=0).T
    size = heads.shape[0] // pieces
    for at in range(pieces):
        refs[at - pieces][...] = heads[at * size : (at + 1) * size, :]


def result_kernel(pieces, mod_ref, middle_ref, own_ref, sister_ref, *refs):
    piece_refs, out_ref = refs[:pieces], refs[-1]
    heads = jnp.concatenate([ref[...] for ref in piece_refs], axis=0)
    change = mod_ref[5:6, :] * dot(heads, ordered(own_ref, sister_ref))
    here = lax.axis_index("frame")
    size = heads.shape[0] // pieces
    for at in range(pieces):
        start = pl.multiple_of((here ^ at) * size, size) if pieces > 1 else 0
        rows = pl.ds(start, size)
        part = change[at * size : (at + 1) * size, :]
        out_ref[0, rows, :] = (middle_ref[rows, :].astype(F32) + part).astype(BF16)


def call(body, operands, outs, scratch=(), limit=24):
    return pl.pallas_call(
        body,
        out_shape=outs,
        in_specs=[pl.BlockSpec(memory_space=pltpu.VMEM)] * len(operands),
        out_specs=[pl.BlockSpec(memory_space=pltpu.VMEM)] * len(outs),
        scratch_shapes=list(scratch),
        compiler_params=pltpu.CompilerParams(vmem_limit_bytes=limit * MIB),
        cost_estimate=pl.CostEstimate(flops=1, bytes_accessed=1, transcendentals=0),
    )(*operands)


def swap(value, axis, offset):
    size = lax.axis_size(axis)
    return lax.ppermute(value, axis, [(at, at ^ offset) for at in range(size)])


def after(value, *others):
    return lax.optimization_barrier((value, *others))[0]


def across(value):
    size = lax.axis_size("patch")
    return [swap(value, "patch", at) if at else value for at in range(0, size, 2)]


def both_cores(blocks):
    return [part for block in blocks for part in (block, swap(block, "patch", 1))]


def gather_chips(weights):
    size = lax.axis_size("patch")
    groups = [list(range(core, size, 2)) for core in range(2)]
    return lax.all_gather(weights, "patch", axis_index_groups=groups)


def per_device(tokens, modulation, spatial_qkv, spatial_out, temporal_qkv, temporal_out):
    _, rows, width = tokens.shape
    shard = spatial_out.shape[0]
    count, frames = lax.axis_size("patch"), lax.axis_size("frame")
    period = rows // frames
    pieces = frames if period % 16 == 0 else 1
    shape = jax.ShapeDtypeStruct
    parts_shape = [shape((rows // pieces, width), BF16)] * pieces

    def exchange_frames(parts):
        if pieces == 1:
            blocks = parts[0].reshape(frames, period, width)
            blocks = lax.all_to_all(blocks, "frame", split_axis=0, concat_axis=0, tiled=True)
            return [blocks.reshape(rows, width)]
        parts = list(parts)
        for at in reversed(range(1, pieces)):
            parts[at] = swap(parts[at], "frame", at)
        return parts

    sister = swap(tokens, "patch", 1)
    far = across(tokens)[1:]
    (near,) = call(
        near_kernel,
        (modulation, spatial_qkv, tokens, sister),
        [shape((3 * shard, 2 * rows), F32)],
    )
    far = both_cores([after(block, near) for block in far])
    temporal_pair = [temporal_qkv, swap(after(temporal_qkv, sister), "patch", 1)]
    spatial_weights = gather_chips(after(spatial_out, sister))
    mixed = call(
        functools.partial(spatial_kernel, count),
        (modulation, spatial_qkv, near, *far),
        [shape((shard, rows), BF16)] * count,
        [pltpu.VMEM((3 * shard, (count - 2) * rows), F32), pltpu.VMEM((shard, count * rows), F32)],
    )
    returned = list(mixed)
    for at in reversed(range(1, count)):
        returned[at] = swap(mixed[at], "patch", at)
    spatial_weights = both_cores([after(spatial_weights, *returned)])
    middle, *parts = call(
        functools.partial(middle_kernel, count, pieces),
        (modulation, tokens, *spatial_weights, *returned),
        [shape((rows, width), BF16)] + parts_shape,
        [pltpu.VMEM((rows, width), BF16)],
    )
    temporal_weights = gather_chips(after(temporal_out, middle))
    (segment,) = call(join_kernel, exchange_frames(parts), [shape((rows, width), BF16)])

    def attend(weights, segments):
        columns = len(segments) * rows
        return call(
            functools.partial(temporal_kernel, len(segments), 2, period),
            (*weights, *segments),
            [shape((2 * shard, rows), BF16)] * len(segments),
            [pltpu.VMEM((6 * shard, columns), F32), pltpu.VMEM((2 * shard, columns), F32)],
        )

    others = across(segment)[1:]
    (own,) = attend(temporal_pair, [segment])
    mixed = attend([after(block, own) for block in temporal_pair], others)
    returned = [own] + [swap(part, "patch", 2 * at + 2) for at, part in enumerate(mixed)]
    temporal_weights = both_cores([after(temporal_weights, *returned)])
    parts = call(functools.partial(turn_kernel, pieces), returned, parts_shape)
    (result,) = call(
        functools.partial(result_kernel, pieces),
        (modulation, middle, *temporal_weights, *exchange_frames(parts)),
        [shape((1, rows, width), BF16)],
    )
    return result


def solution(mesh):
    in_specs = (
        P("frame", "patch", None),
        P(),
        P("patch", None),
        P("patch", None),
        P("patch", None),
        P("patch", None),
    )
    out_specs = P("frame", "patch", None)
    return jax.shard_map(
        per_device, mesh=mesh, in_specs=in_specs, out_specs=out_specs, check_vma=False
    )
```

```python
import functools

import jax
import jax.numpy as jnp
from jax import lax
from jax.experimental import pallas as pl
from jax.experimental.pallas import tpu as pltpu
from jax.sharding import PartitionSpec as P

HD = 72
MIB = 1 << 20
LOG2E = 1.4426950408889634
F32 = jnp.float32
BF16 = jnp.bfloat16


def norm_rows(values, shift, scale):
    average = jnp.mean(values, axis=-1, keepdims=True)
    centred = values - average
    variance = jnp.mean(centred * centred, axis=-1, keepdims=True)
    normed = centred * lax.rsqrt(variance + 1e-06)
    return (normed * (1.0 + scale) + shift).astype(BF16)


def dot(left, right, left_dim=1, right_dim=0):
    return lax.dot_general(
        left, right, (((left_dim,), (right_dim,)), ((), ())), preferred_element_type=F32
    )


def softmax_over_rows(scores, mask=None):
    if mask is not None:
        scores = jnp.where(mask, scores, -1e30)
    top = jnp.max(scores, axis=0, keepdims=True)
    grown = jnp.exp2((scores - top) * (HD**-0.5 * LOG2E))
    total = jnp.sum(grown, axis=0, keepdims=True)
    return (grown * (1.0 / total)).astype(BF16)


def project(mod_ref, weight_ref, token_refs, proj_ref):
    shift, scale = mod_ref[0:1, :], mod_ref[1:2, :]
    block = token_refs[0].shape[1]
    for at in range(0, len(token_refs), 2):
        rows = [norm_rows(ref[0].astype(F32), shift, scale) for ref in token_refs[at : at + 2]]
        rows = jnp.concatenate(rows, axis=0)
        proj_ref[:, at * block : (at + 2) * block] = dot(weight_ref[...], rows, 1, 1)


def near_kernel(mod_ref, weight_ref, own_ref, sister_ref, proj_ref):
    project(mod_ref, weight_ref, (own_ref, sister_ref), proj_ref)


def spatial_kernel(count, mod_ref, weight_ref, near_ref, *refs):
    token_refs, out_refs = refs[: count - 2], refs[count - 2 : -2]
    far_ref, heads_ref = refs[-2:]
    block = token_refs[0].shape[1]
    heads = weight_ref.shape[0] // (3 * HD)
    project(mod_ref, weight_ref, token_refs, far_ref)

    def whole(start):
        parts = [ref[start : start + HD, :].astype(BF16) for ref in (near_ref, far_ref)]
        return jnp.concatenate(parts, axis=1)

    for head in range(heads):
        base = head * 3 * HD
        queries, keys, values = (whole(base + part * HD) for part in range(3))
        keys = keys.T
        for at in range(0, count, 2):
            cols = slice(at * block, (at + 2) * block)
            probs = softmax_over_rows(dot(keys, queries[:, cols]))
            heads_ref[head * HD : (head + 1) * HD, cols] = dot(values, probs)
    for at in range(count):
        out_refs[at][...] = heads_ref[:, at * block : (at + 1) * block].astype(BF16)


def middle_kernel(count, mod_ref, token_ref, *refs):
    head_refs, weight_refs = refs[:count], refs[count : 2 * count]
    middle_ref, normed_ref = refs[2 * count :]
    heads = jnp.concatenate([ref[...] for ref in head_refs], axis=0)
    weights = jnp.concatenate([ref[...] for ref in weight_refs], axis=0)
    update = dot(heads.T, weights)
    middle = (token_ref[0].astype(F32) + mod_ref[2:3, :] * update).astype(BF16)
    middle_ref[...] = middle
    normed_ref[...] = norm_rows(middle.astype(F32), mod_ref[3:4, :], mod_ref[4:5, :])


def temporal_kernel(groups, cores, period, *refs):
    weight_refs = refs[:cores]
    row_refs = refs[cores : cores + groups]
    out_refs = refs[cores + groups : -2]
    proj_ref, heads_ref = refs[-2:]
    rows = jnp.concatenate([ref[...] for ref in row_refs], axis=0)
    block = rows.shape[0] // groups
    depth = weight_refs[0].shape[0]
    for core in range(cores):
        proj_ref[core * depth : (core + 1) * depth, :] = dot(weight_refs[core][...], rows, 1, 1)
    heads = cores * depth // (3 * HD)
    key_patch = lax.broadcasted_iota(jnp.int32, (block, block), 0) % period
    query_patch = lax.broadcasted_iota(jnp.int32, (block, block), 1) % period
    mask = key_patch == query_patch
    for head in range(heads):
        base = head * 3 * HD
        for group in range(groups):
            cols = slice(group * block, (group + 1) * block)
            query = proj_ref[base : base + HD, cols].astype(BF16)
            keys = proj_ref[base + HD : base + 2 * HD, cols].astype(BF16)
            values = proj_ref[base + 2 * HD : base + 3 * HD, cols].astype(BF16)
            probs = softmax_over_rows(dot(keys.T, query), mask)
            heads_ref[head * HD : (head + 1) * HD, cols] = dot(values, probs)
    for group in range(groups):
        out_refs[group][...] = heads_ref[:, group * block : (group + 1) * block].astype(BF16)


def turn_kernel(*refs):
    refs[-1][...] = jnp.concatenate([ref[...] for ref in refs[:-1]], axis=0).T


def result_kernel(mod_ref, middle_ref, heads_ref, *refs):
    weights = jnp.concatenate([ref[...] for ref in refs[:-1]], axis=0)
    update = dot(heads_ref[...], weights)
    refs[-1][0] = (middle_ref[...].astype(F32) + mod_ref[5:6, :] * update).astype(BF16)


def call(body, operands, outs, scratch=(), limit=24):
    return pl.pallas_call(
        body,
        out_shape=outs,
        in_specs=[pl.BlockSpec(memory_space=pltpu.VMEM)] * len(operands),
        out_specs=[pl.BlockSpec(memory_space=pltpu.VMEM)] * len(outs),
        scratch_shapes=list(scratch),
        compiler_params=pltpu.CompilerParams(vmem_limit_bytes=limit * MIB),
        cost_estimate=pl.CostEstimate(flops=1, bytes_accessed=1, transcendentals=0),
    )(*operands)


def swap(value, axis, offset):
    size = lax.axis_size(axis)
    return lax.ppermute(value, axis, [(at, at ^ offset) for at in range(size)])


def after(value, *others):
    return lax.optimization_barrier((value, *others))[0]


def across(value):
    size = lax.axis_size("patch")
    return [swap(value, "patch", at) if at else value for at in range(0, size, 2)]


def both_cores(blocks):
    return [part for block in blocks for part in (block, swap(block, "patch", 1))]


def per_device(tokens, modulation, spatial_qkv, spatial_out, temporal_qkv, temporal_out):
    _, rows, width = tokens.shape
    shard = spatial_out.shape[0]
    count, frames = lax.axis_size("patch"), lax.axis_size("frame")
    period = rows // frames
    groups = count // 2
    shape = jax.ShapeDtypeStruct

    def exchange_frames(value):
        blocks = value.reshape(frames, period, width)
        blocks = lax.all_to_all(blocks, "frame", split_axis=0, concat_axis=0, tiled=True)
        return blocks.reshape(rows, width)

    sister = swap(tokens, "patch", 1)
    far = across(tokens)[1:]
    early_out = after(spatial_out, sister)
    near_weights = [spatial_out, swap(early_out, "patch", 1)]
    far_weights = across(early_out)[1:]
    temporal_pair = [temporal_qkv, swap(after(temporal_qkv, near_weights[1]), "patch", 1)]
    (near,) = call(
        near_kernel,
        (modulation, spatial_qkv, tokens, sister),
        [shape((3 * shard, 2 * rows), F32)],
    )
    far = both_cores([after(block, near) for block in far])
    mixed = call(
        functools.partial(spatial_kernel, count),
        (modulation, spatial_qkv, near, *far),
        [shape((shard, rows), BF16)] * count,
        [pltpu.VMEM((3 * shard, (count - 2) * rows), F32), pltpu.VMEM((shard, count * rows), F32)],
    )
    returned = list(mixed)
    for at in reversed(range(1, count)):
        returned[at] = swap(mixed[at], "patch", at)
    far_weights = both_cores([after(block, *returned[2:]) for block in far_weights])
    late_out = after(temporal_out, *returned)
    late_near = [temporal_out, swap(late_out, "patch", 1)]
    late_far = across(late_out)[1:]
    middle, part = call(
        functools.partial(middle_kernel, count),
        (modulation, tokens, *returned, *near_weights, *far_weights),
        [shape((rows, width), BF16)] * 2,
    )
    segments = across(exchange_frames(part))
    mixed = call(
        functools.partial(temporal_kernel, groups, 2, period),
        (*temporal_pair, *segments),
        [shape((2 * shard, rows), BF16)] * groups,
        [pltpu.VMEM((6 * shard, groups * rows), F32), pltpu.VMEM((2 * shard, groups * rows), F32)],
    )
    late_far = both_cores([after(block, mixed[0]) for block in late_far])
    returned = [swap(mixed[at], "patch", 2 * at) if at else mixed[0] for at in range(groups)]
    (turned,) = call(turn_kernel, returned, [shape((rows, width), BF16)])
    (result,) = call(
        result_kernel,
        (modulation, middle, exchange_frames(turned), *late_near, *late_far),
        [shape((1, rows, width), BF16)],
    )
    return result


def solution(mesh):
    in_specs = (
        P("frame", "patch", None),
        P(),
        P("patch", None),
        P("patch", None),
        P("patch", None),
        P("patch", None),
    )
    out_specs = P("frame", "patch", None)
    return jax.shard_map(
        per_device, mesh=mesh, in_specs=in_specs, out_specs=out_specs, check_vma=False
    )
```

```python
import functools

import jax
import jax.numpy as jnp
from jax import lax
from jax.experimental import pallas as pl
from jax.experimental.pallas import tpu as pltpu
from jax.sharding import PartitionSpec as P

HD = 72
MIB = 1 << 20
LOG2E = 1.4426950408889634
F32 = jnp.float32
BF16 = jnp.bfloat16


def norm_rows(values, shift, scale):
    average = jnp.mean(values, axis=-1, keepdims=True)
    centred = values - average
    variance = jnp.mean(centred * centred, axis=-1, keepdims=True)
    normed = centred * lax.rsqrt(variance + 1e-06)
    return (normed * (1.0 + scale) + shift).astype(BF16)


def dot(left, right, left_dim=1, right_dim=0):
    return lax.dot_general(
        left, right, (((left_dim,), (right_dim,)), ((), ())), preferred_element_type=F32
    )


def softmax_over_rows(scores, mask=None):
    if mask is not None:
        scores = jnp.where(mask, scores, -1e30)
    top = jnp.max(scores, axis=0, keepdims=True)
    grown = jnp.exp2((scores - top) * (HD**-0.5 * LOG2E))
    total = jnp.sum(grown, axis=0, keepdims=True)
    return (grown * (1.0 / total)).astype(BF16)


def project(mod_ref, weight_ref, token_refs, proj_ref):
    shift, scale = mod_ref[0:1, :], mod_ref[1:2, :]
    block = token_refs[0].shape[1]
    for at in range(0, len(token_refs), 2):
        rows = [norm_rows(ref[0].astype(F32), shift, scale) for ref in token_refs[at : at + 2]]
        rows = jnp.concatenate(rows, axis=0)
        proj_ref[:, at * block : (at + 2) * block] = dot(weight_ref[...], rows, 1, 1)


def near_kernel(mod_ref, weight_ref, own_ref, sister_ref, proj_ref):
    project(mod_ref, weight_ref, (own_ref, sister_ref), proj_ref)


def spatial_kernel(count, mod_ref, weight_ref, near_ref, *refs):
    token_refs, (kept_ref, sent_ref, far_ref, heads_ref) = refs[: count - 2], refs[count - 2 :]
    block = token_refs[0].shape[1]
    heads = weight_ref.shape[0] // (3 * HD)
    project(mod_ref, weight_ref, token_refs, far_ref)

    def whole(start):
        parts = [ref[start : start + HD, :].astype(BF16) for ref in (near_ref, far_ref)]
        return jnp.concatenate(parts, axis=1)

    for head in range(heads):
        base = head * 3 * HD
        queries, keys, values = (whole(base + part * HD) for part in range(3))
        keys = keys.T
        for at in range(0, count, 2):
            cols = slice(at * block, (at + 2) * block)
            probs = softmax_over_rows(dot(keys, queries[:, cols]))
            heads_ref[head * HD : (head + 1) * HD, cols] = dot(values, probs)
    for at in range(count):
        out_ref = (kept_ref, sent_ref)[at % 2]
        cols = slice(at // 2 * block, (at // 2 + 1) * block)
        out_ref[:, cols] = heads_ref[:, at * block : (at + 1) * block].astype(BF16)


def partial_kernel(first, *refs):
    head_refs, weight_refs, out_refs = refs[:2], refs[2:4], refs[4:]
    weights = jnp.concatenate([ref[...] for ref in weight_refs], axis=0)
    block = out_refs[0].shape[0]
    for at, ref in enumerate(out_refs, first):
        cols = slice(at * block, (at + 1) * block)
        heads = jnp.concatenate([heads[:, cols] for heads in head_refs], axis=0)
        ref[...] = dot(heads.T, weights).astype(ref.dtype)


def middle_kernel(mod_ref, token_ref, *refs):
    middle_ref, normed_ref = refs[-2:]
    update = sum(ref[...].astype(F32) for ref in refs[:-2])
    middle = (token_ref[0].astype(F32) + mod_ref[2:3, :] * update).astype(BF16)
    middle_ref[...] = middle
    normed_ref[...] = norm_rows(middle.astype(F32), mod_ref[3:4, :], mod_ref[4:5, :])


def temporal_kernel(groups, period, *refs):
    weight_refs, output_refs, row_refs = refs[:2], refs[2:4], refs[4 : 4 + groups]
    update_refs = refs[4 + groups : -2]
    proj_ref, heads_ref = refs[-2:]
    rows = jnp.concatenate([ref[...] for ref in row_refs], axis=0)
    block = rows.shape[0] // groups
    depth = weight_refs[0].shape[0]
    for core in range(2):
        proj_ref[core * depth : (core + 1) * depth, :] = dot(weight_refs[core][...], rows, 1, 1)
    heads = 2 * depth // (3 * HD)
    key_patch = lax.broadcasted_iota(jnp.int32, (block, block), 0) % period
    query_patch = lax.broadcasted_iota(jnp.int32, (block, block), 1) % period
    mask = key_patch == query_patch
    for head in range(heads):
        base = head * 3 * HD
        for group in range(groups):
            cols = slice(group * block, (group + 1) * block)
            query = proj_ref[base : base + HD, cols].astype(BF16)
            keys = proj_ref[base + HD : base + 2 * HD, cols].astype(BF16)
            values = proj_ref[base + 2 * HD : base + 3 * HD, cols].astype(BF16)
            probs = softmax_over_rows(dot(keys.T, query), mask)
            heads_ref[head * HD : (head + 1) * HD, cols] = dot(values, probs)
    weights = jnp.concatenate([ref[...] for ref in output_refs], axis=0)
    for group, ref in enumerate(update_refs):
        mixed = heads_ref[:, group * block : (group + 1) * block].astype(BF16)
        ref[...] = dot(mixed.T, weights).astype(ref.dtype)


def sum_kernel(*refs):
    refs[-1][...] = sum(ref[...].astype(F32) for ref in refs[:-1]).astype(BF16)


def result_kernel(mod_ref, middle_ref, update_ref, out_ref):
    update = update_ref[...].astype(F32)
    out_ref[0] = (middle_ref[...].astype(F32) + mod_ref[5:6, :] * update).astype(BF16)


def call(body, operands, outs, scratch=(), limit=24):
    return pl.pallas_call(
        body,
        out_shape=outs,
        in_specs=[pl.BlockSpec(memory_space=pltpu.VMEM)] * len(operands),
        out_specs=[pl.BlockSpec(memory_space=pltpu.VMEM)] * len(outs),
        scratch_shapes=list(scratch),
        compiler_params=pltpu.CompilerParams(vmem_limit_bytes=limit * MIB),
        cost_estimate=pl.CostEstimate(flops=1, bytes_accessed=1, transcendentals=0),
    )(*operands)


def swap(value, axis, offset):
    size = lax.axis_size(axis)
    return lax.ppermute(value, axis, [(at, at ^ offset) for at in range(size)])


def after(value, *others):
    return lax.optimization_barrier((value, *others))[0]


def across(value):
    size = lax.axis_size("patch")
    return [swap(value, "patch", at) if at else value for at in range(0, size, 2)]


def both_cores(blocks):
    return [part for block in blocks for part in (block, swap(block, "patch", 1))]


def per_device(tokens, modulation, spatial_qkv, spatial_out, temporal_qkv, temporal_out):
    _, rows, width = tokens.shape
    shard = spatial_out.shape[0]
    count, frames = lax.axis_size("patch"), lax.axis_size("frame")
    period = rows // frames
    groups = count // 2
    shape = jax.ShapeDtypeStruct

    def exchange_frames(value):
        blocks = value.reshape(frames, period, width)
        blocks = lax.all_to_all(blocks, "frame", split_axis=0, concat_axis=0, tiled=True)
        return blocks.reshape(rows, width)

    def with_sister(weights, *others):
        return [weights, swap(after(weights, *others), "patch", 1)]

    def return_far(parts):
        return [swap(part, "patch", 2 * at) for at, part in enumerate(parts, 1)]

    own_update = [shape((rows, width), F32)]
    far_updates = [shape((rows, width), BF16)] * (groups - 1)

    sister = swap(tokens, "patch", 1)
    far = across(tokens)[1:]
    (near,) = call(
        near_kernel,
        (modulation, spatial_qkv, tokens, sister),
        [shape((3 * shard, 2 * rows), F32)],
    )
    far = both_cores([after(block, near) for block in far])
    out_pair = with_sister(spatial_out, *far)
    temporal_pair = with_sister(temporal_qkv, *far)
    late_pair = with_sister(temporal_out, *far)

    kept, sent = call(
        functools.partial(spatial_kernel, count),
        (modulation, spatial_qkv, near, *far),
        [shape((shard, groups * rows), BF16)] * 2,
        [pltpu.VMEM((3 * shard, (count - 2) * rows), F32), pltpu.VMEM((shard, count * rows), F32)],
    )
    heads = (kept, swap(sent, "patch", 1))
    parts = call(functools.partial(partial_kernel, 1), (*heads, *out_pair), far_updates)
    own = call(functools.partial(partial_kernel, 0), (*heads, *out_pair), own_update)
    middle, part = call(
        middle_kernel,
        (modulation, tokens, *own, *return_far(parts)),
        [shape((rows, width), BF16)] * 2,
    )

    def attend(segments, updates):
        columns = len(segments) * rows
        return call(
            functools.partial(temporal_kernel, len(segments), period),
            (*temporal_pair, *late_pair, *segments),
            updates,
            [pltpu.VMEM((6 * shard, columns), F32), pltpu.VMEM((2 * shard, columns), F32)],
        )

    segments = across(exchange_frames(part))
    own = attend(segments[:1], own_update)
    parts = attend(segments[1:], far_updates)
    (update,) = call(sum_kernel, (*own, *return_far(parts)), [shape((rows, width), BF16)])
    (result,) = call(
        result_kernel,
        (modulation, middle, exchange_frames(update)),
        [shape((1, rows, width), BF16)],
    )
    return result


def solution(mesh):
    in_specs = (
        P("frame", "patch", None),
        P(),
        P("patch", None),
        P("patch", None),
        P("patch", None),
        P("patch", None),
    )
    out_specs = P("frame", "patch", None)
    return jax.shard_map(
        per_device, mesh=mesh, in_specs=in_specs, out_specs=out_specs, check_vma=False
    )
```

```python
import functools

import jax
import jax.numpy as jnp
from jax import lax
from jax.experimental import pallas as pl
from jax.experimental.pallas import tpu as pltpu
from jax.sharding import PartitionSpec as P

HD = 72
MIB = 1 << 20
LOG2E = 1.4426950408889634
F32 = jnp.float32
BF16 = jnp.bfloat16


def norm_rows(values, shift, scale):
    average = jnp.mean(values, axis=-1, keepdims=True)
    centred = values - average
    variance = jnp.mean(centred * centred, axis=-1, keepdims=True)
    normed = centred * lax.rsqrt(variance + 1e-06)
    return (normed * (1.0 + scale) + shift).astype(BF16)


def dot(left, right, left_dim=1, right_dim=0):
    return lax.dot_general(
        left, right, (((left_dim,), (right_dim,)), ((), ())), preferred_element_type=F32
    )


def softmax_over_rows(scores, mask=None):
    if mask is not None:
        scores = jnp.where(mask, scores, -1e30)
    top = jnp.max(scores, axis=0, keepdims=True)
    grown = jnp.exp2((scores - top) * (HD**-0.5 * LOG2E))
    total = jnp.sum(grown, axis=0, keepdims=True)
    return (grown * (1.0 / total)).astype(BF16)


def project(mod_ref, weight_ref, token_refs, proj_ref):
    shift, scale = mod_ref[0:1, :], mod_ref[1:2, :]
    block = token_refs[0].shape[1]
    for at in range(0, len(token_refs), 2):
        rows = [norm_rows(ref[0].astype(F32), shift, scale) for ref in token_refs[at : at + 2]]
        rows = jnp.concatenate(rows, axis=0)
        proj_ref[:, at * block : (at + 2) * block] = dot(weight_ref[...], rows, 1, 1)


def near_kernel(mod_ref, weight_ref, own_ref, sister_ref, proj_ref):
    project(mod_ref, weight_ref, (own_ref, sister_ref), proj_ref)


def spatial_kernel(count, mod_ref, weight_ref, near_ref, *refs):
    token_refs, (kept_ref, sent_ref, far_ref, heads_ref) = refs[: count - 2], refs[count - 2 :]
    block = token_refs[0].shape[1]
    heads = weight_ref.shape[0] // (3 * HD)
    project(mod_ref, weight_ref, token_refs, far_ref)

    def whole(start):
        parts = [ref[start : start + HD, :].astype(BF16) for ref in (near_ref, far_ref)]
        return jnp.concatenate(parts, axis=1)

    for head in range(heads):
        base = head * 3 * HD
        queries, keys, values = (whole(base + part * HD) for part in range(3))
        keys = keys.T
        for at in range(0, count, 2):
            cols = slice(at * block, (at + 2) * block)
            probs = softmax_over_rows(dot(keys, queries[:, cols]))
            heads_ref[head * HD : (head + 1) * HD, cols] = dot(values, probs)
    for at in range(count):
        out_ref = (kept_ref, sent_ref)[at % 2]
        cols = slice(at // 2 * block, (at // 2 + 1) * block)
        out_ref[:, cols] = heads_ref[:, at * block : (at + 1) * block].astype(BF16)


def halves(value, size):
    return [
        jnp.concatenate(
            [value[at : at + size] for at in range(first * size, value.shape[0], 2 * size)], axis=0
        )
        for first in range(2)
    ]


def of_this_half(value, size):
    even, odd = halves(value, size)
    first = lax.axis_index("frame") % 2 == 0
    return jnp.where(first, even, odd), jnp.where(first, odd, even)


def partial_kernel(first, period, *refs):
    head_refs, weight_refs, out_refs = refs[:2], refs[2:4], refs[4:]
    weights = jnp.concatenate([ref[...] for ref in weight_refs], axis=0)
    block = 2 * out_refs[0].shape[0]
    for at in range(len(out_refs) // 2):
        cols = slice((first + at) * block, (first + at + 1) * block)
        heads = jnp.concatenate([ref[:, cols] for ref in head_refs], axis=0)
        for ref, part in zip(
            out_refs[2 * at : 2 * at + 2], of_this_half(dot(heads.T, weights), period)
        ):
            ref[...] = part.astype(ref.dtype)


def middle_kernel(pieces, groups, mod_ref, own_ref, paired_ref, *refs):
    update_refs = (refs[:groups], refs[groups : 2 * groups])
    kept_ref, sent_ref, *piece_refs, scratch = refs[2 * groups :]
    _, period, width = kept_ref.shape
    for at, (token_ref, middle_ref) in enumerate(((own_ref, kept_ref), (paired_ref, sent_ref))):
        update = sum(ref[...].astype(F32) for ref in update_refs[at])
        tokens = of_this_half(token_ref[0].astype(F32), period)[0]
        middle = (tokens + mod_ref[2:3, :] * update).astype(BF16)
        normed = norm_rows(middle.astype(F32), mod_ref[3:4, :], mod_ref[4:5, :])
        for piece in range(pieces):
            rows = slice(piece * period, (piece + 1) * period)
            middle_ref[piece] = middle[rows]
            scratch[piece, at * period : (at + 1) * period, :] = normed[rows]
    here = lax.axis_index("frame") // 2
    for at, ref in enumerate(piece_refs):
        ref[...] = scratch[here ^ at]


def join_kernel(*refs):
    size = refs[0].shape[0]
    for at, ref in enumerate(refs[:-1]):
        refs[-1][at * size : (at + 1) * size, :] = ref[...]


def temporal_kernel(groups, period, *refs):
    weight_refs, output_refs, row_refs = refs[:2], refs[2:4], refs[4 : 4 + groups]
    update_refs = refs[4 + groups : -2]
    proj_ref, heads_ref = refs[-2:]
    rows = jnp.concatenate([ref[...] for ref in row_refs], axis=0)
    block = rows.shape[0] // groups
    depth = weight_refs[0].shape[0]
    for core in range(2):
        proj_ref[core * depth : (core + 1) * depth, :] = dot(weight_refs[core][...], rows, 1, 1)
    heads = 2 * depth // (3 * HD)
    key_patch = lax.broadcasted_iota(jnp.int32, (block, block), 0) % period
    query_patch = lax.broadcasted_iota(jnp.int32, (block, block), 1) % period
    mask = key_patch == query_patch
    for head in range(heads):
        base = head * 3 * HD
        for group in range(groups):
            cols = slice(group * block, (group + 1) * block)
            query = proj_ref[base : base + HD, cols].astype(BF16)
            keys = proj_ref[base + HD : base + 2 * HD, cols].astype(BF16)
            values = proj_ref[base + 2 * HD : base + 3 * HD, cols].astype(BF16)
            probs = softmax_over_rows(dot(keys.T, query), mask)
            heads_ref[head * HD : (head + 1) * HD, cols] = dot(values, probs)
    weights = jnp.concatenate([ref[...] for ref in output_refs], axis=0)
    for group in range(groups):
        mixed = heads_ref[:, group * block : (group + 1) * block].astype(BF16)
        parts = halves(dot(mixed.T, weights), period)
        for ref, part in zip(update_refs[2 * group : 2 * group + 2], parts):
            ref[...] = part.astype(ref.dtype)


def sum_kernel(pieces, groups, *refs):
    update_refs, piece_refs = (refs[:groups], refs[groups : 2 * groups]), refs[2 * groups :]
    period = piece_refs[0].shape[0] // 2
    for at, parts in enumerate(update_refs):
        update = sum(ref[...].astype(F32) for ref in parts).astype(BF16)
        for piece, ref in enumerate(piece_refs):
            rows = update[piece * period : (piece + 1) * period]
            ref[at * period : (at + 1) * period, :] = rows


def result_kernel(pieces, mod_ref, kept_ref, other_ref, *refs):
    piece_refs, out_ref = refs[:-1], refs[-1]
    period = kept_ref.shape[1]
    here = lax.axis_index("frame")
    for at, ref in enumerate(piece_refs):
        there = here // 2 ^ at
        for half, middle_ref in enumerate((kept_ref, other_ref)):
            update = ref[half * period : (half + 1) * period, :].astype(F32)
            middle = middle_ref[there].astype(F32)
            out_ref[2 * there + (here % 2 ^ half)] = (middle + mod_ref[5:6, :] * update).astype(
                BF16
            )


def call(body, operands, outs, scratch=(), limit=24):
    return pl.pallas_call(
        body,
        out_shape=outs,
        in_specs=[pl.BlockSpec(memory_space=pltpu.VMEM)] * len(operands),
        out_specs=[pl.BlockSpec(memory_space=pltpu.VMEM)] * len(outs),
        scratch_shapes=list(scratch),
        compiler_params=pltpu.CompilerParams(vmem_limit_bytes=limit * MIB),
        cost_estimate=pl.CostEstimate(flops=1, bytes_accessed=1, transcendentals=0),
    )(*operands)


def swap(value, axis, offset):
    size = lax.axis_size(axis)
    return lax.ppermute(value, axis, [(at, at ^ offset) for at in range(size)])


def after(value, *others):
    return lax.optimization_barrier((value, *others))[0]


def across(value):
    size = lax.axis_size("patch")
    return [swap(value, "patch", at) if at else value for at in range(0, size, 2)]


def both_cores(blocks):
    return [part for block in blocks for part in (block, swap(block, "patch", 1))]


def swap_diagonal(value, offset):
    frames, size = lax.axis_size("frame"), lax.axis_size("patch")
    pairs = [
        (frame * size + at, (frame ^ 1) * size + (at ^ offset))
        for frame in range(frames)
        for at in range(size)
    ]
    return lax.ppermute(value, ("frame", "patch"), pairs)


def per_device(tokens, modulation, spatial_qkv, spatial_out, temporal_qkv, temporal_out):
    _, rows, width = tokens.shape
    shard = spatial_out.shape[0]
    count, frames = lax.axis_size("patch"), lax.axis_size("frame")
    period = rows // frames
    pieces, groups = frames // 2, count // 2
    shape = jax.ShapeDtypeStruct

    def with_sister(weights, *others):
        return [weights, swap(after(weights, *others), "patch", 1)]

    def exchange_frames(parts):
        parts = list(parts)
        for at in reversed(range(1, pieces)):
            parts[at] = swap(parts[at], "frame", 2 * at)
        return parts

    def return_updates(own, far):
        kept, sent = own
        same = [swap(part, "patch", 2 * at) for at, part in enumerate(far[::2], 1)]
        diagonal = [swap_diagonal(part, 2 * at) for at, part in enumerate(far[1::2], 1)]
        return [kept, *same, swap(sent, "frame", 1), *diagonal]

    def halves_shape(dtype):
        return shape((rows // 2, width), dtype)

    own_shapes = [halves_shape(F32), halves_shape(BF16)]
    far_shapes = [halves_shape(BF16)] * (2 * groups - 2)
    piece_shapes = [shape((2 * period, width), BF16)] * pieces

    sister = swap(tokens, "patch", 1)
    far = across(tokens)[1:]
    (near,) = call(
        near_kernel,
        (modulation, spatial_qkv, tokens, sister),
        [shape((3 * shard, 2 * rows), F32)],
    )
    paired = swap(after(tokens, sister), "frame", 1)
    far = both_cores([after(block, near, paired) for block in far])
    out_pair = with_sister(spatial_out, *far)
    temporal_pair = with_sister(temporal_qkv, *far)

    kept, sent = call(
        functools.partial(spatial_kernel, count),
        (modulation, spatial_qkv, near, *far),
        [shape((shard, groups * rows), BF16)] * 2,
        [pltpu.VMEM((3 * shard, (count - 2) * rows), F32), pltpu.VMEM((shard, count * rows), F32)],
    )
    heads = (kept, swap(sent, "patch", 1), *out_pair)
    far_parts = call(functools.partial(partial_kernel, 1, period), heads, far_shapes)
    own_parts = call(functools.partial(partial_kernel, 0, period), heads, own_shapes)
    late_pair = with_sister(temporal_out, far_parts[0])
    middle, middle_sent, *parts = call(
        functools.partial(middle_kernel, pieces, groups),
        (modulation, tokens, paired, *return_updates(own_parts, far_parts)),
        [shape((pieces, period, width), BF16)] * 2 + piece_shapes,
        [pltpu.VMEM((pieces, 2 * period, width), BF16)],
    )
    (segment,) = call(join_kernel, exchange_frames(parts), [shape((rows, width), BF16)])

    def attend(segments, shapes):
        columns = len(segments) * rows
        return call(
            functools.partial(temporal_kernel, len(segments), period),
            (*temporal_pair, *late_pair, *segments),
            shapes,
            [pltpu.VMEM((6 * shard, columns), F32), pltpu.VMEM((2 * shard, columns), F32)],
        )

    segments = across(segment)
    middle_other = swap(after(middle_sent, segment), "frame", 1)
    own_parts = attend([segment], own_shapes)
    far_parts = attend([after(block, own_parts[0]) for block in segments[1:]], far_shapes)
    parts = call(
        functools.partial(sum_kernel, pieces, groups),
        return_updates(own_parts, far_parts),
        piece_shapes,
    )
    (result,) = call(
        functools.partial(result_kernel, pieces),
        (modulation, middle, middle_other, *exchange_frames(parts)),
        [shape((frames, period, width), BF16)],
    )
    return result.reshape(1, rows, width)


def solution(mesh):
    in_specs = (
        P("frame", "patch", None),
        P(),
        P("patch", None),
        P("patch", None),
        P("patch", None),
        P("patch", None),
    )
    out_specs = P("frame", "patch", None)
    return jax.shard_map(
        per_device, mesh=mesh, in_specs=in_specs, out_specs=out_specs, check_vma=False
    )
```

```python
import functools

import jax
import jax.numpy as jnp
from jax import lax
from jax.experimental import pallas as pl
from jax.experimental.pallas import tpu as pltpu
from jax.sharding import PartitionSpec as P

HD = 72
MIB = 1 << 20
LOG2E = 1.4426950408889634
F32 = jnp.float32
BF16 = jnp.bfloat16


def norm_rows(values, shift, scale):
    average = jnp.mean(values, axis=-1, keepdims=True)
    centred = values - average
    variance = jnp.mean(centred * centred, axis=-1, keepdims=True)
    normed = centred * lax.rsqrt(variance + 1e-06)
    return (normed * (1.0 + scale) + shift).astype(BF16)


def dot(left, right, left_dim=1, right_dim=0):
    return lax.dot_general(
        left, right, (((left_dim,), (right_dim,)), ((), ())), preferred_element_type=F32
    )


def attend(keys, query, values, mask=None):
    scores = dot(keys, query)
    if mask is not None:
        scores = jnp.where(mask, scores, -1e30)
    top = jnp.max(scores, axis=0, keepdims=True)
    weights = jnp.exp2((scores - top) * (HD**-0.5 * LOG2E)).astype(BF16)
    ones = jnp.ones((8, values.shape[1]), F32)
    mixed = dot(jnp.concatenate([values, ones], axis=0).astype(BF16), weights)
    return mixed[:HD] * (1.0 / mixed[HD : HD + 1])


def project(mod_ref, weight_ref, token_refs, proj_ref):
    shift, scale = mod_ref[0:1, :], mod_ref[1:2, :]
    block = token_refs[0].shape[1]
    for at in range(0, len(token_refs), 2):
        rows = [norm_rows(ref[0].astype(F32), shift, scale) for ref in token_refs[at : at + 2]]
        rows = jnp.concatenate(rows, axis=0)
        proj_ref[:, at * block : (at + 2) * block] = dot(weight_ref[...], rows, 1, 1)


def near_kernel(mod_ref, weight_ref, own_ref, sister_ref, proj_ref):
    project(mod_ref, weight_ref, (own_ref, sister_ref), proj_ref)


def spatial_kernel(count, mod_ref, weight_ref, near_ref, *refs):
    token_refs, (kept_ref, sent_ref, far_ref, heads_ref) = refs[: count - 2], refs[count - 2 :]
    block = token_refs[0].shape[1]
    heads = weight_ref.shape[0] // (3 * HD)
    project(mod_ref, weight_ref, token_refs, far_ref)

    def whole(start):
        return jnp.concatenate([ref[start : start + HD, :] for ref in (near_ref, far_ref)], axis=1)

    for head in range(heads):
        base = head * 3 * HD
        queries, keys, values = (whole(base + part * HD) for part in range(3))
        keys, queries = keys.astype(BF16).T, queries.astype(BF16)
        for at in range(0, count, 2):
            cols = slice(at * block, (at + 2) * block)
            rows = slice(head * HD, (head + 1) * HD)
            heads_ref[rows, cols] = attend(keys, queries[:, cols], values)
    for at in range(count):
        out_ref = (kept_ref, sent_ref)[at % 2]
        cols = slice(at // 2 * block, (at // 2 + 1) * block)
        out_ref[:, cols] = heads_ref[:, at * block : (at + 1) * block].astype(BF16)


def halves(value, size):
    return [
        jnp.concatenate(
            [value[at : at + size] for at in range(first * size, value.shape[0], 2 * size)], axis=0
        )
        for first in range(2)
    ]


def of_this_half(value, size):
    even, odd = (half.astype(F32) for half in halves(value, size))
    first = lax.axis_index("frame") % 2 == 0
    return jnp.where(first, even, odd), jnp.where(first, odd, even)


def share_kernel(period, token_ref, sent_ref):
    sent_ref[...] = of_this_half(token_ref[0], period)[1].astype(BF16)


def partial_kernel(period, *refs):
    head_refs, weight_refs, out_refs = refs[:2], refs[2:4], refs[4:]
    weights = jnp.concatenate([ref[...] for ref in weight_refs], axis=0)
    block = 2 * out_refs[0].shape[0]
    for at in range(len(out_refs) // 2):
        cols = slice(at * block, (at + 1) * block)
        heads = jnp.concatenate([ref[:, cols] for ref in head_refs], axis=0)
        for ref, part in zip(
            out_refs[2 * at : 2 * at + 2], of_this_half(dot(heads.T, weights), period)
        ):
            ref[...] = part.astype(ref.dtype)


def middle_kernel(pieces, groups, mod_ref, own_ref, paired_ref, *refs):
    update_refs = (refs[:groups], refs[groups : 2 * groups])
    kept_ref, sent_ref, *piece_refs, scratch = refs[2 * groups :]
    _, period, width = kept_ref.shape
    inputs = (of_this_half(own_ref[0], period)[0], paired_ref[...])
    for at, (tokens, middle_ref) in enumerate(zip(inputs, (kept_ref, sent_ref))):
        update = sum(ref[...].astype(F32) for ref in update_refs[at])
        middle = (tokens.astype(F32) + mod_ref[2:3, :] * update).astype(BF16)
        normed = norm_rows(middle.astype(F32), mod_ref[3:4, :], mod_ref[4:5, :])
        for piece in range(pieces):
            rows = slice(piece * period, (piece + 1) * period)
            middle_ref[piece] = middle[rows]
            scratch[piece, at * period : (at + 1) * period, :] = normed[rows]
    here = lax.axis_index("frame") // 2
    for at, ref in enumerate(piece_refs):
        ref[...] = scratch[here ^ (pieces - 1 - at)]


def join_kernel(*refs):
    size = refs[0].shape[0]
    for at, ref in enumerate(refs[:-1]):
        refs[-1][at * size : (at + 1) * size, :] = ref[...]


def temporal_kernel(groups, period, *refs):
    weight_refs, output_refs, row_refs = refs[:2], refs[2:4], refs[4 : 4 + groups]
    update_refs = refs[4 + groups : -2]
    proj_ref, heads_ref = refs[-2:]
    rows = jnp.concatenate([ref[...] for ref in row_refs], axis=0)
    block = rows.shape[0] // groups
    depth = weight_refs[0].shape[0]
    for core in range(2):
        proj_ref[core * depth : (core + 1) * depth, :] = dot(weight_refs[core][...], rows, 1, 1)
    heads = 2 * depth // (3 * HD)
    key_patch = lax.broadcasted_iota(jnp.int32, (block, block), 0) % period
    query_patch = lax.broadcasted_iota(jnp.int32, (block, block), 1) % period
    mask = key_patch == query_patch
    for head in range(heads):
        base = head * 3 * HD
        for group in range(groups):
            cols = slice(group * block, (group + 1) * block)
            query = proj_ref[base : base + HD, cols].astype(BF16)
            keys = proj_ref[base + HD : base + 2 * HD, cols].astype(BF16)
            values = proj_ref[base + 2 * HD : base + 3 * HD, cols]
            heads_ref[head * HD : (head + 1) * HD, cols] = attend(keys.T, query, values, mask)
    weights = jnp.concatenate([ref[...] for ref in output_refs], axis=0)
    for group in range(groups):
        mixed = heads_ref[:, group * block : (group + 1) * block].astype(BF16)
        parts = halves(dot(mixed.T, weights), period)
        for ref, part in zip(update_refs[2 * group : 2 * group + 2], parts):
            ref[...] = part.astype(ref.dtype)


def sum_kernel(pieces, groups, *refs):
    update_refs, piece_refs = (refs[:groups], refs[groups : 2 * groups]), refs[2 * groups :]
    period = piece_refs[0].shape[0] // 2
    for at, parts in enumerate(update_refs):
        update = sum(ref[...].astype(F32) for ref in parts).astype(BF16)
        for piece, ref in enumerate(piece_refs):
            rows = update[piece * period : (piece + 1) * period]
            ref[at * period : (at + 1) * period, :] = rows


def result_kernel(pieces, mod_ref, kept_ref, other_ref, *refs):
    piece_refs, out_ref = refs[:-1], refs[-1]
    period = kept_ref.shape[1]
    here = lax.axis_index("frame")
    for at, ref in enumerate(piece_refs):
        there = here // 2 ^ (pieces - 1 - at)
        for half, middle_ref in enumerate((kept_ref, other_ref)):
            update = ref[half * period : (half + 1) * period, :].astype(F32)
            middle = middle_ref[there].astype(F32)
            out_ref[2 * there + (here % 2 ^ half)] = (middle + mod_ref[5:6, :] * update).astype(
                BF16
            )


def call(body, operands, outs, scratch=(), limit=24):
    return pl.pallas_call(
        body,
        out_shape=outs,
        in_specs=[pl.BlockSpec(memory_space=pltpu.VMEM)] * len(operands),
        out_specs=[pl.BlockSpec(memory_space=pltpu.VMEM)] * len(outs),
        scratch_shapes=list(scratch),
        compiler_params=pltpu.CompilerParams(vmem_limit_bytes=limit * MIB),
        cost_estimate=pl.CostEstimate(flops=1, bytes_accessed=1, transcendentals=0),
    )(*operands)


def swap(value, axis, offset):
    size = lax.axis_size(axis)
    return lax.ppermute(value, axis, [(at, at ^ offset) for at in range(size)])


def after(value, *others):
    return lax.optimization_barrier((value, *others))[0]


def across(value):
    size = lax.axis_size("patch")
    return [swap(value, "patch", at) if at else value for at in range(0, size, 2)]


def both_cores(blocks):
    return [part for block in blocks for part in (block, swap(block, "patch", 1))]


def swap_diagonal(value, offset):
    frames, size = lax.axis_size("frame"), lax.axis_size("patch")
    pairs = [
        (frame * size + at, (frame ^ 1) * size + (at ^ offset))
        for frame in range(frames)
        for at in range(size)
    ]
    return lax.ppermute(value, ("frame", "patch"), pairs)


def per_device(tokens, modulation, spatial_qkv, spatial_out, temporal_qkv, temporal_out):
    _, rows, width = tokens.shape
    shard = spatial_out.shape[0]
    count, frames = lax.axis_size("patch"), lax.axis_size("frame")
    period = rows // frames
    pieces, groups = frames // 2, count // 2
    shape = jax.ShapeDtypeStruct

    def with_sister(weights, *others):
        return [weights, swap(after(weights, *others), "patch", 1)]

    def exchange_frames(parts):
        offsets = reversed(range(pieces))
        return [swap(part, "frame", 2 * at) if at else part for at, part in zip(offsets, parts)]

    def return_updates(own, far):
        kept, sent = own
        same = [swap(part, "patch", 2 * at) for at, part in enumerate(far[::2], 1)]
        diagonal = [swap_diagonal(part, 2 * at) for at, part in enumerate(far[1::2], 1)]
        return [kept, *same, swap(sent, "frame", 1), *diagonal]

    def halves_shape(dtype):
        return shape((rows // 2, width), dtype)

    own_shapes = [halves_shape(F32), halves_shape(BF16)]
    far_shapes = [halves_shape(BF16)] * (2 * groups - 2)
    piece_shapes = [shape((2 * period, width), BF16)] * pieces

    sister = swap(tokens, "patch", 1)
    far = across(tokens)[1:]
    (near,) = call(
        near_kernel,
        (modulation, spatial_qkv, tokens, sister),
        [shape((3 * shard, 2 * rows), F32)],
    )
    (shared,) = call(
        functools.partial(share_kernel, period), (after(tokens, sister),), [halves_shape(BF16)]
    )
    paired = swap(shared, "frame", 1)
    out_pair = with_sister(spatial_out, near)
    far = both_cores([after(block, near, paired) for block in far])
    temporal_pair = with_sister(temporal_qkv, *far)
    late_pair = with_sister(temporal_out, *far)

    kept, sent = call(
        functools.partial(spatial_kernel, count),
        (modulation, spatial_qkv, near, *far),
        [shape((shard, groups * rows), BF16)] * 2,
        [pltpu.VMEM((3 * shard, (count - 2) * rows), F32), pltpu.VMEM((shard, count * rows), F32)],
    )
    parts = call(
        functools.partial(partial_kernel, period),
        (kept, swap(sent, "patch", 1), *out_pair),
        own_shapes + far_shapes,
    )
    updates = return_updates(parts[:2], parts[2:])
    middle, middle_sent, *parts = call(
        functools.partial(middle_kernel, pieces, groups),
        (modulation, tokens, paired, *updates),
        [shape((pieces, period, width), BF16)] * 2 + piece_shapes,
        [pltpu.VMEM((pieces, 2 * period, width), BF16)],
    )
    (segment,) = call(join_kernel, exchange_frames(parts), [shape((rows, width), BF16)])

    def attend_frames(segments, shapes):
        columns = len(segments) * rows
        return call(
            functools.partial(temporal_kernel, len(segments), period),
            (*temporal_pair, *late_pair, *segments),
            shapes,
            [pltpu.VMEM((6 * shard, columns), F32), pltpu.VMEM((2 * shard, columns), F32)],
        )

    others = across(segment)[1:]
    middle_other = swap(after(middle_sent, segment), "frame", 1)
    own_parts = attend_frames([segment], own_shapes)
    others = [after(block, own_parts[0], middle_other) for block in others]
    far_parts = attend_frames(others, far_shapes)
    parts = call(
        functools.partial(sum_kernel, pieces, groups),
        return_updates(own_parts, far_parts),
        piece_shapes,
    )
    (result,) = call(
        functools.partial(result_kernel, pieces),
        (modulation, middle, middle_other, *exchange_frames(parts)),
        [shape((frames, period, width), BF16)],
    )
    return result.reshape(1, rows, width)


def solution(mesh):
    in_specs = (
        P("frame", "patch", None),
        P(),
        P("patch", None),
        P("patch", None),
        P("patch", None),
        P("patch", None),
    )
    out_specs = P("frame", "patch", None)
    return jax.shard_map(
        per_device, mesh=mesh, in_specs=in_specs, out_specs=out_specs, check_vma=False
    )
```

```python
import functools

import jax
import jax.numpy as jnp
from jax import lax
from jax.experimental import pallas as pl
from jax.experimental.pallas import tpu as pltpu
from jax.sharding import PartitionSpec as P

HD = 72
MIB = 1 << 20
LOG2E = 1.4426950408889634
F32 = jnp.float32
BF16 = jnp.bfloat16


def norm_rows(values, shift, scale):
    average = jnp.mean(values, axis=-1, keepdims=True)
    centred = values - average
    variance = jnp.mean(centred * centred, axis=-1, keepdims=True)
    normed = centred * lax.rsqrt(variance + 1e-06)
    return (normed * (1.0 + scale) + shift).astype(BF16)


def dot(left, right, left_dim=1, right_dim=0):
    return lax.dot_general(
        left, right, (((left_dim,), (right_dim,)), ((), ())), preferred_element_type=F32
    )


def soften(scores):
    top = jnp.max(scores, axis=0, keepdims=True)
    return jnp.exp2((scores - top) * (HD**-0.5 * LOG2E)).astype(BF16)


def mix(values, weights):
    ones = jnp.ones((8, values.shape[1]), F32)
    mixed = dot(jnp.concatenate([values, ones], axis=0).astype(BF16), weights)
    return mixed[:HD] * (1.0 / mixed[HD : HD + 1])


def project(mod_ref, weight_ref, token_refs, proj_ref):
    shift, scale = mod_ref[0:1, :], mod_ref[1:2, :]
    block = token_refs[0].shape[1]
    for at in range(0, len(token_refs), 2):
        rows = [norm_rows(ref[0].astype(F32), shift, scale) for ref in token_refs[at : at + 2]]
        rows = jnp.concatenate(rows, axis=0)
        proj_ref[:, at * block : (at + 2) * block] = dot(weight_ref[...], rows, 1, 1)


def near_kernel(mod_ref, weight_ref, own_ref, sister_ref, proj_ref):
    project(mod_ref, weight_ref, (own_ref, sister_ref), proj_ref)


def spatial_kernel(count, mod_ref, weight_ref, near_ref, *refs):
    token_refs, (kept_ref, sent_ref, far_ref, heads_ref) = refs[: count - 2], refs[count - 2 :]
    block = token_refs[0].shape[1]
    heads = weight_ref.shape[0] // (3 * HD)
    project(mod_ref, weight_ref, token_refs, far_ref)

    def whole(start):
        return jnp.concatenate([ref[start : start + HD, :] for ref in (near_ref, far_ref)], axis=1)

    def score(head, at):
        base = head * 3 * HD
        source, start = (near_ref, 0) if at == 0 else (far_ref, (at - 2) * block)
        query = source[base : base + HD, start : start + 2 * block].astype(BF16)
        return dot(whole(base + HD).astype(BF16).T, query)

    steps = [(head, at) for head in range(heads) for at in range(0, count, 2)]
    scores = score(*steps[0])
    for (head, at), later in zip(steps, [*steps[1:], None]):
        coming = score(*later) if later else None
        rows, cols = slice(head * HD, (head + 1) * HD), slice(at * block, (at + 2) * block)
        heads_ref[rows, cols] = mix(whole(head * 3 * HD + 2 * HD), soften(scores))
        scores = coming
    for at in range(count):
        out_ref = (kept_ref, sent_ref)[at % 2]
        cols = slice(at // 2 * block, (at // 2 + 1) * block)
        out_ref[:, cols] = heads_ref[:, at * block : (at + 1) * block].astype(BF16)


def halves(value, size):
    return [
        jnp.concatenate(
            [value[at : at + size] for at in range(first * size, value.shape[0], 2 * size)], axis=0
        )
        for first in range(2)
    ]


def of_this_half(value, size):
    even, odd = (half.astype(F32) for half in halves(value, size))
    first = lax.axis_index("frame") % 2 == 0
    return jnp.where(first, even, odd), jnp.where(first, odd, even)


def share_kernel(period, token_ref, sent_ref):
    sent_ref[...] = of_this_half(token_ref[0], period)[1].astype(BF16)


def partial_kernel(period, *refs):
    head_refs, weight_refs, out_refs = refs[:2], refs[2:4], refs[4:]
    weights = jnp.concatenate([ref[...] for ref in weight_refs], axis=0)
    block = 2 * out_refs[0].shape[0]
    for at in range(len(out_refs) // 2):
        cols = slice(at * block, (at + 1) * block)
        heads = jnp.concatenate([ref[:, cols] for ref in head_refs], axis=0)
        for ref, part in zip(
            out_refs[2 * at : 2 * at + 2], of_this_half(dot(heads.T, weights), period)
        ):
            ref[...] = part.astype(ref.dtype)


def middle_kernel(pieces, groups, mod_ref, own_ref, paired_ref, *refs):
    update_refs = (refs[:groups], refs[groups : 2 * groups])
    kept_ref, sent_ref, *piece_refs, scratch = refs[2 * groups :]
    _, period, width = kept_ref.shape
    inputs = (of_this_half(own_ref[0], period)[0], paired_ref[...])
    for at, (tokens, middle_ref) in enumerate(zip(inputs, (kept_ref, sent_ref))):
        update = sum(ref[...].astype(F32) for ref in update_refs[at])
        middle = (tokens.astype(F32) + mod_ref[2:3, :] * update).astype(BF16)
        normed = norm_rows(middle.astype(F32), mod_ref[3:4, :], mod_ref[4:5, :])
        for piece in range(pieces):
            rows = slice(piece * period, (piece + 1) * period)
            middle_ref[piece] = middle[rows]
            scratch[piece, at * period : (at + 1) * period, :] = normed[rows]
    here = lax.axis_index("frame") // 2
    for at, ref in enumerate(piece_refs):
        ref[...] = scratch[here ^ (pieces - 1 - at)]


def join_kernel(*refs):
    size = refs[0].shape[0]
    for at, ref in enumerate(refs[:-1]):
        refs[-1][at * size : (at + 1) * size, :] = ref[...]


def temporal_kernel(period, block, *refs):
    weight_refs, output_refs, (proj_ref, heads_ref) = refs[:2], refs[2:4], refs[-2:]
    groups = proj_ref.shape[1] // block
    row_refs, update_refs = refs[4 : -2 - 2 * groups], refs[-2 - 2 * groups : -2]
    rows = jnp.concatenate([ref[...] for ref in row_refs], axis=0)
    depth = weight_refs[0].shape[0]
    for core in range(2):
        proj_ref[core * depth : (core + 1) * depth, :] = dot(weight_refs[core][...], rows, 1, 1)
    heads = 2 * depth // (3 * HD)
    key_patch = lax.broadcasted_iota(jnp.int32, (block, block), 0) % period
    query_patch = lax.broadcasted_iota(jnp.int32, (block, block), 1) % period
    mask = key_patch == query_patch
    weights = jnp.concatenate([ref[...] for ref in output_refs], axis=0)
    for group in range(groups):
        cols = slice(group * block, (group + 1) * block)

        def part(head, at):
            start = (head * 3 + at) * HD
            return proj_ref[start : start + HD, cols]

        scores = []
        for head in range(heads):
            keys, query = part(head, 1).astype(BF16).T, part(head, 0).astype(BF16)
            scores.append(jnp.where(mask, dot(keys, query), -1e30))
        soft = soften(jnp.concatenate(scores, axis=1))
        for head in range(heads):
            mixed = mix(part(head, 2), soft[:, head * block : (head + 1) * block])
            heads_ref[head * HD : (head + 1) * HD, cols] = mixed
        mixed = heads_ref[:, cols].astype(BF16)
        parts = halves(dot(mixed.T, weights), period)
        for ref, half in zip(update_refs[2 * group : 2 * group + 2], parts):
            ref[...] = half.astype(ref.dtype)


def sum_kernel(pieces, groups, *refs):
    update_refs, piece_refs = (refs[:groups], refs[groups : 2 * groups]), refs[2 * groups :]
    period = piece_refs[0].shape[0] // 2
    for at, parts in enumerate(update_refs):
        update = sum(ref[...].astype(F32) for ref in parts).astype(BF16)
        for piece, ref in enumerate(piece_refs):
            rows = update[piece * period : (piece + 1) * period]
            ref[at * period : (at + 1) * period, :] = rows


def result_kernel(pieces, mod_ref, kept_ref, other_ref, *refs):
    piece_refs, out_ref = refs[:-1], refs[-1]
    period = kept_ref.shape[1]
    here = lax.axis_index("frame")
    for at, ref in enumerate(piece_refs):
        there = here // 2 ^ (pieces - 1 - at)
        for half, middle_ref in enumerate((kept_ref, other_ref)):
            update = ref[half * period : (half + 1) * period, :].astype(F32)
            middle = middle_ref[there].astype(F32)
            out_ref[2 * there + (here % 2 ^ half)] = (middle + mod_ref[5:6, :] * update).astype(
                BF16
            )


def call(body, operands, outs, scratch=(), limit=24):
    return pl.pallas_call(
        body,
        out_shape=outs,
        in_specs=[pl.BlockSpec(memory_space=pltpu.VMEM)] * len(operands),
        out_specs=[pl.BlockSpec(memory_space=pltpu.VMEM)] * len(outs),
        scratch_shapes=list(scratch),
        compiler_params=pltpu.CompilerParams(vmem_limit_bytes=limit * MIB),
        cost_estimate=pl.CostEstimate(flops=1, bytes_accessed=1, transcendentals=0),
    )(*operands)


def swap(value, axis, offset):
    size = lax.axis_size(axis)
    return lax.ppermute(value, axis, [(at, at ^ offset) for at in range(size)])


def after(value, *others):
    return lax.optimization_barrier((value, *others))[0]


def across(value):
    size = lax.axis_size("patch")
    return [swap(value, "patch", at) if at else value for at in range(0, size, 2)]


def both_cores(blocks):
    return [part for block in blocks for part in (block, swap(block, "patch", 1))]


def swap_diagonal(value, offset):
    frames, size = lax.axis_size("frame"), lax.axis_size("patch")
    pairs = [
        (frame * size + at, (frame ^ 1) * size + (at ^ offset))
        for frame in range(frames)
        for at in range(size)
    ]
    return lax.ppermute(value, ("frame", "patch"), pairs)


def per_device(tokens, modulation, spatial_qkv, spatial_out, temporal_qkv, temporal_out):
    _, rows, width = tokens.shape
    shard = spatial_out.shape[0]
    count, frames = lax.axis_size("patch"), lax.axis_size("frame")
    period = rows // frames
    pieces, groups = frames // 2, count // 2
    shape = jax.ShapeDtypeStruct

    def with_sister(weights, *others):
        return [weights, swap(after(weights, *others), "patch", 1)]

    def exchange_frames(parts):
        offsets = reversed(range(pieces))
        return [swap(part, "frame", 2 * at) if at else part for at, part in zip(offsets, parts)]

    def return_updates(own, far):
        kept, sent = own
        same = [swap(part, "patch", 2 * at) for at, part in enumerate(far[::2], 1)]
        diagonal = [swap_diagonal(part, 2 * at) for at, part in enumerate(far[1::2], 1)]
        return [kept, *same, swap(sent, "frame", 1), *diagonal]

    def halves_shape(dtype):
        return shape((rows // 2, width), dtype)

    own_shapes = [halves_shape(F32), halves_shape(BF16)]
    far_shapes = [halves_shape(BF16)] * (2 * groups - 2)
    piece_shapes = [shape((2 * period, width), BF16)] * pieces

    sister = swap(tokens, "patch", 1)
    far = across(tokens)[1:]
    (near,) = call(
        near_kernel,
        (modulation, spatial_qkv, tokens, sister),
        [shape((3 * shard, 2 * rows), F32)],
    )
    (shared,) = call(
        functools.partial(share_kernel, period), (after(tokens, sister),), [halves_shape(BF16)]
    )
    paired = swap(shared, "frame", 1)
    out_pair = with_sister(spatial_out, near)
    far = both_cores([after(block, near, paired) for block in far])
    temporal_pair = with_sister(temporal_qkv, *far)
    late_pair = with_sister(temporal_out, *far)

    kept, sent = call(
        functools.partial(spatial_kernel, count),
        (modulation, spatial_qkv, near, *far),
        [shape((shard, groups * rows), BF16)] * 2,
        [pltpu.VMEM((3 * shard, (count - 2) * rows), F32), pltpu.VMEM((shard, count * rows), F32)],
    )
    parts = call(
        functools.partial(partial_kernel, period),
        (kept, swap(sent, "patch", 1), *out_pair),
        own_shapes + far_shapes,
    )
    updates = return_updates(parts[:2], parts[2:])
    middle, middle_sent, *parts = call(
        functools.partial(middle_kernel, pieces, groups),
        (modulation, tokens, paired, *updates),
        [shape((pieces, period, width), BF16)] * 2 + piece_shapes,
        [pltpu.VMEM((pieces, 2 * period, width), BF16)],
    )
    arrived = exchange_frames(parts)
    first = [[part] for part in across(parts[-1])]
    (rest,) = call(join_kernel, arrived[:-1], [shape((rows - 2 * period, width), BF16)])
    rest = across(after(rest, *(part for (part,) in first[1:])))
    segments = [[late, *early] for late, early in zip(rest, first)]

    def attend_frames(segments, shapes, *others):
        columns = len(segments) * rows
        inputs = [after(part, *others) for segment in segments for part in segment]
        return call(
            functools.partial(temporal_kernel, period, rows),
            (*temporal_pair, *late_pair, *inputs),
            shapes,
            [pltpu.VMEM((6 * shard, columns), F32), pltpu.VMEM((2 * shard, columns), F32)],
        )

    middle_other = swap(after(middle_sent, rest[0]), "frame", 1)
    own_parts = attend_frames(segments[:1], own_shapes)
    far_parts = attend_frames(segments[1:], far_shapes, own_parts[0], middle_other)
    parts = call(
        functools.partial(sum_kernel, pieces, groups),
        return_updates(own_parts, far_parts),
        piece_shapes,
    )
    (result,) = call(
        functools.partial(result_kernel, pieces),
        (modulation, middle, middle_other, *exchange_frames(parts)),
        [shape((frames, period, width), BF16)],
    )
    return result.reshape(1, rows, width)


def solution(mesh):
    in_specs = (
        P("frame", "patch", None),
        P(),
        P("patch", None),
        P("patch", None),
        P("patch", None),
        P("patch", None),
    )
    out_specs = P("frame", "patch", None)
    return jax.shard_map(
        per_device, mesh=mesh, in_specs=in_specs, out_specs=out_specs, check_vma=False
    )
```

```python
import functools

import jax
import jax.numpy as jnp
from jax import lax
from jax.experimental import pallas as pl
from jax.experimental.pallas import tpu as pltpu
from jax.sharding import PartitionSpec as P

HD = 72
MIB = 1 << 20
LOG2E = 1.4426950408889634
F32 = jnp.float32
BF16 = jnp.bfloat16


def norm_rows(values, shift, scale):
    average = jnp.mean(values, axis=-1, keepdims=True)
    centred = values - average
    variance = jnp.mean(centred * centred, axis=-1, keepdims=True)
    normed = centred * lax.rsqrt(variance + 1e-06)
    return (normed * (1.0 + scale) + shift).astype(BF16)


def dot(left, right, left_dim=1, right_dim=0):
    return lax.dot_general(
        left, right, (((left_dim,), (right_dim,)), ((), ())), preferred_element_type=F32
    )


def soften(scores):
    top = jnp.max(scores, axis=0, keepdims=True)
    return jnp.exp2((scores - top) * (HD**-0.5 * LOG2E)).astype(BF16)


def mix(values, weights):
    ones = jnp.ones((8, values.shape[1]), F32)
    mixed = dot(jnp.concatenate([values, ones], axis=0).astype(BF16), weights)
    return mixed[:HD] * (1.0 / mixed[HD : HD + 1])


def project(mod_ref, weight_ref, token_refs, proj_ref):
    shift, scale = mod_ref[0:1, :], mod_ref[1:2, :]
    block = token_refs[0].shape[1]
    for at in range(0, len(token_refs), 2):
        rows = [norm_rows(ref[0].astype(F32), shift, scale) for ref in token_refs[at : at + 2]]
        rows = jnp.concatenate(rows, axis=0)
        proj_ref[:, at * block : (at + 2) * block] = dot(weight_ref[...], rows, 1, 1)


def near_kernel(mod_ref, weight_ref, own_ref, sister_ref, proj_ref):
    project(mod_ref, weight_ref, (own_ref, sister_ref), proj_ref)


def spatial_kernel(count, mod_ref, weight_ref, near_ref, *refs):
    token_refs, (kept_ref, sent_ref, far_ref, heads_ref) = refs[: count - 2], refs[count - 2 :]
    block = token_refs[0].shape[1]
    heads = weight_ref.shape[0] // (3 * HD)
    project(mod_ref, weight_ref, token_refs, far_ref)

    def whole(start):
        return jnp.concatenate([ref[start : start + HD, :] for ref in (near_ref, far_ref)], axis=1)

    def score(head, at):
        base = head * 3 * HD
        source, start = (near_ref, 0) if at == 0 else (far_ref, (at - 2) * block)
        query = source[base : base + HD, start : start + 2 * block].astype(BF16)
        return dot(whole(base + HD).astype(BF16).T, query)

    steps = [(head, at) for head in range(heads) for at in range(0, count, 2)]
    scores = score(*steps[0])
    for (head, at), later in zip(steps, [*steps[1:], None]):
        coming = score(*later) if later else None
        rows, cols = slice(head * HD, (head + 1) * HD), slice(at * block, (at + 2) * block)
        heads_ref[rows, cols] = mix(whole(head * 3 * HD + 2 * HD), soften(scores))
        scores = coming
    for at in range(count):
        out_ref = (kept_ref, sent_ref)[at % 2]
        cols = slice(at // 2 * block, (at // 2 + 1) * block)
        out_ref[:, cols] = heads_ref[:, at * block : (at + 1) * block].astype(BF16)


def halves(value, size):
    return [
        jnp.concatenate(
            [value[at : at + size] for at in range(first * size, value.shape[0], 2 * size)], axis=0
        )
        for first in range(2)
    ]


def of_this_half(value, size):
    even, odd = (half.astype(F32) for half in halves(value, size))
    first = lax.axis_index("frame") % 2 == 0
    return jnp.where(first, even, odd), jnp.where(first, odd, even)


def share_kernel(period, token_ref, sent_ref):
    sent_ref[...] = of_this_half(token_ref[0], period)[1].astype(BF16)


def joined(refs):
    return jnp.concatenate([ref[...] for ref in refs], axis=0)


def partial_kernel(period, *refs):
    head_refs, weights, out_refs = refs[:2], joined(refs[2:4]), refs[4:]
    block = 2 * out_refs[0].shape[0]
    for at in range(len(out_refs) // 2):
        cols = slice(at * block, (at + 1) * block)
        heads = jnp.concatenate([ref[:, cols] for ref in head_refs], axis=0).T
        if at == 0:
            kept, sent = (half.astype(BF16) for half in of_this_half(heads, period))
            parts = dot(kept, weights), sent
        else:
            parts = of_this_half(dot(heads, weights), period)
        for ref, part in zip(out_refs[2 * at : 2 * at + 2], parts):
            ref[...] = part.astype(ref.dtype)


def total_updates(groups, weight_refs, refs):
    kept = sum(ref[...].astype(F32) for ref in refs[:groups])
    paired = dot(refs[groups][...], joined(weight_refs))
    return kept, paired + sum(ref[...].astype(F32) for ref in refs[groups + 1 : 2 * groups])


def middle_kernel(pieces, groups, mod_ref, own_ref, paired_ref, *refs):
    kept_ref, sent_ref, *piece_refs, scratch = refs[2 + 2 * groups :]
    updates = total_updates(groups, refs[:2], refs[2:])
    _, period, width = kept_ref.shape
    inputs = (of_this_half(own_ref[0], period)[0], paired_ref[...])
    for at, (tokens, middle_ref) in enumerate(zip(inputs, (kept_ref, sent_ref))):
        update = updates[at]
        middle = (tokens.astype(F32) + mod_ref[2:3, :] * update).astype(BF16)
        normed = norm_rows(middle.astype(F32), mod_ref[3:4, :], mod_ref[4:5, :])
        for piece in range(pieces):
            rows = slice(piece * period, (piece + 1) * period)
            middle_ref[piece] = middle[rows]
            scratch[piece, at * period : (at + 1) * period, :] = normed[rows]
    here = lax.axis_index("frame") // 2
    for at, ref in enumerate(piece_refs):
        ref[...] = scratch[here ^ (pieces - 1 - at)]


def join_kernel(*refs):
    size = refs[0].shape[0]
    for at, ref in enumerate(refs[:-1]):
        refs[-1][at * size : (at + 1) * size, :] = ref[...]


def temporal_kernel(own, period, block, *refs):
    weight_refs, output_refs, (proj_ref, heads_ref) = refs[:2], refs[2:4], refs[-2:]
    groups = proj_ref.shape[1] // block
    row_refs, update_refs = refs[4 : -2 - 2 * groups], refs[-2 - 2 * groups : -2]
    rows = jnp.concatenate([ref[...] for ref in row_refs], axis=0)
    depth = weight_refs[0].shape[0]
    for core in range(2):
        proj_ref[core * depth : (core + 1) * depth, :] = dot(weight_refs[core][...], rows, 1, 1)
    heads = 2 * depth // (3 * HD)
    key_patch = lax.broadcasted_iota(jnp.int32, (block, block), 0) % period
    query_patch = lax.broadcasted_iota(jnp.int32, (block, block), 1) % period
    mask = key_patch == query_patch
    weights = joined(output_refs)
    for group in range(groups):
        cols = slice(group * block, (group + 1) * block)

        def part(head, at):
            start = (head * 3 + at) * HD
            return proj_ref[start : start + HD, cols]

        scores = []
        for head in range(heads):
            keys, query = part(head, 1).astype(BF16).T, part(head, 0).astype(BF16)
            scores.append(jnp.where(mask, dot(keys, query), -1e30))
        soft = soften(jnp.concatenate(scores, axis=1))
        for head in range(heads):
            mixed = mix(part(head, 2), soft[:, head * block : (head + 1) * block])
            heads_ref[head * HD : (head + 1) * HD, cols] = mixed
        mixed = heads_ref[:, cols].astype(BF16).T
        if own:
            kept, sent = halves(mixed, period)
            parts = dot(kept, weights), sent
        else:
            parts = halves(dot(mixed, weights), period)
        for ref, half in zip(update_refs[2 * group : 2 * group + 2], parts):
            ref[...] = half.astype(ref.dtype)


def sum_kernel(groups, *refs):
    piece_refs = refs[2 + 2 * groups :]
    period = piece_refs[0].shape[0] // 2
    for at, update in enumerate(total_updates(groups, refs[:2], refs[2:])):
        update = update.astype(BF16)
        for piece, ref in enumerate(piece_refs):
            rows = update[piece * period : (piece + 1) * period]
            ref[at * period : (at + 1) * period, :] = rows


def result_kernel(pieces, mod_ref, kept_ref, other_ref, *refs):
    piece_refs, out_ref = refs[:-1], refs[-1]
    period = kept_ref.shape[1]
    here = lax.axis_index("frame")
    for at, ref in enumerate(piece_refs):
        there = here // 2 ^ (pieces - 1 - at)
        for half, middle_ref in enumerate((kept_ref, other_ref)):
            update = ref[half * period : (half + 1) * period, :].astype(F32)
            middle = middle_ref[there].astype(F32)
            out_ref[2 * there + (here % 2 ^ half)] = (middle + mod_ref[5:6, :] * update).astype(
                BF16
            )


def call(body, operands, outs, scratch=(), limit=24):
    return pl.pallas_call(
        body,
        out_shape=outs,
        in_specs=[pl.BlockSpec(memory_space=pltpu.VMEM)] * len(operands),
        out_specs=[pl.BlockSpec(memory_space=pltpu.VMEM)] * len(outs),
        scratch_shapes=list(scratch),
        compiler_params=pltpu.CompilerParams(vmem_limit_bytes=limit * MIB),
        cost_estimate=pl.CostEstimate(flops=1, bytes_accessed=1, transcendentals=0),
    )(*operands)


def swap(value, axis, offset):
    size = lax.axis_size(axis)
    return lax.ppermute(value, axis, [(at, at ^ offset) for at in range(size)])


def after(value, *others):
    return lax.optimization_barrier((value, *others))[0]


def across(value):
    size = lax.axis_size("patch")
    return [swap(value, "patch", at) if at else value for at in range(0, size, 2)]


def both_cores(blocks):
    return [part for block in blocks for part in (block, swap(block, "patch", 1))]


def swap_diagonal(value, offset):
    frames, size = lax.axis_size("frame"), lax.axis_size("patch")
    pairs = [
        (frame * size + at, (frame ^ 1) * size + (at ^ offset))
        for frame in range(frames)
        for at in range(size)
    ]
    return lax.ppermute(value, ("frame", "patch"), pairs)


def per_device(tokens, modulation, spatial_qkv, spatial_out, temporal_qkv, temporal_out):
    _, rows, width = tokens.shape
    shard = spatial_out.shape[0]
    count, frames = lax.axis_size("patch"), lax.axis_size("frame")
    period = rows // frames
    pieces, groups = frames // 2, count // 2
    shape = jax.ShapeDtypeStruct

    def with_sister(weights, *others):
        return [weights, swap(after(weights, *others), "patch", 1)]

    def exchange_frames(parts):
        offsets = reversed(range(pieces))
        return [swap(part, "frame", 2 * at) if at else part for at, part in zip(offsets, parts)]

    def return_updates(own, far):
        same = [swap(part, "patch", 2 * at) for at, part in enumerate(far[::2], 1)]
        diagonal = [swap_diagonal(part, 2 * at) for at, part in enumerate(far[1::2], 1)]
        return [own[0], *same, own[1], *diagonal]

    def halves_shape(dtype):
        return shape((rows // 2, width), dtype)

    own_shapes = [halves_shape(F32), shape((rows // 2, 2 * shard), BF16)]
    far_shapes = [halves_shape(BF16)] * (2 * groups - 2)
    piece_shapes = [shape((2 * period, width), BF16)] * pieces

    sister = swap(tokens, "patch", 1)
    far = across(tokens)[1:]
    (near,) = call(
        near_kernel,
        (modulation, spatial_qkv, tokens, sister),
        [shape((3 * shard, 2 * rows), F32)],
    )
    (shared,) = call(
        functools.partial(share_kernel, period), (after(tokens, sister),), [halves_shape(BF16)]
    )
    paired = swap(shared, "frame", 1)
    out_pair = with_sister(spatial_out, near)
    far = both_cores([after(block, near, paired) for block in far])
    temporal_pair = with_sister(temporal_qkv, *far)
    late_pair = with_sister(temporal_out, *far)

    kept, sent = call(
        functools.partial(spatial_kernel, count),
        (modulation, spatial_qkv, near, *far),
        [shape((shard, groups * rows), BF16)] * 2,
        [pltpu.VMEM((3 * shard, (count - 2) * rows), F32), pltpu.VMEM((shard, count * rows), F32)],
    )
    parts = call(
        functools.partial(partial_kernel, period),
        (kept, swap(sent, "patch", 1), *out_pair),
        own_shapes + far_shapes,
    )
    updates = return_updates((parts[0], swap(parts[1], "frame", 1)), parts[2:])
    middle, middle_sent, *parts = call(
        functools.partial(middle_kernel, pieces, groups),
        (modulation, tokens, paired, *out_pair, *updates),
        [shape((pieces, period, width), BF16)] * 2 + piece_shapes,
        [pltpu.VMEM((pieces, 2 * period, width), BF16)],
    )
    arrived = exchange_frames(parts)
    (segment,) = call(join_kernel, arrived, [shape((rows, width), BF16)])
    segments = across(segment)

    def attend_frames(own, segments, shapes):
        columns = len(segments) * rows
        return call(
            functools.partial(temporal_kernel, own, period, rows),
            (*temporal_pair, *late_pair, *segments),
            shapes,
            [pltpu.VMEM((6 * shard, columns), F32), pltpu.VMEM((2 * shard, columns), F32)],
        )

    kept, sent = attend_frames(True, [segment], own_shapes)
    received = swap(sent, "frame", 1)
    middle_other = swap(after(middle_sent, segment), "frame", 1)
    others = [after(block, received, middle_other) for block in segments[1:]]
    far_parts = attend_frames(False, others, far_shapes)
    updates = return_updates((kept, received), far_parts)
    parts = call(
        functools.partial(sum_kernel, groups),
        (*late_pair, *updates),
        piece_shapes,
    )
    (result,) = call(
        functools.partial(result_kernel, pieces),
        (modulation, middle, middle_other, *exchange_frames(parts)),
        [shape((frames, period, width), BF16)],
    )
    return result.reshape(1, rows, width)


def solution(mesh):
    in_specs = (
        P("frame", "patch", None),
        P(),
        P("patch", None),
        P("patch", None),
        P("patch", None),
        P("patch", None),
    )
    out_specs = P("frame", "patch", None)
    return jax.shard_map(
        per_device, mesh=mesh, in_specs=in_specs, out_specs=out_specs, check_vma=False
    )
```

```python
import functools

import jax
import jax.numpy as jnp
from jax import lax
from jax.experimental import pallas as pl
from jax.experimental.pallas import tpu as pltpu
from jax.sharding import PartitionSpec as P

HD = 72
MIB = 1 << 20
LOG2E = 1.4426950408889634
F32 = jnp.float32
BF16 = jnp.bfloat16


def norm_rows(values, shift, scale):
    average = jnp.mean(values, axis=-1, keepdims=True)
    centred = values - average
    variance = jnp.mean(centred * centred, axis=-1, keepdims=True)
    normed = centred * lax.rsqrt(variance + 1e-06)
    return (normed * (1.0 + scale) + shift).astype(BF16)


def dot(left, right, left_dim=1, right_dim=0):
    return lax.dot_general(
        left, right, (((left_dim,), (right_dim,)), ((), ())), preferred_element_type=F32
    )


def soften(scores):
    top = jnp.max(scores, axis=0, keepdims=True)
    return jnp.exp2((scores - top) * (HD**-0.5 * LOG2E)).astype(BF16)


def mix(values, weights):
    ones = jnp.ones((8, values.shape[1]), F32)
    mixed = dot(jnp.concatenate([values, ones], axis=0).astype(BF16), weights)
    return mixed[:HD] * (1.0 / mixed[HD : HD + 1])


def project(mod_ref, weight_ref, token_refs, proj_ref):
    shift, scale = mod_ref[0:1, :], mod_ref[1:2, :]
    block = token_refs[0].shape[1]
    for at in range(0, len(token_refs), 2):
        rows = [norm_rows(ref[0].astype(F32), shift, scale) for ref in token_refs[at : at + 2]]
        rows = jnp.concatenate(rows, axis=0)
        proj_ref[:, at * block : (at + 2) * block] = dot(weight_ref[...], rows, 1, 1)


def near_kernel(mod_ref, weight_ref, own_ref, sister_ref, proj_ref):
    project(mod_ref, weight_ref, (own_ref, sister_ref), proj_ref)


def spatial_kernel(count, mod_ref, weight_ref, near_ref, *refs):
    token_refs, (kept_ref, sent_ref, far_ref, heads_ref) = refs[: count - 2], refs[count - 2 :]
    block = token_refs[0].shape[1]
    heads = weight_ref.shape[0] // (3 * HD)
    project(mod_ref, weight_ref, token_refs, far_ref)

    def whole(start):
        return jnp.concatenate([ref[start : start + HD, :] for ref in (near_ref, far_ref)], axis=1)

    def score(head, at):
        base = head * 3 * HD
        source, start = (near_ref, 0) if at == 0 else (far_ref, (at - 2) * block)
        query = source[base : base + HD, start : start + 2 * block].astype(BF16)
        return dot(whole(base + HD).astype(BF16).T, query)

    steps = [(head, at) for head in range(heads) for at in range(0, count, 2)]
    scores = score(*steps[0])
    for (head, at), later in zip(steps, [*steps[1:], None]):
        coming = score(*later) if later else None
        rows, cols = slice(head * HD, (head + 1) * HD), slice(at * block, (at + 2) * block)
        heads_ref[rows, cols] = mix(whole(head * 3 * HD + 2 * HD), soften(scores))
        scores = coming
    for at in range(count):
        out_ref = (kept_ref, sent_ref)[at % 2]
        cols = slice(at // 2 * block, (at // 2 + 1) * block)
        out_ref[:, cols] = heads_ref[:, at * block : (at + 1) * block].astype(BF16)


def halves(value, size):
    return [
        jnp.concatenate(
            [value[at : at + size] for at in range(first * size, value.shape[0], 2 * size)], axis=0
        )
        for first in range(2)
    ]


def of_this_half(value, size):
    even, odd = (half.astype(F32) for half in halves(value, size))
    first = lax.axis_index("frame") % 2 == 0
    return jnp.where(first, even, odd), jnp.where(first, odd, even)


def share_kernel(period, token_ref, sent_ref):
    sent_ref[...] = of_this_half(token_ref[0], period)[1].astype(BF16)


def joined(refs):
    return jnp.concatenate([ref[...] for ref in refs], axis=0)


def partial_kernel(period, *refs):
    head_refs, weights, out_refs = refs[:2], joined(refs[2:4]), refs[4:]
    block = 2 * out_refs[0].shape[0]
    for at in range(len(out_refs) // 2):
        cols = slice(at * block, (at + 1) * block)
        heads = jnp.concatenate([ref[:, cols] for ref in head_refs], axis=0).T
        if at == 0:
            kept, sent = (half.astype(BF16) for half in of_this_half(heads, period))
            parts = dot(kept, weights), sent
        else:
            parts = of_this_half(dot(heads, weights), period)
        for ref, part in zip(out_refs[2 * at : 2 * at + 2], parts):
            ref[...] = part.astype(ref.dtype)


def total_updates(groups, weight_refs, refs):
    kept = sum(ref[...].astype(F32) for ref in refs[:groups])
    paired = dot(refs[groups][...], joined(weight_refs))
    return kept, paired + sum(ref[...].astype(F32) for ref in refs[groups + 1 : 2 * groups])


def middle_kernel(offsets, groups, mod_ref, own_ref, paired_ref, *refs):
    kept_ref, sent_ref, *piece_refs, scratch = refs[2 + 2 * groups :]
    updates = total_updates(groups, refs[:2], refs[2:])
    _, period, width = kept_ref.shape
    inputs = (of_this_half(own_ref[0], period)[0], paired_ref[...])
    for at, (tokens, middle_ref) in enumerate(zip(inputs, (kept_ref, sent_ref))):
        update = updates[at]
        middle = (tokens.astype(F32) + mod_ref[2:3, :] * update).astype(BF16)
        normed = norm_rows(middle.astype(F32), mod_ref[3:4, :], mod_ref[4:5, :])
        for piece in range(len(offsets)):
            rows = slice(piece * period, (piece + 1) * period)
            middle_ref[piece] = middle[rows]
            scratch[piece, at * period : (at + 1) * period, :] = normed[rows]
    here = lax.axis_index("frame") // 2
    for offset, ref in zip(offsets, piece_refs):
        ref[...] = scratch[here ^ offset]


def join_kernel(*refs):
    size = refs[0].shape[0]
    for at, ref in enumerate(refs[:-1]):
        refs[-1][at * size : (at + 1) * size, :] = ref[...]


def temporal_kernel(own, period, block, *refs):
    weight_refs, output_refs, (proj_ref, heads_ref) = refs[:2], refs[2:4], refs[-2:]
    groups = proj_ref.shape[1] // block
    row_refs, update_refs = refs[4 : -2 - 2 * groups], refs[-2 - 2 * groups : -2]
    rows = jnp.concatenate([ref[...] for ref in row_refs], axis=0)
    depth = weight_refs[0].shape[0]
    for core in range(2):
        proj_ref[core * depth : (core + 1) * depth, :] = dot(weight_refs[core][...], rows, 1, 1)
    heads = 2 * depth // (3 * HD)
    key_patch = lax.broadcasted_iota(jnp.int32, (block, block), 0) % period
    query_patch = lax.broadcasted_iota(jnp.int32, (block, block), 1) % period
    mask = key_patch == query_patch
    weights = joined(output_refs)
    for group in range(groups):
        cols = slice(group * block, (group + 1) * block)

        def part(head, at):
            start = (head * 3 + at) * HD
            return proj_ref[start : start + HD, cols]

        scores = []
        for head in range(heads):
            keys, query = part(head, 1).astype(BF16).T, part(head, 0).astype(BF16)
            scores.append(jnp.where(mask, dot(keys, query), -1e30))
        soft = soften(jnp.concatenate(scores, axis=1))
        for head in range(heads):
            mixed = mix(part(head, 2), soft[:, head * block : (head + 1) * block])
            heads_ref[head * HD : (head + 1) * HD, cols] = mixed
        mixed = heads_ref[:, cols].astype(BF16).T
        if own:
            kept, sent = halves(mixed, period)
            parts = dot(kept, weights), sent
        else:
            parts = halves(dot(mixed, weights), period)
        for ref, half in zip(update_refs[2 * group : 2 * group + 2], parts):
            ref[...] = half.astype(ref.dtype)


def sum_kernel(groups, *refs):
    piece_refs = refs[2 + 2 * groups :]
    period = piece_refs[0].shape[0] // 2
    for at, update in enumerate(total_updates(groups, refs[:2], refs[2:])):
        update = update.astype(BF16)
        for piece, ref in enumerate(piece_refs):
            rows = update[piece * period : (piece + 1) * period]
            ref[at * period : (at + 1) * period, :] = rows


def result_kernel(offsets, mod_ref, kept_ref, other_ref, *refs):
    piece_refs, out_ref = refs[:-1], refs[-1]
    period = kept_ref.shape[1]
    here = lax.axis_index("frame")
    for offset, ref in zip(offsets, piece_refs):
        there = here // 2 ^ offset
        for half, middle_ref in enumerate((kept_ref, other_ref)):
            update = ref[half * period : (half + 1) * period, :].astype(F32)
            middle = middle_ref[there].astype(F32)
            out_ref[2 * there + (here % 2 ^ half)] = (middle + mod_ref[5:6, :] * update).astype(
                BF16
            )


def call(body, operands, outs, scratch=(), limit=24):
    return pl.pallas_call(
        body,
        out_shape=outs,
        in_specs=[pl.BlockSpec(memory_space=pltpu.VMEM)] * len(operands),
        out_specs=[pl.BlockSpec(memory_space=pltpu.VMEM)] * len(outs),
        scratch_shapes=list(scratch),
        compiler_params=pltpu.CompilerParams(vmem_limit_bytes=limit * MIB),
        cost_estimate=pl.CostEstimate(flops=1, bytes_accessed=1, transcendentals=0),
    )(*operands)


def swap(value, axis, offset):
    size = lax.axis_size(axis)
    return lax.ppermute(value, axis, [(at, at ^ offset) for at in range(size)])


def after(value, *others):
    return lax.optimization_barrier((value, *others))[0]


def across(value):
    size = lax.axis_size("patch")
    return [swap(value, "patch", at) if at else value for at in range(0, size, 2)]


def both_cores(blocks):
    return [part for block in blocks for part in (block, swap(block, "patch", 1))]


def swap_diagonal(value, offset):
    frames, size = lax.axis_size("frame"), lax.axis_size("patch")
    pairs = [
        (frame * size + at, (frame ^ 1) * size + (at ^ offset))
        for frame in range(frames)
        for at in range(size)
    ]
    return lax.ppermute(value, ("frame", "patch"), pairs)


def per_device(tokens, modulation, spatial_qkv, spatial_out, temporal_qkv, temporal_out):
    _, rows, width = tokens.shape
    shard = spatial_out.shape[0]
    count, frames = lax.axis_size("patch"), lax.axis_size("frame")
    period = rows // frames
    pieces, groups = frames // 2, count // 2
    shape = jax.ShapeDtypeStruct

    first = pieces // 2
    offsets = (*reversed(range(first + 1, pieces)), 0, *reversed(range(1, first + 1)))

    def with_sister(weights, *others):
        return [weights, swap(after(weights, *others), "patch", 1)]

    def exchange_frames(parts):
        return [swap(part, "frame", 2 * at) if at else part for at, part in zip(offsets, parts)]

    def return_updates(own, far):
        same = [swap(part, "patch", 2 * at) for at, part in enumerate(far[::2], 1)]
        diagonal = [swap_diagonal(part, 2 * at) for at, part in enumerate(far[1::2], 1)]
        return [own[0], *same, own[1], *diagonal]

    def halves_shape(dtype):
        return shape((rows // 2, width), dtype)

    own_shapes = [halves_shape(F32), shape((rows // 2, 2 * shard), BF16)]
    far_shapes = [halves_shape(BF16)] * (2 * groups - 2)
    piece_shapes = [shape((2 * period, width), BF16)] * pieces

    sister = swap(tokens, "patch", 1)
    far = across(tokens)[1:]
    (near,) = call(
        near_kernel,
        (modulation, spatial_qkv, tokens, sister),
        [shape((3 * shard, 2 * rows), F32)],
    )
    (shared,) = call(
        functools.partial(share_kernel, period), (after(tokens, sister),), [halves_shape(BF16)]
    )
    paired = swap(shared, "frame", 1)
    out_pair = with_sister(spatial_out, near)
    far = both_cores([after(block, near, paired) for block in far])
    temporal_pair = with_sister(temporal_qkv, *far)
    late_pair = with_sister(temporal_out, *far)

    kept, sent = call(
        functools.partial(spatial_kernel, count),
        (modulation, spatial_qkv, near, *far),
        [shape((shard, groups * rows), BF16)] * 2,
        [pltpu.VMEM((3 * shard, (count - 2) * rows), F32), pltpu.VMEM((shard, count * rows), F32)],
    )
    received = swap(sent, "patch", 1)
    parts = call(
        functools.partial(partial_kernel, period),
        (kept, received, *out_pair),
        own_shapes + far_shapes,
    )
    updates = return_updates((parts[0], swap(parts[1], "frame", 1)), parts[2:])
    middle, middle_sent, *parts = call(
        functools.partial(middle_kernel, offsets, groups),
        (modulation, tokens, paired, *out_pair, *updates),
        [shape((pieces, period, width), BF16)] * 2 + piece_shapes,
        [pltpu.VMEM((pieces, 2 * period, width), BF16)],
    )
    arrived = exchange_frames(parts)
    half_shape = [halves_shape(BF16)]
    early = across(call(join_kernel, arrived[:first], half_shape)[0])
    late = across(call(join_kernel, arrived[first:], half_shape)[0])

    def attend_frames(own, segments, shapes):
        columns = len(segments) // 2 * rows
        return call(
            functools.partial(temporal_kernel, own, period, rows),
            (*temporal_pair, *late_pair, *segments),
            shapes,
            [pltpu.VMEM((6 * shard, columns), F32), pltpu.VMEM((2 * shard, columns), F32)],
        )

    own_early = after(early[0], *early[1:])
    middle_other = swap(after(middle_sent, *late[1:]), "frame", 1)
    kept, sent = attend_frames(True, [own_early, late[0]], own_shapes)
    received = swap(sent, "frame", 1)
    others = [part for pair in zip(early[1:], late[1:]) for part in pair]
    others = [after(part, received) for part in others]
    far_parts = attend_frames(False, others, far_shapes)
    updates = return_updates((after(kept, middle_other), received), far_parts)
    parts = call(
        functools.partial(sum_kernel, groups),
        (*late_pair, *updates),
        piece_shapes,
    )
    (result,) = call(
        functools.partial(result_kernel, offsets),
        (modulation, middle, middle_other, *exchange_frames(parts)),
        [shape((frames, period, width), BF16)],
    )
    return result.reshape(1, rows, width)


def solution(mesh):
    in_specs = (
        P("frame", "patch", None),
        P(),
        P("patch", None),
        P("patch", None),
        P("patch", None),
        P("patch", None),
    )
    out_specs = P("frame", "patch", None)
    return jax.shard_map(
        per_device, mesh=mesh, in_specs=in_specs, out_specs=out_specs, check_vma=False
    )
```

```python
import functools

import jax
import jax.numpy as jnp
from jax import lax
from jax.experimental import pallas as pl
from jax.experimental.pallas import tpu as pltpu
from jax.sharding import PartitionSpec as P

HD = 72
MIB = 1 << 20
LOG2E = 1.4426950408889634
F32 = jnp.float32
BF16 = jnp.bfloat16


def norm_rows(values, shift, scale):
    average = jnp.mean(values, axis=-1, keepdims=True)
    centred = values - average
    variance = jnp.mean(centred * centred, axis=-1, keepdims=True)
    normed = centred * lax.rsqrt(variance + 1e-06)
    return (normed * (1.0 + scale) + shift).astype(BF16)


def dot(left, right, left_dim=1, right_dim=0):
    return lax.dot_general(
        left, right, (((left_dim,), (right_dim,)), ((), ())), preferred_element_type=F32
    )


def soften(scores):
    top = jnp.max(scores, axis=0, keepdims=True)
    return jnp.exp2((scores - top) * (HD**-0.5 * LOG2E)).astype(BF16)


def mix(values, weights):
    ones = jnp.ones((8, values.shape[1]), F32)
    mixed = dot(jnp.concatenate([values, ones], axis=0).astype(BF16), weights)
    return mixed[:HD] * (1.0 / mixed[HD : HD + 1])


def project(mod_ref, weight_ref, token_refs, proj_ref):
    shift, scale = mod_ref[0:1, :], mod_ref[1:2, :]
    block = token_refs[0].shape[1]
    for at in range(0, len(token_refs), 2):
        rows = [norm_rows(ref[0].astype(F32), shift, scale) for ref in token_refs[at : at + 2]]
        rows = jnp.concatenate(rows, axis=0)
        proj_ref[:, at * block : (at + 2) * block] = dot(weight_ref[...], rows, 1, 1)


def near_kernel(mod_ref, weight_ref, own_ref, sister_ref, proj_ref):
    project(mod_ref, weight_ref, (own_ref, sister_ref), proj_ref)


def spatial_kernel(count, mod_ref, weight_ref, near_ref, *refs):
    token_refs, (kept_ref, sent_ref, far_ref, heads_ref) = refs[: count - 2], refs[count - 2 :]
    block = token_refs[0].shape[1]
    heads = weight_ref.shape[0] // (3 * HD)
    project(mod_ref, weight_ref, token_refs, far_ref)

    def whole(start):
        return jnp.concatenate([ref[start : start + HD, :] for ref in (near_ref, far_ref)], axis=1)

    def score(head, at):
        base = head * 3 * HD
        source, start = (near_ref, 0) if at == 0 else (far_ref, (at - 2) * block)
        query = source[base : base + HD, start : start + 2 * block].astype(BF16)
        return dot(whole(base + HD).astype(BF16).T, query)

    steps = [(head, at) for head in range(heads) for at in range(0, count, 2)]
    scores = score(*steps[0])
    for (head, at), later in zip(steps, [*steps[1:], None]):
        coming = score(*later) if later else None
        rows, cols = slice(head * HD, (head + 1) * HD), slice(at * block, (at + 2) * block)
        heads_ref[rows, cols] = mix(whole(head * 3 * HD + 2 * HD), soften(scores))
        scores = coming
    for at in range(count):
        out_ref = (kept_ref, sent_ref)[at % 2]
        cols = slice(at // 2 * block, (at // 2 + 1) * block)
        out_ref[:, cols] = heads_ref[:, at * block : (at + 1) * block].astype(BF16)


def halves(value, size):
    return [
        jnp.concatenate(
            [value[at : at + size] for at in range(first * size, value.shape[0], 2 * size)], axis=0
        )
        for first in range(2)
    ]


def of_this_half(value, size):
    even, odd = (half.astype(F32) for half in halves(value, size))
    first = lax.axis_index("frame") % 2 == 0
    return jnp.where(first, even, odd), jnp.where(first, odd, even)


def share_kernel(period, token_ref, sent_ref):
    sent_ref[...] = of_this_half(token_ref[0], period)[1].astype(BF16)


def joined(refs):
    return jnp.concatenate([ref[...] for ref in refs], axis=0)


def partial_kernel(period, *refs):
    head_refs, weights, out_refs = refs[:2], joined(refs[2:4]), refs[4:]
    block = 2 * out_refs[0].shape[0]
    for at in range(len(out_refs) // 2):
        cols = slice(at * block, (at + 1) * block)
        heads = jnp.concatenate([ref[:, cols] for ref in head_refs], axis=0).T
        if at == 0:
            kept, sent = (half.astype(BF16) for half in of_this_half(heads, period))
            parts = dot(kept, weights), sent
        else:
            parts = of_this_half(dot(heads, weights), period)
        for ref, part in zip(out_refs[2 * at : 2 * at + 2], parts):
            ref[...] = part.astype(ref.dtype)


def total_updates(groups, weight_refs, refs):
    kept = sum(ref[...].astype(F32) for ref in refs[:groups])
    paired = dot(refs[groups][...], joined(weight_refs))
    return kept, paired + sum(ref[...].astype(F32) for ref in refs[groups + 1 : 2 * groups])


def middle_kernel(pieces, groups, mod_ref, own_ref, paired_ref, *refs):
    kept_ref, sent_ref, normed_ref = refs[2 + 2 * groups :]
    updates = total_updates(groups, refs[:2], refs[2:])
    _, period, width = kept_ref.shape
    inputs = (of_this_half(own_ref[0], period)[0], paired_ref[...])
    for at, (tokens, middle_ref) in enumerate(zip(inputs, (kept_ref, sent_ref))):
        update = updates[at]
        middle = (tokens.astype(F32) + mod_ref[2:3, :] * update).astype(BF16)
        normed = norm_rows(middle.astype(F32), mod_ref[3:4, :], mod_ref[4:5, :])
        for piece in range(pieces):
            rows = slice(piece * period, (piece + 1) * period)
            middle_ref[piece] = middle[rows]
            normed_ref[piece, at * period : (at + 1) * period, :] = normed[rows]


def temporal_kernel(own, period, block, *refs):
    weight_refs, output_refs, (proj_ref, heads_ref) = refs[:2], refs[2:4], refs[-2:]
    groups = proj_ref.shape[1] // block
    row_refs, update_refs = refs[4 : -2 - 2 * groups], refs[-2 - 2 * groups : -2]
    rows = jnp.concatenate([ref[...] for ref in row_refs], axis=0)
    depth = weight_refs[0].shape[0]
    for core in range(2):
        proj_ref[core * depth : (core + 1) * depth, :] = dot(weight_refs[core][...], rows, 1, 1)
    heads = 2 * depth // (3 * HD)
    key_patch = lax.broadcasted_iota(jnp.int32, (block, block), 0) % period
    query_patch = lax.broadcasted_iota(jnp.int32, (block, block), 1) % period
    mask = key_patch == query_patch
    weights = joined(output_refs)
    for group in range(groups):
        cols = slice(group * block, (group + 1) * block)

        def part(head, at):
            start = (head * 3 + at) * HD
            return proj_ref[start : start + HD, cols]

        scores = []
        for head in range(heads):
            keys, query = part(head, 1).astype(BF16).T, part(head, 0).astype(BF16)
            scores.append(jnp.where(mask, dot(keys, query), -1e30))
        soft = soften(jnp.concatenate(scores, axis=1))
        for head in range(heads):
            mixed = mix(part(head, 2), soft[:, head * block : (head + 1) * block])
            heads_ref[head * HD : (head + 1) * HD, cols] = mixed
        mixed = heads_ref[:, cols].astype(BF16).T
        if own:
            kept, sent = halves(mixed, period)
            parts = dot(kept, weights), sent
        else:
            parts = halves(dot(mixed, weights), period)
        for ref, half in zip(update_refs[2 * group : 2 * group + 2], parts):
            ref[...] = half.astype(ref.dtype)


def sum_kernel(groups, *refs):
    out_ref = refs[-1]
    pieces, period = out_ref.shape[0], out_ref.shape[1] // 2
    for at, update in enumerate(total_updates(groups, refs[:2], refs[2:])):
        update = update.astype(BF16)
        for piece in range(pieces):
            rows = update[piece * period : (piece + 1) * period]
            out_ref[piece, at * period : (at + 1) * period, :] = rows


def result_kernel(mod_ref, kept_ref, other_ref, update_ref, out_ref):
    pieces, period, _ = kept_ref.shape
    here = lax.axis_index("frame") % 2
    for piece in range(pieces):
        for half, middle_ref in enumerate((kept_ref, other_ref)):
            update = update_ref[piece, half * period : (half + 1) * period, :].astype(F32)
            middle = middle_ref[piece].astype(F32) + mod_ref[5:6, :] * update
            out_ref[2 * piece + (here ^ half)] = middle.astype(BF16)


def call(body, operands, outs, scratch=(), limit=24):
    return pl.pallas_call(
        body,
        out_shape=outs,
        in_specs=[pl.BlockSpec(memory_space=pltpu.VMEM)] * len(operands),
        out_specs=[pl.BlockSpec(memory_space=pltpu.VMEM)] * len(outs),
        scratch_shapes=list(scratch),
        compiler_params=pltpu.CompilerParams(vmem_limit_bytes=limit * MIB),
        cost_estimate=pl.CostEstimate(flops=1, bytes_accessed=1, transcendentals=0),
    )(*operands)


def swap(value, axis, offset):
    size = lax.axis_size(axis)
    return lax.ppermute(value, axis, [(at, at ^ offset) for at in range(size)])


def after(value, *others):
    return lax.optimization_barrier((value, *others))[0]


def across(value):
    size = lax.axis_size("patch")
    return [swap(value, "patch", at) if at else value for at in range(0, size, 2)]


def both_cores(blocks):
    return [part for block in blocks for part in (block, swap(block, "patch", 1))]


def swap_diagonal(value, offset):
    frames, size = lax.axis_size("frame"), lax.axis_size("patch")
    pairs = [
        (frame * size + at, (frame ^ 1) * size + (at ^ offset))
        for frame in range(frames)
        for at in range(size)
    ]
    return lax.ppermute(value, ("frame", "patch"), pairs)


def per_device(tokens, modulation, spatial_qkv, spatial_out, temporal_qkv, temporal_out):
    _, rows, width = tokens.shape
    shard = spatial_out.shape[0]
    count, frames = lax.axis_size("patch"), lax.axis_size("frame")
    period = rows // frames
    pieces, groups = frames // 2, count // 2
    shape = jax.ShapeDtypeStruct

    def with_sister(weights, *others):
        return [weights, swap(after(weights, *others), "patch", 1)]

    def exchange_frames(blocks):
        lines = [list(range(first, frames, 2)) for first in range(2)]
        return lax.all_to_all(
            blocks, "frame", split_axis=0, concat_axis=0, tiled=True, axis_index_groups=lines
        )

    def return_updates(own, far):
        same = [swap(part, "patch", 2 * at) for at, part in enumerate(far[::2], 1)]
        diagonal = [swap_diagonal(part, 2 * at) for at, part in enumerate(far[1::2], 1)]
        return [own[0], *same, own[1], *diagonal]

    def halves_shape(dtype):
        return shape((rows // 2, width), dtype)

    own_shapes = [halves_shape(F32), shape((rows // 2, 2 * shard), BF16)]
    far_shapes = [halves_shape(BF16)] * (2 * groups - 2)
    blocks_shape = shape((pieces, 2 * period, width), BF16)

    sister = swap(tokens, "patch", 1)
    far = across(tokens)[1:]
    (near,) = call(
        near_kernel,
        (modulation, spatial_qkv, tokens, sister),
        [shape((3 * shard, 2 * rows), F32)],
    )
    (shared,) = call(
        functools.partial(share_kernel, period), (after(tokens, sister),), [halves_shape(BF16)]
    )
    paired = swap(shared, "frame", 1)
    out_pair = with_sister(spatial_out, near)
    far = both_cores([after(block, near, paired) for block in far])
    temporal_pair = with_sister(temporal_qkv, *far)
    late_pair = with_sister(temporal_out, *far)

    kept, sent = call(
        functools.partial(spatial_kernel, count),
        (modulation, spatial_qkv, near, *far),
        [shape((shard, groups * rows), BF16)] * 2,
        [pltpu.VMEM((3 * shard, (count - 2) * rows), F32), pltpu.VMEM((shard, count * rows), F32)],
    )
    parts = call(
        functools.partial(partial_kernel, period),
        (kept, swap(sent, "patch", 1), *out_pair),
        own_shapes + far_shapes,
    )
    updates = return_updates((parts[0], swap(parts[1], "frame", 1)), parts[2:])
    middle, middle_sent, normed = call(
        functools.partial(middle_kernel, pieces, groups),
        (modulation, tokens, paired, *out_pair, *updates),
        [shape((pieces, period, width), BF16)] * 2 + [blocks_shape],
    )
    segment = exchange_frames(normed).reshape(rows, width)
    segments = across(segment)

    def attend_frames(own, segments, shapes):
        columns = len(segments) * rows
        return call(
            functools.partial(temporal_kernel, own, period, rows),
            (*temporal_pair, *late_pair, *segments),
            shapes,
            [pltpu.VMEM((6 * shard, columns), F32), pltpu.VMEM((2 * shard, columns), F32)],
        )

    kept, sent = attend_frames(True, [segment], own_shapes)
    received = swap(sent, "frame", 1)
    middle_other = swap(after(middle_sent, segment), "frame", 1)
    others = [after(block, received, middle_other) for block in segments[1:]]
    far_parts = attend_frames(False, others, far_shapes)
    updates = return_updates((kept, received), far_parts)
    (update,) = call(
        functools.partial(sum_kernel, groups),
        (*late_pair, *updates),
        [blocks_shape],
    )
    (result,) = call(
        result_kernel,
        (modulation, middle, middle_other, exchange_frames(update)),
        [shape((frames, period, width), BF16)],
    )
    return result.reshape(1, rows, width)


def solution(mesh):
    in_specs = (
        P("frame", "patch", None),
        P(),
        P("patch", None),
        P("patch", None),
        P("patch", None),
        P("patch", None),
    )
    out_specs = P("frame", "patch", None)
    return jax.shard_map(
        per_device, mesh=mesh, in_specs=in_specs, out_specs=out_specs, check_vma=False
    )
```

```python
import functools

import jax
import jax.numpy as jnp
from jax import lax
from jax.experimental import pallas as pl
from jax.experimental.pallas import tpu as pltpu
from jax.sharding import PartitionSpec as P

HD = 72
MIB = 1 << 20
LOG2E = 1.4426950408889634
F32 = jnp.float32
BF16 = jnp.bfloat16


def norm_rows(values, shift, scale):
    average = jnp.mean(values, axis=-1, keepdims=True)
    centred = values - average
    variance = jnp.mean(centred * centred, axis=-1, keepdims=True)
    normed = centred * lax.rsqrt(variance + 1e-06)
    return (normed * (1.0 + scale) + shift).astype(BF16)


def dot(left, right, left_dim=1, right_dim=0):
    return lax.dot_general(
        left, right, (((left_dim,), (right_dim,)), ((), ())), preferred_element_type=F32
    )


def soften(scores):
    top = jnp.max(scores, axis=0, keepdims=True)
    return jnp.exp2((scores - top) * (HD**-0.5 * LOG2E)).astype(BF16)


def mix(values, weights):
    ones = jnp.ones((8, values.shape[1]), F32)
    mixed = dot(jnp.concatenate([values, ones], axis=0).astype(BF16), weights)
    return mixed[:HD] * (1.0 / mixed[HD : HD + 1])


def project(mod_ref, weight_ref, token_refs, proj_ref):
    shift, scale = mod_ref[0:1, :], mod_ref[1:2, :]
    block = token_refs[0].shape[1]
    for at in range(0, len(token_refs), 2):
        rows = [norm_rows(ref[0].astype(F32), shift, scale) for ref in token_refs[at : at + 2]]
        rows = jnp.concatenate(rows, axis=0)
        proj_ref[:, at * block : (at + 2) * block] = dot(weight_ref[...], rows, 1, 1)


def near_kernel(mod_ref, weight_ref, own_ref, sister_ref, proj_ref):
    project(mod_ref, weight_ref, (own_ref, sister_ref), proj_ref)


def spatial_kernel(count, mod_ref, weight_ref, near_ref, *refs):
    token_refs, (kept_ref, sent_ref, far_ref, heads_ref) = refs[: count - 2], refs[count - 2 :]
    block = token_refs[0].shape[1]
    heads = weight_ref.shape[0] // (3 * HD)
    project(mod_ref, weight_ref, token_refs, far_ref)

    def whole(start):
        return jnp.concatenate([ref[start : start + HD, :] for ref in (near_ref, far_ref)], axis=1)

    def score(head, at):
        base = head * 3 * HD
        source, start = (near_ref, 0) if at == 0 else (far_ref, (at - 2) * block)
        query = source[base : base + HD, start : start + 2 * block].astype(BF16)
        return dot(whole(base + HD).astype(BF16).T, query)

    steps = [(head, at) for head in range(heads) for at in range(0, count, 2)]
    scores = score(*steps[0])
    for (head, at), later in zip(steps, [*steps[1:], None]):
        coming = score(*later) if later else None
        rows, cols = slice(head * HD, (head + 1) * HD), slice(at * block, (at + 2) * block)
        heads_ref[rows, cols] = mix(whole(head * 3 * HD + 2 * HD), soften(scores))
        scores = coming
    for at in range(count):
        out_ref = (kept_ref, sent_ref)[at % 2]
        cols = slice(at // 2 * block, (at // 2 + 1) * block)
        out_ref[:, cols] = heads_ref[:, at * block : (at + 1) * block].astype(BF16)


def halves(value, size):
    return [
        jnp.concatenate(
            [value[at : at + size] for at in range(first * size, value.shape[0], 2 * size)], axis=0
        )
        for first in range(2)
    ]


def of_this_half(value, size):
    even, odd = (half.astype(F32) for half in halves(value, size))
    first = lax.axis_index("frame") % 2 == 0
    return jnp.where(first, even, odd), jnp.where(first, odd, even)


def share_kernel(period, token_ref, sent_ref):
    sent_ref[...] = of_this_half(token_ref[0], period)[1].astype(BF16)


def joined(refs):
    return jnp.concatenate([ref[...] for ref in refs], axis=0)


def partial_kernel(period, *refs):
    head_refs, weights, out_refs = refs[:2], joined(refs[2:4]), refs[4:]
    block = 2 * out_refs[0].shape[0]
    for at in range(len(out_refs) // 2):
        cols = slice(at * block, (at + 1) * block)
        heads = jnp.concatenate([ref[:, cols] for ref in head_refs], axis=0).T
        if at == 0:
            kept, sent = (half.astype(BF16) for half in of_this_half(heads, period))
            parts = dot(kept, weights), sent
        else:
            parts = of_this_half(dot(heads, weights), period)
        for ref, part in zip(out_refs[2 * at : 2 * at + 2], parts):
            ref[...] = part.astype(ref.dtype)


def total_updates(groups, weight_refs, refs):
    kept = sum(ref[...].astype(F32) for ref in refs[:groups])
    paired = dot(refs[groups][...], joined(weight_refs))
    return kept, paired + sum(ref[...].astype(F32) for ref in refs[groups + 1 : 2 * groups])


def middle_kernel(pieces, groups, mod_ref, own_ref, paired_ref, *refs):
    kept_ref, sent_ref, *piece_refs, scratch = refs[2 + 2 * groups :]
    updates = total_updates(groups, refs[:2], refs[2:])
    _, period, width = kept_ref.shape
    inputs = (of_this_half(own_ref[0], period)[0], paired_ref[...])
    for at, (tokens, middle_ref) in enumerate(zip(inputs, (kept_ref, sent_ref))):
        update = updates[at]
        middle = (tokens.astype(F32) + mod_ref[2:3, :] * update).astype(BF16)
        normed = norm_rows(middle.astype(F32), mod_ref[3:4, :], mod_ref[4:5, :])
        for piece in range(pieces):
            rows = slice(piece * period, (piece + 1) * period)
            middle_ref[piece] = middle[rows]
            scratch[piece, at * period : (at + 1) * period, :] = normed[rows]
    here = lax.axis_index("frame") // 2
    for at, ref in enumerate(piece_refs):
        ref[...] = scratch[here ^ (pieces - 1 - at)]


def join_kernel(*refs):
    size = refs[0].shape[0]
    for at, ref in enumerate(refs[:-1]):
        refs[-1][at * size : (at + 1) * size, :] = ref[...]


def temporal_kernel(own, period, block, *refs):
    weight_refs, output_refs, (proj_ref, heads_ref) = refs[:2], refs[2:4], refs[-2:]
    groups = proj_ref.shape[1] // block
    row_refs, update_refs = refs[4 : -2 - 2 * groups], refs[-2 - 2 * groups : -2]
    rows = jnp.concatenate([ref[...] for ref in row_refs], axis=0)
    depth = weight_refs[0].shape[0]
    for core in range(2):
        proj_ref[core * depth : (core + 1) * depth, :] = dot(weight_refs[core][...], rows, 1, 1)
    heads = 2 * depth // (3 * HD)
    key_patch = lax.broadcasted_iota(jnp.int32, (block, block), 0) % period
    query_patch = lax.broadcasted_iota(jnp.int32, (block, block), 1) % period
    mask = key_patch == query_patch
    weights = joined(output_refs)
    for group in range(groups):
        cols = slice(group * block, (group + 1) * block)

        def part(head, at):
            start = (head * 3 + at) * HD
            return proj_ref[start : start + HD, cols]

        scores = []
        for head in range(heads):
            keys, query = part(head, 1).astype(BF16).T, part(head, 0).astype(BF16)
            scores.append(jnp.where(mask, dot(keys, query), -1e30))
        soft = soften(jnp.concatenate(scores, axis=1))
        for head in range(heads):
            mixed = mix(part(head, 2), soft[:, head * block : (head + 1) * block])
            heads_ref[head * HD : (head + 1) * HD, cols] = mixed
        mixed = heads_ref[:, cols].astype(BF16).T
        if own:
            kept, sent = halves(mixed, period)
            parts = dot(kept, weights), sent
        else:
            parts = halves(dot(mixed, weights), period)
        for ref, half in zip(update_refs[2 * group : 2 * group + 2], parts):
            ref[...] = half.astype(ref.dtype)


def sum_kernel(groups, *refs):
    piece_refs = refs[2 + 2 * groups :]
    period = piece_refs[0].shape[0] // 2
    for at, update in enumerate(total_updates(groups, refs[:2], refs[2:])):
        update = update.astype(BF16)
        for piece, ref in enumerate(piece_refs):
            rows = update[piece * period : (piece + 1) * period]
            ref[at * period : (at + 1) * period, :] = rows


def result_kernel(pieces, mod_ref, kept_ref, other_ref, *refs):
    piece_refs, out_ref = refs[:-1], refs[-1]
    period = kept_ref.shape[1]
    here = lax.axis_index("frame")
    for at, ref in enumerate(piece_refs):
        there = here // 2 ^ (pieces - 1 - at)
        for half, middle_ref in enumerate((kept_ref, other_ref)):
            update = ref[half * period : (half + 1) * period, :].astype(F32)
            middle = middle_ref[there].astype(F32)
            out_ref[2 * there + (here % 2 ^ half)] = (middle + mod_ref[5:6, :] * update).astype(
                BF16
            )


def call(body, operands, outs, scratch=(), limit=24):
    return pl.pallas_call(
        body,
        out_shape=outs,
        in_specs=[pl.BlockSpec(memory_space=pltpu.VMEM)] * len(operands),
        out_specs=[pl.BlockSpec(memory_space=pltpu.VMEM)] * len(outs),
        scratch_shapes=list(scratch),
        compiler_params=pltpu.CompilerParams(vmem_limit_bytes=limit * MIB),
        cost_estimate=pl.CostEstimate(flops=1, bytes_accessed=1, transcendentals=0),
    )(*operands)


def swap(value, axis, offset):
    size = lax.axis_size(axis)
    return lax.ppermute(value, axis, [(at, at ^ offset) for at in range(size)])


def after(value, *others):
    return lax.optimization_barrier((value, *others))[0]


def across(value):
    size = lax.axis_size("patch")
    return [swap(value, "patch", at) if at else value for at in range(0, size, 2)]


def both_cores(blocks):
    return [part for block in blocks for part in (block, swap(block, "patch", 1))]


def swap_diagonal(value, offset):
    frames, size = lax.axis_size("frame"), lax.axis_size("patch")
    pairs = [
        (frame * size + at, (frame ^ 1) * size + (at ^ offset))
        for frame in range(frames)
        for at in range(size)
    ]
    return lax.ppermute(value, ("frame", "patch"), pairs)


def per_device(tokens, modulation, spatial_qkv, spatial_out, temporal_qkv, temporal_out):
    _, rows, width = tokens.shape
    shard = spatial_out.shape[0]
    count, frames = lax.axis_size("patch"), lax.axis_size("frame")
    period = rows // frames
    pieces, groups = frames // 2, count // 2
    shape = jax.ShapeDtypeStruct

    def with_sister(weights, *others):
        return [weights, swap(after(weights, *others), "patch", 1)]

    def exchange_frames(parts):
        offsets = reversed(range(pieces))
        return [swap(part, "frame", 2 * at) if at else part for at, part in zip(offsets, parts)]

    def return_updates(own, far):
        same = [swap(part, "patch", 2 * at) for at, part in enumerate(far[::2], 1)]
        diagonal = [swap_diagonal(part, 2 * at) for at, part in enumerate(far[1::2], 1)]
        return [own[0], *same, own[1], *diagonal]

    def halves_shape(dtype):
        return shape((rows // 2, width), dtype)

    own_shapes = [halves_shape(F32), shape((rows // 2, 2 * shard), BF16)]
    far_shapes = [halves_shape(BF16)] * (2 * groups - 2)
    piece_shapes = [shape((2 * period, width), BF16)] * pieces

    sister = swap(tokens, "patch", 1)
    far = across(tokens)[1:]
    (near,) = call(
        near_kernel,
        (modulation, spatial_qkv, tokens, sister),
        [shape((3 * shard, 2 * rows), F32)],
    )
    (shared,) = call(
        functools.partial(share_kernel, period), (after(tokens, sister),), [halves_shape(BF16)]
    )
    paired = swap(shared, "frame", 1)
    out_pair = with_sister(spatial_out, near)
    far = both_cores([after(block, near, paired) for block in far])
    temporal_pair = with_sister(temporal_qkv, *far)

    kept, sent = call(
        functools.partial(spatial_kernel, count),
        (modulation, spatial_qkv, near, *far),
        [shape((shard, groups * rows), BF16)] * 2,
        [pltpu.VMEM((3 * shard, (count - 2) * rows), F32), pltpu.VMEM((shard, count * rows), F32)],
    )
    parts = call(
        functools.partial(partial_kernel, period),
        (kept, swap(sent, "patch", 1), *out_pair),
        own_shapes + far_shapes,
    )
    late_pair = with_sister(temporal_out, parts[0])
    updates = return_updates((parts[0], swap(parts[1], "frame", 1)), parts[2:])
    middle, middle_sent, *parts = call(
        functools.partial(middle_kernel, pieces, groups),
        (modulation, tokens, paired, *out_pair, *updates),
        [shape((pieces, period, width), BF16)] * 2 + piece_shapes,
        [pltpu.VMEM((pieces, 2 * period, width), BF16)],
    )
    arrived = exchange_frames(parts)
    (segment,) = call(join_kernel, arrived, [shape((rows, width), BF16)])
    segments = across(segment)

    def attend_frames(own, segments, shapes):
        columns = len(segments) * rows
        return call(
            functools.partial(temporal_kernel, own, period, rows),
            (*temporal_pair, *late_pair, *segments),
            shapes,
            [pltpu.VMEM((6 * shard, columns), F32), pltpu.VMEM((2 * shard, columns), F32)],
        )

    kept, sent = attend_frames(True, [segment], own_shapes)
    received = swap(sent, "frame", 1)
    middle_other = swap(after(middle_sent, segment), "frame", 1)
    others = [after(block, received) for block in segments[1:]]
    far_parts = attend_frames(False, others, far_shapes)
    updates = return_updates((kept, received), far_parts)
    parts = call(
        functools.partial(sum_kernel, groups),
        (*late_pair, *updates),
        piece_shapes,
    )
    (result,) = call(
        functools.partial(result_kernel, pieces),
        (modulation, middle, middle_other, *exchange_frames(parts)),
        [shape((frames, period, width), BF16)],
    )
    return result.reshape(1, rows, width)


def solution(mesh):
    in_specs = (
        P("frame", "patch", None),
        P(),
        P("patch", None),
        P("patch", None),
        P("patch", None),
        P("patch", None),
    )
    out_specs = P("frame", "patch", None)
    return jax.shard_map(
        per_device, mesh=mesh, in_specs=in_specs, out_specs=out_specs, check_vma=False
    )
```

```python
import functools

import jax
import jax.numpy as jnp
from jax import lax
from jax.experimental import pallas as pl
from jax.experimental.pallas import tpu as pltpu
from jax.sharding import PartitionSpec as P

HD = 72
MIB = 1 << 20
LOG2E = 1.4426950408889634
F32 = jnp.float32
BF16 = jnp.bfloat16


def norm_rows(values, shift, scale):
    average = jnp.mean(values, axis=-1, keepdims=True)
    centred = values - average
    variance = jnp.mean(centred * centred, axis=-1, keepdims=True)
    normed = centred * lax.rsqrt(variance + 1e-06)
    return (normed * (1.0 + scale) + shift).astype(BF16)


def dot(left, right, left_dim=1, right_dim=0):
    return lax.dot_general(
        left, right, (((left_dim,), (right_dim,)), ((), ())), preferred_element_type=F32
    )


def soften(scores):
    top = jnp.max(scores, axis=0, keepdims=True)
    return jnp.exp2((scores - top) * (HD**-0.5 * LOG2E)).astype(BF16)


def mix(values, weights):
    ones = jnp.ones((8, values.shape[1]), F32)
    mixed = dot(jnp.concatenate([values, ones], axis=0).astype(BF16), weights)
    return mixed[:HD] * (1.0 / mixed[HD : HD + 1])


def project(mod_ref, weight_ref, token_refs, proj_ref):
    shift, scale = mod_ref[0:1, :], mod_ref[1:2, :]
    block = token_refs[0].shape[1]
    for at in range(0, len(token_refs), 2):
        rows = [norm_rows(ref[0].astype(F32), shift, scale) for ref in token_refs[at : at + 2]]
        rows = jnp.concatenate(rows, axis=0)
        proj_ref[:, at * block : (at + 2) * block] = dot(weight_ref[...], rows, 1, 1)


def near_kernel(mod_ref, weight_ref, own_ref, sister_ref, proj_ref):
    project(mod_ref, weight_ref, (own_ref, sister_ref), proj_ref)


def spatial_kernel(count, mod_ref, weight_ref, near_ref, *refs):
    token_refs, (kept_ref, sent_ref, far_ref, heads_ref) = refs[: count - 2], refs[count - 2 :]
    block = token_refs[0].shape[1]
    heads = weight_ref.shape[0] // (3 * HD)
    project(mod_ref, weight_ref, token_refs, far_ref)

    def whole(start):
        return jnp.concatenate([ref[start : start + HD, :] for ref in (near_ref, far_ref)], axis=1)

    def score(head, at):
        base = head * 3 * HD
        source, start = (near_ref, 0) if at == 0 else (far_ref, (at - 2) * block)
        query = source[base : base + HD, start : start + 2 * block].astype(BF16)
        return dot(whole(base + HD).astype(BF16).T, query)

    steps = [(head, at) for head in range(heads) for at in range(0, count, 2)]
    scores = score(*steps[0])
    for (head, at), later in zip(steps, [*steps[1:], None]):
        coming = score(*later) if later else None
        rows, cols = slice(head * HD, (head + 1) * HD), slice(at * block, (at + 2) * block)
        heads_ref[rows, cols] = mix(whole(head * 3 * HD + 2 * HD), soften(scores))
        scores = coming
    for at in range(count):
        out_ref = (kept_ref, sent_ref)[at % 2]
        cols = slice(at // 2 * block, (at // 2 + 1) * block)
        out_ref[:, cols] = heads_ref[:, at * block : (at + 1) * block].astype(BF16)


def halves(value, size):
    return [
        jnp.concatenate(
            [value[at : at + size] for at in range(first * size, value.shape[0], 2 * size)], axis=0
        )
        for first in range(2)
    ]


def of_this_half(value, size):
    even, odd = (half.astype(F32) for half in halves(value, size))
    first = lax.axis_index("frame") % 2 == 0
    return jnp.where(first, even, odd), jnp.where(first, odd, even)


def share_kernel(period, token_ref, sent_ref):
    sent_ref[...] = of_this_half(token_ref[0], period)[1].astype(BF16)


def joined(refs):
    return jnp.concatenate([ref[...] for ref in refs], axis=0)


def partial_kernel(period, *refs):
    head_refs, weights, out_refs = refs[:2], joined(refs[2:4]), refs[4:]
    block = 2 * out_refs[0].shape[0]
    for at in range(len(out_refs) // 2):
        cols = slice(at * block, (at + 1) * block)
        heads = jnp.concatenate([ref[:, cols] for ref in head_refs], axis=0).T
        if at == 0:
            kept, sent = (half.astype(BF16) for half in of_this_half(heads, period))
            parts = dot(kept, weights), sent
        else:
            parts = of_this_half(dot(heads, weights), period)
        for ref, part in zip(out_refs[2 * at : 2 * at + 2], parts):
            ref[...] = part.astype(ref.dtype)


def total_updates(count, weight_refs, refs):
    kept = sum(ref[...].astype(F32) for ref in refs[:count])
    paired = dot(refs[count][...], joined(weight_refs))
    return kept, paired + sum(ref[...].astype(F32) for ref in refs[count + 1 : 2 * count])


def middle_kernel(pieces, count, mod_ref, own_ref, paired_ref, *refs):
    kept_ref, sent_ref, *piece_refs, scratch = refs[2 + 2 * count :]
    updates = total_updates(count, refs[:2], refs[2:])
    _, period, width = kept_ref.shape
    inputs = (of_this_half(own_ref[0], period)[0], paired_ref[...])
    for at, (tokens, middle_ref) in enumerate(zip(inputs, (kept_ref, sent_ref))):
        update = updates[at]
        middle = (tokens.astype(F32) + mod_ref[2:3, :] * update).astype(BF16)
        normed = norm_rows(middle.astype(F32), mod_ref[3:4, :], mod_ref[4:5, :])
        for piece in range(pieces):
            rows = slice(piece * period, (piece + 1) * period)
            middle_ref[piece] = middle[rows]
            scratch[piece, at * period : (at + 1) * period, :] = normed[rows]
    here = lax.axis_index("frame") // 2
    for at, ref in enumerate(piece_refs):
        ref[...] = scratch[here ^ (pieces - 1 - at)]


def join_kernel(*refs):
    size = refs[0].shape[0]
    for at, ref in enumerate(refs[:-1]):
        refs[-1][at * size : (at + 1) * size, :] = ref[...]


def temporal_kernel(own, period, block, *refs):
    weight_refs, output_refs, (proj_ref, heads_ref) = refs[:2], refs[2:4], refs[-2:]
    groups = proj_ref.shape[1] // block
    row_refs, update_refs = refs[4 : -2 - 2 * groups], refs[-2 - 2 * groups : -2]
    rows = jnp.concatenate([ref[...] for ref in row_refs], axis=0)
    depth = weight_refs[0].shape[0]
    for core in range(2):
        proj_ref[core * depth : (core + 1) * depth, :] = dot(weight_refs[core][...], rows, 1, 1)
    heads = 2 * depth // (3 * HD)
    key_patch = lax.broadcasted_iota(jnp.int32, (block, block), 0) % period
    query_patch = lax.broadcasted_iota(jnp.int32, (block, block), 1) % period
    mask = key_patch == query_patch
    weights = joined(output_refs)
    for group in range(groups):
        cols = slice(group * block, (group + 1) * block)

        def part(head, at):
            start = (head * 3 + at) * HD
            return proj_ref[start : start + HD, cols]

        scores = []
        for head in range(heads):
            keys, query = part(head, 1).astype(BF16).T, part(head, 0).astype(BF16)
            scores.append(jnp.where(mask, dot(keys, query), -1e30))
        soft = soften(jnp.concatenate(scores, axis=1))
        for head in range(heads):
            mixed = mix(part(head, 2), soft[:, head * block : (head + 1) * block])
            heads_ref[head * HD : (head + 1) * HD, cols] = mixed
        mixed = heads_ref[:, cols].astype(BF16).T
        if own:
            kept, sent = halves(mixed, period)
            parts = dot(kept, weights), sent
        else:
            parts = halves(dot(mixed, weights), period)
        for ref, half in zip(update_refs[2 * group : 2 * group + 2], parts):
            ref[...] = half.astype(ref.dtype)


def sum_kernel(count, *refs):
    piece_refs = refs[2 + 2 * count :]
    period = piece_refs[0].shape[0] // 2
    for at, update in enumerate(total_updates(count, refs[:2], refs[2:])):
        update = update.astype(BF16)
        for piece, ref in enumerate(piece_refs):
            rows = update[piece * period : (piece + 1) * period]
            ref[at * period : (at + 1) * period, :] = rows


def result_kernel(pieces, mod_ref, kept_ref, other_ref, *refs):
    piece_refs, out_ref = refs[:-1], refs[-1]
    period = kept_ref.shape[1]
    here = lax.axis_index("frame")
    for at, ref in enumerate(piece_refs):
        there = here // 2 ^ (pieces - 1 - at)
        for half, middle_ref in enumerate((kept_ref, other_ref)):
            update = ref[half * period : (half + 1) * period, :].astype(F32)
            middle = middle_ref[there].astype(F32)
            out_ref[2 * there + (here % 2 ^ half)] = (middle + mod_ref[5:6, :] * update).astype(
                BF16
            )


def call(body, operands, outs, scratch=(), limit=24):
    return pl.pallas_call(
        body,
        out_shape=outs,
        in_specs=[pl.BlockSpec(memory_space=pltpu.VMEM)] * len(operands),
        out_specs=[pl.BlockSpec(memory_space=pltpu.VMEM)] * len(outs),
        scratch_shapes=list(scratch),
        compiler_params=pltpu.CompilerParams(vmem_limit_bytes=limit * MIB),
        cost_estimate=pl.CostEstimate(flops=1, bytes_accessed=1, transcendentals=0),
    )(*operands)


def swap(value, axis, offset):
    size = lax.axis_size(axis)
    return lax.ppermute(value, axis, [(at, at ^ offset) for at in range(size)])


def after(value, *others):
    return lax.optimization_barrier((value, *others))[0]


def across(value):
    size = lax.axis_size("patch")
    return [swap(value, "patch", at) if at else value for at in range(0, size, 2)]


def both_cores(blocks):
    return [part for block in blocks for part in (block, swap(block, "patch", 1))]


def swap_far(value, offset, paired, cores=(0, 1)):
    frames, size = lax.axis_size("frame"), lax.axis_size("patch")
    pairs = [
        (frame * size + at, (frame ^ paired) * size + (at ^ offset))
        for frame in range(frames)
        for at in range(size)
        if at % 2 in cores
    ]
    return lax.ppermute(value, ("frame", "patch"), pairs)


def per_device(tokens, modulation, spatial_qkv, spatial_out, temporal_qkv, temporal_out):
    _, rows, width = tokens.shape
    shard = spatial_out.shape[0]
    count, frames = lax.axis_size("patch"), lax.axis_size("frame")
    period = rows // frames
    pieces, groups = frames // 2, count // 2
    shape = jax.ShapeDtypeStruct

    def with_sister(weights, *others):
        return [weights, swap(after(weights, *others), "patch", 1)]

    def exchange_frames(parts):
        offsets = reversed(range(pieces))
        return [swap(part, "frame", 2 * at) if at else part for at, part in zip(offsets, parts)]

    def swap_updates(far, cores=(0, 1)):
        return [
            [swap_far(part, 2 * at, paired, cores) for at, part in enumerate(far[paired::2], 1)]
            for paired in range(2)
        ]

    def halves_shape(dtype):
        return shape((rows // 2, width), dtype)

    own_shapes = [halves_shape(F32), shape((rows // 2, 2 * shard), BF16)]
    far_shapes = [halves_shape(BF16)] * (2 * groups - 2)
    piece_shapes = [shape((2 * period, width), BF16)] * pieces

    sister = swap(tokens, "patch", 1)
    far = across(tokens)[1:]
    (near,) = call(
        near_kernel,
        (modulation, spatial_qkv, tokens, sister),
        [shape((3 * shard, 2 * rows), F32)],
    )
    (shared,) = call(
        functools.partial(share_kernel, period), (after(tokens, sister),), [halves_shape(BF16)]
    )
    paired = swap(shared, "frame", 1)
    out_pair = with_sister(spatial_out, near)
    far = both_cores([after(block, near, paired) for block in far])
    temporal_pair = with_sister(temporal_qkv, *far)

    kept, sent = call(
        functools.partial(spatial_kernel, count),
        (modulation, spatial_qkv, near, *far),
        [shape((shard, groups * rows), BF16)] * 2,
        [pltpu.VMEM((3 * shard, (count - 2) * rows), F32), pltpu.VMEM((shard, count * rows), F32)],
    )
    parts = call(
        functools.partial(partial_kernel, period),
        (kept, swap(sent, "patch", 1), *out_pair),
        own_shapes + far_shapes,
    )
    late_pair = with_sister(temporal_out, parts[0])
    odd = swap_updates(parts[2:], (1,))
    turns = [(at, at ^ 1) for at in range(1, count, 2)]
    turn = lax.ppermute(after(modulation, *odd[0]), "patch", turns)
    even = swap_updates([after(part, turn) for part in parts[2:]], (0,))
    updates = [parts[0], *odd[0], *even[0], swap(parts[1], "frame", 1), *odd[1], *even[1]]
    middle, middle_sent, *parts = call(
        functools.partial(middle_kernel, pieces, 2 * groups - 1),
        (modulation, tokens, paired, *out_pair, *updates),
        [shape((pieces, period, width), BF16)] * 2 + piece_shapes,
        [pltpu.VMEM((pieces, 2 * period, width), BF16)],
    )
    arrived = exchange_frames(parts)
    (segment,) = call(join_kernel, arrived, [shape((rows, width), BF16)])
    segments = across(segment)

    def attend_frames(own, segments, shapes):
        columns = len(segments) * rows
        return call(
            functools.partial(temporal_kernel, own, period, rows),
            (*temporal_pair, *late_pair, *segments),
            shapes,
            [pltpu.VMEM((6 * shard, columns), F32), pltpu.VMEM((2 * shard, columns), F32)],
        )

    kept, sent = attend_frames(True, [segment], own_shapes)
    received = swap(sent, "frame", 1)
    middle_other = swap(after(middle_sent, segment), "frame", 1)
    others = [after(block, received) for block in segments[1:]]
    far_parts = attend_frames(False, others, far_shapes)
    same, diagonal = swap_updates(far_parts)
    updates = [kept, *same, received, *diagonal]
    parts = call(
        functools.partial(sum_kernel, groups),
        (*late_pair, *updates),
        piece_shapes,
    )
    (result,) = call(
        functools.partial(result_kernel, pieces),
        (modulation, middle, middle_other, *exchange_frames(parts)),
        [shape((frames, period, width), BF16)],
    )
    return result.reshape(1, rows, width)


def solution(mesh):
    in_specs = (
        P("frame", "patch", None),
        P(),
        P("patch", None),
        P("patch", None),
        P("patch", None),
        P("patch", None),
    )
    out_specs = P("frame", "patch", None)
    return jax.shard_map(
        per_device, mesh=mesh, in_specs=in_specs, out_specs=out_specs, check_vma=False
    )
```

```python
import functools

import jax
import jax.numpy as jnp
from jax import lax
from jax.experimental import pallas as pl
from jax.experimental.pallas import tpu as pltpu
from jax.sharding import PartitionSpec as P

HD = 72
MIB = 1 << 20
LOG2E = 1.4426950408889634
F32 = jnp.float32
BF16 = jnp.bfloat16


def norm_rows(values, shift, scale):
    average = jnp.mean(values, axis=-1, keepdims=True)
    centred = values - average
    variance = jnp.mean(centred * centred, axis=-1, keepdims=True)
    normed = centred * lax.rsqrt(variance + 1e-06)
    return (normed * (1.0 + scale) + shift).astype(BF16)


def dot(left, right, left_dim=1, right_dim=0):
    return lax.dot_general(
        left, right, (((left_dim,), (right_dim,)), ((), ())), preferred_element_type=F32
    )


def soften(scores):
    top = jnp.max(scores, axis=0, keepdims=True)
    return jnp.exp2((scores - top) * (HD**-0.5 * LOG2E)).astype(BF16)


def mix(values, weights):
    ones = jnp.ones((8, values.shape[1]), F32)
    mixed = dot(jnp.concatenate([values, ones], axis=0).astype(BF16), weights)
    return mixed[:HD] * (1.0 / mixed[HD : HD + 1])


def project(mod_ref, weight_ref, token_refs, proj_ref):
    shift, scale = mod_ref[0:1, :], mod_ref[1:2, :]
    block = token_refs[0].shape[1]
    for at in range(0, len(token_refs), 2):
        rows = [norm_rows(ref[0].astype(F32), shift, scale) for ref in token_refs[at : at + 2]]
        rows = jnp.concatenate(rows, axis=0)
        proj_ref[:, at * block : (at + 2) * block] = dot(weight_ref[...], rows, 1, 1)


def near_kernel(mod_ref, weight_ref, own_ref, sister_ref, proj_ref):
    project(mod_ref, weight_ref, (own_ref, sister_ref), proj_ref)


def spatial_kernel(count, mod_ref, weight_ref, near_ref, *refs):
    token_refs, (kept_ref, sent_ref, far_ref, heads_ref) = refs[: count - 2], refs[count - 2 :]
    block = token_refs[0].shape[1]
    heads = weight_ref.shape[0] // (3 * HD)
    project(mod_ref, weight_ref, token_refs, far_ref)

    def whole(start):
        return jnp.concatenate([ref[start : start + HD, :] for ref in (near_ref, far_ref)], axis=1)

    def score(head, at):
        base = head * 3 * HD
        source, start = (near_ref, 0) if at == 0 else (far_ref, (at - 2) * block)
        query = source[base : base + HD, start : start + 2 * block].astype(BF16)
        return dot(whole(base + HD).astype(BF16).T, query)

    steps = [(head, at) for head in range(heads) for at in range(0, count, 2)]
    scores = score(*steps[0])
    for (head, at), later in zip(steps, [*steps[1:], None]):
        coming = score(*later) if later else None
        rows, cols = slice(head * HD, (head + 1) * HD), slice(at * block, (at + 2) * block)
        heads_ref[rows, cols] = mix(whole(head * 3 * HD + 2 * HD), soften(scores))
        scores = coming
    for at in range(count):
        out_ref = (kept_ref, sent_ref)[at % 2]
        cols = slice(at // 2 * block, (at // 2 + 1) * block)
        out_ref[:, cols] = heads_ref[:, at * block : (at + 1) * block].astype(BF16)


def halves(value, size):
    return [
        jnp.concatenate(
            [value[at : at + size] for at in range(first * size, value.shape[0], 2 * size)], axis=0
        )
        for first in range(2)
    ]


def of_this_half(value, size):
    even, odd = (half.astype(F32) for half in halves(value, size))
    first = lax.axis_index("frame") % 2 == 0
    return jnp.where(first, even, odd), jnp.where(first, odd, even)


def share_kernel(period, token_ref, weight_ref, sent_ref, half_ref):
    sent_ref[...] = of_this_half(token_ref[0], period)[1].astype(BF16)
    half_ref[...] = of_this_half(weight_ref[...], half_ref.shape[0])[0].astype(BF16)


def joined(refs):
    return jnp.concatenate([ref[...] for ref in refs], axis=0)


def partial_kernel(period, *refs):
    head_refs, weights, out_refs = refs[:2], joined(refs[2:4]), refs[4:]
    block = 2 * out_refs[0].shape[0]
    for at in range(len(out_refs) // 2):
        cols = slice(at * block, (at + 1) * block)
        heads = jnp.concatenate([ref[:, cols] for ref in head_refs], axis=0).T
        if at == 0:
            kept, sent = (half.astype(BF16) for half in of_this_half(heads, period))
            parts = dot(kept, weights), sent
        else:
            parts = of_this_half(dot(heads, weights), period)
        for ref, part in zip(out_refs[2 * at : 2 * at + 2], parts):
            ref[...] = part.astype(ref.dtype)


def total_updates(groups, weight_refs, refs):
    kept = sum(ref[...].astype(F32) for ref in refs[:groups])
    paired = dot(refs[groups][...], joined(weight_refs))
    return kept, paired + sum(ref[...].astype(F32) for ref in refs[groups + 1 : 2 * groups])


def middle_kernel(pieces, groups, mod_ref, own_ref, paired_ref, *refs):
    kept_ref, sent_ref, *piece_refs, scratch = refs[2 + 2 * groups :]
    updates = total_updates(groups, refs[:2], refs[2:])
    _, period, width = kept_ref.shape
    inputs = (of_this_half(own_ref[0], period)[0], paired_ref[...])
    for at, (tokens, middle_ref) in enumerate(zip(inputs, (kept_ref, sent_ref))):
        update = updates[at]
        middle = (tokens.astype(F32) + mod_ref[2:3, :] * update).astype(BF16)
        normed = norm_rows(middle.astype(F32), mod_ref[3:4, :], mod_ref[4:5, :])
        for piece in range(pieces):
            rows = slice(piece * period, (piece + 1) * period)
            middle_ref[piece] = middle[rows]
            scratch[piece, at * period : (at + 1) * period, :] = normed[rows]
    here = lax.axis_index("frame") // 2
    for at, ref in enumerate(piece_refs):
        ref[...] = scratch[here ^ (pieces - 1 - at)]


def join_kernel(*refs):
    size = refs[0].shape[0]
    for at, ref in enumerate(refs[:-1]):
        refs[-1][at * size : (at + 1) * size, :] = ref[...]


def temporal_kernel(period, block, *refs):
    weight_refs, (proj_ref, heads_ref) = refs[:2], refs[-2:]
    groups = proj_ref.shape[1] // block
    row_refs, out_refs = refs[2 : -2 - 2 * groups], refs[-2 - 2 * groups : -2]
    rows = jnp.concatenate([ref[...] for ref in row_refs], axis=0)
    depth = weight_refs[0].shape[0]
    for core in range(2):
        proj_ref[core * depth : (core + 1) * depth, :] = dot(weight_refs[core][...], rows, 1, 1)
    heads = 2 * depth // (3 * HD)
    key_patch = lax.broadcasted_iota(jnp.int32, (block, block), 0) % period
    query_patch = lax.broadcasted_iota(jnp.int32, (block, block), 1) % period
    mask = key_patch == query_patch
    for group in range(groups):
        cols = slice(group * block, (group + 1) * block)

        def part(head, at):
            start = (head * 3 + at) * HD
            return proj_ref[start : start + HD, cols]

        scores = []
        for head in range(heads):
            keys, query = part(head, 1).astype(BF16).T, part(head, 0).astype(BF16)
            scores.append(jnp.where(mask, dot(keys, query), -1e30))
        soft = soften(jnp.concatenate(scores, axis=1))
        for head in range(heads):
            mixed = mix(part(head, 2), soft[:, head * block : (head + 1) * block])
            heads_ref[head * HD : (head + 1) * HD, cols] = mixed
        parts = halves(heads_ref[:, cols].astype(BF16).T, period)
        for ref, half in zip(out_refs[2 * group : 2 * group + 2], parts):
            ref[...] = half


def update_kernel(groups, *refs):
    head_refs, refs = (refs[:groups], refs[groups : 2 * groups]), refs[2 * groups :]
    weight_refs, piece_refs = refs[: 4 * groups - 2], refs[4 * groups - 2 :]
    period = piece_refs[0].shape[0] // 2
    size = head_refs[0][0].shape[0]
    first = lax.axis_index("frame") % 2 == 0
    update = 0.0
    for group in range(groups):
        heads = joined([refs[group] for refs in head_refs])
        if group == 0:
            weights = joined(weight_refs[:2])
        else:
            at = 4 * group - 2
            parts = []
            for here, there in (weight_refs[at : at + 2], weight_refs[at + 2 : at + 4]):
                here, there = here[...].astype(F32), there[...].astype(F32)
                parts += [jnp.where(first, here, there), jnp.where(first, there, here)]
            weights = jnp.concatenate(parts, axis=0).astype(BF16)
        update += dot(heads, weights)
    for at in range(2):
        part = update[at * size : (at + 1) * size].astype(BF16)
        for piece, ref in enumerate(piece_refs):
            rows = part[piece * period : (piece + 1) * period]
            ref[at * period : (at + 1) * period, :] = rows


def result_kernel(pieces, mod_ref, kept_ref, other_ref, *refs):
    piece_refs, out_ref = refs[:-1], refs[-1]
    period = kept_ref.shape[1]
    here = lax.axis_index("frame")
    for at, ref in enumerate(piece_refs):
        there = here // 2 ^ (pieces - 1 - at)
        for half, middle_ref in enumerate((kept_ref, other_ref)):
            update = ref[half * period : (half + 1) * period, :].astype(F32)
            middle = middle_ref[there].astype(F32)
            out_ref[2 * there + (here % 2 ^ half)] = (middle + mod_ref[5:6, :] * update).astype(
                BF16
            )


def call(body, operands, outs, scratch=(), limit=24):
    return pl.pallas_call(
        body,
        out_shape=outs,
        in_specs=[pl.BlockSpec(memory_space=pltpu.VMEM)] * len(operands),
        out_specs=[pl.BlockSpec(memory_space=pltpu.VMEM)] * len(outs),
        scratch_shapes=list(scratch),
        compiler_params=pltpu.CompilerParams(vmem_limit_bytes=limit * MIB),
        cost_estimate=pl.CostEstimate(flops=1, bytes_accessed=1, transcendentals=0),
    )(*operands)


def swap(value, axis, offset):
    size = lax.axis_size(axis)
    return lax.ppermute(value, axis, [(at, at ^ offset) for at in range(size)])


def after(value, *others):
    return lax.optimization_barrier((value, *others))[0]


def across(value):
    size = lax.axis_size("patch")
    return [swap(value, "patch", at) if at else value for at in range(0, size, 2)]


def both_cores(blocks):
    return [part for block in blocks for part in (block, swap(block, "patch", 1))]


def swap_diagonal(value, offset):
    frames, size = lax.axis_size("frame"), lax.axis_size("patch")
    pairs = [
        (frame * size + at, (frame ^ 1) * size + (at ^ offset))
        for frame in range(frames)
        for at in range(size)
    ]
    return lax.ppermute(value, ("frame", "patch"), pairs)


def per_device(tokens, modulation, spatial_qkv, spatial_out, temporal_qkv, temporal_out):
    _, rows, width = tokens.shape
    shard = spatial_out.shape[0]
    count, frames = lax.axis_size("patch"), lax.axis_size("frame")
    period = rows // frames
    pieces, groups = frames // 2, count // 2
    shape = jax.ShapeDtypeStruct

    def with_sister(weights, *others):
        return [weights, swap(after(weights, *others), "patch", 1)]

    def exchange_frames(parts):
        offsets = reversed(range(pieces))
        return [swap(part, "frame", 2 * at) if at else part for at, part in zip(offsets, parts)]

    def swap_updates(far):
        same = [swap(part, "patch", 2 * at) for at, part in enumerate(far[::2], 1)]
        return same, [swap_diagonal(part, 2 * at) for at, part in enumerate(far[1::2], 1)]

    def halves_shape(dtype):
        return shape((rows // 2, width), dtype)

    own_shapes = [halves_shape(F32), shape((rows // 2, 2 * shard), BF16)]
    far_shapes = [halves_shape(BF16)] * (2 * groups - 2)
    piece_shapes = [shape((2 * period, width), BF16)] * pieces

    sister = swap(tokens, "patch", 1)
    far = across(tokens)[1:]
    (near,) = call(
        near_kernel,
        (modulation, spatial_qkv, tokens, sister),
        [shape((3 * shard, 2 * rows), F32)],
    )
    shared, half_out = call(
        functools.partial(share_kernel, period),
        (after(tokens, sister), temporal_out),
        [halves_shape(BF16), shape((shard // 2, width), BF16)],
    )
    paired = swap(shared, "frame", 1)
    out_pair = with_sister(spatial_out, near)
    far = both_cores([after(block, near, paired) for block in far])
    temporal_pair = with_sister(temporal_qkv, *far)

    kept, sent = call(
        functools.partial(spatial_kernel, count),
        (modulation, spatial_qkv, near, *far),
        [shape((shard, groups * rows), BF16)] * 2,
        [pltpu.VMEM((3 * shard, (count - 2) * rows), F32), pltpu.VMEM((shard, count * rows), F32)],
    )
    parts = call(
        functools.partial(partial_kernel, period),
        (kept, swap(sent, "patch", 1), *out_pair),
        own_shapes + far_shapes,
    )
    late_pair = with_sister(temporal_out, parts[0])
    same, diagonal = swap_updates(parts[2:])
    updates = [parts[0], *same, swap(parts[1], "frame", 1), *diagonal]
    middle, middle_sent, *parts = call(
        functools.partial(middle_kernel, pieces, groups),
        (modulation, tokens, paired, *out_pair, *updates),
        [shape((pieces, period, width), BF16)] * 2 + piece_shapes,
        [pltpu.VMEM((pieces, 2 * period, width), BF16)],
    )
    halves_here = [swap(after(half_out, middle), "patch", 2 * at) for at in range(1, groups)]
    arrived = exchange_frames(parts)
    arrived[0] = after(arrived[0], *halves_here)
    (segment,) = call(join_kernel, arrived, [shape((rows, width), BF16)])
    segments = across(segment)
    halves_there = [swap(after(part, segment), "frame", 1) for part in halves_here]

    heads_shape = [shape((rows // 2, 2 * shard), BF16)] * 2

    def attend_frames(segments):
        columns = len(segments) * rows
        return call(
            functools.partial(temporal_kernel, period, rows),
            (*temporal_pair, *segments),
            heads_shape * len(segments),
            [pltpu.VMEM((6 * shard, columns), F32), pltpu.VMEM((2 * shard, columns), F32)],
        )

    kept, sent = attend_frames([segment])
    others = [after(block, kept) for block in segments[1:]]
    far_heads = attend_frames(others)
    same, diagonal = swap_updates(far_heads)
    late_far = []
    for pair in zip(halves_here, halves_there):
        late_far += [*pair, *(swap(after(part, *far_heads), "patch", 1) for part in pair)]
    middle_other = swap(after(middle_sent, segment), "frame", 1)
    parts = call(
        functools.partial(update_kernel, groups),
        (kept, *same, swap(sent, "frame", 1), *diagonal, *late_pair, *late_far),
        piece_shapes,
    )
    (result,) = call(
        functools.partial(result_kernel, pieces),
        (modulation, middle, middle_other, *exchange_frames(parts)),
        [shape((frames, period, width), BF16)],
    )
    return result.reshape(1, rows, width)


def solution(mesh):
    in_specs = (
        P("frame", "patch", None),
        P(),
        P("patch", None),
        P("patch", None),
        P("patch", None),
        P("patch", None),
    )
    out_specs = P("frame", "patch", None)
    return jax.shard_map(
        per_device, mesh=mesh, in_specs=in_specs, out_specs=out_specs, check_vma=False
    )
```

```python
import functools

import jax
import jax.numpy as jnp
from jax import lax
from jax.experimental import pallas as pl
from jax.experimental.pallas import tpu as pltpu
from jax.sharding import PartitionSpec as P

HD = 72
MIB = 1 << 20
LOG2E = 1.4426950408889634
F32 = jnp.float32
BF16 = jnp.bfloat16


def norm_rows(values, shift, scale):
    average = jnp.mean(values, axis=-1, keepdims=True)
    centred = values - average
    variance = jnp.mean(centred * centred, axis=-1, keepdims=True)
    normed = centred * lax.rsqrt(variance + 1e-06)
    return (normed * (1.0 + scale) + shift).astype(BF16)


def dot(left, right, left_dim=1, right_dim=0):
    return lax.dot_general(
        left, right, (((left_dim,), (right_dim,)), ((), ())), preferred_element_type=F32
    )


def soften(scores):
    top = jnp.max(scores, axis=0, keepdims=True)
    return jnp.exp2((scores - top) * (HD**-0.5 * LOG2E)).astype(BF16)


def mix(values, weights):
    ones = jnp.ones((8, values.shape[1]), F32)
    mixed = dot(jnp.concatenate([values, ones], axis=0).astype(BF16), weights)
    return mixed[:HD] * (1.0 / mixed[HD : HD + 1])


def project(mod_ref, weight_ref, token_refs, proj_ref):
    shift, scale = mod_ref[0:1, :], mod_ref[1:2, :]
    block = token_refs[0].shape[1]
    for at in range(0, len(token_refs), 2):
        rows = [norm_rows(ref[0].astype(F32), shift, scale) for ref in token_refs[at : at + 2]]
        rows = jnp.concatenate(rows, axis=0)
        proj_ref[:, at * block : (at + 2) * block] = dot(weight_ref[...], rows, 1, 1)


def near_kernel(mod_ref, weight_ref, own_ref, sister_ref, proj_ref):
    project(mod_ref, weight_ref, (own_ref, sister_ref), proj_ref)


def spatial_kernel(count, mod_ref, weight_ref, near_ref, *refs):
    token_refs, (kept_ref, sent_ref, far_ref, heads_ref) = refs[: count - 2], refs[count - 2 :]
    block = token_refs[0].shape[1]
    heads = weight_ref.shape[0] // (3 * HD)
    project(mod_ref, weight_ref, token_refs, far_ref)

    def whole(start):
        return jnp.concatenate([ref[start : start + HD, :] for ref in (near_ref, far_ref)], axis=1)

    def score(head, at):
        base = head * 3 * HD
        source, start = (near_ref, 0) if at == 0 else (far_ref, (at - 2) * block)
        query = source[base : base + HD, start : start + 2 * block].astype(BF16)
        return dot(whole(base + HD).astype(BF16).T, query)

    steps = [(head, at) for head in range(heads) for at in range(0, count, 2)]
    scores = score(*steps[0])
    for (head, at), later in zip(steps, [*steps[1:], None]):
        coming = score(*later) if later else None
        rows, cols = slice(head * HD, (head + 1) * HD), slice(at * block, (at + 2) * block)
        heads_ref[rows, cols] = mix(whole(head * 3 * HD + 2 * HD), soften(scores))
        scores = coming
    for at in range(count):
        out_ref = (kept_ref, sent_ref)[at % 2]
        cols = slice(at // 2 * block, (at // 2 + 1) * block)
        out_ref[:, cols] = heads_ref[:, at * block : (at + 1) * block].astype(BF16)


def halves(value, size):
    return [
        jnp.concatenate(
            [value[at : at + size] for at in range(first * size, value.shape[0], 2 * size)], axis=0
        )
        for first in range(2)
    ]


def of_this_half(value, size):
    even, odd = (half.astype(F32) for half in halves(value, size))
    first = lax.axis_index("frame") % 2 == 0
    return jnp.where(first, even, odd), jnp.where(first, odd, even)


def share_kernel(period, token_ref, sent_ref):
    sent_ref[...] = of_this_half(token_ref[0], period)[1].astype(BF16)


def joined(refs):
    return jnp.concatenate([ref[...] for ref in refs], axis=0)


def partial_kernel(period, *refs):
    head_refs, weights, out_refs = refs[:2], joined(refs[2:4]), refs[4:]
    block = 2 * out_refs[0].shape[0]
    for at in range(len(out_refs) // 2):
        cols = slice(at * block, (at + 1) * block)
        heads = jnp.concatenate([ref[:, cols] for ref in head_refs], axis=0).T
        if at == 0:
            kept, sent = (half.astype(BF16) for half in of_this_half(heads, period))
            parts = dot(kept, weights), sent
        else:
            parts = of_this_half(dot(heads, weights), period)
        for ref, part in zip(out_refs[2 * at : 2 * at + 2], parts):
            ref[...] = part.astype(ref.dtype)


def total_updates(groups, weight_refs, refs):
    kept = sum(ref[...].astype(F32) for ref in refs[:groups])
    paired = dot(refs[groups][...], joined(weight_refs))
    return kept, paired + sum(ref[...].astype(F32) for ref in refs[groups + 1 : 2 * groups])


def middle_kernel(pieces, groups, mod_ref, own_ref, paired_ref, *refs):
    kept_ref, sent_ref, *piece_refs, scratch = refs[2 + 2 * groups :]
    updates = total_updates(groups, refs[:2], refs[2:])
    _, period, width = kept_ref.shape
    inputs = (of_this_half(own_ref[0], period)[0], paired_ref[...])
    for at, (tokens, middle_ref) in enumerate(zip(inputs, (kept_ref, sent_ref))):
        update = updates[at]
        middle = (tokens.astype(F32) + mod_ref[2:3, :] * update).astype(BF16)
        normed = norm_rows(middle.astype(F32), mod_ref[3:4, :], mod_ref[4:5, :])
        for piece in range(pieces):
            rows = slice(piece * period, (piece + 1) * period)
            middle_ref[piece] = middle[rows]
            scratch[piece, at * period : (at + 1) * period, :] = normed[rows]
    here = lax.axis_index("frame") // 2
    for at, ref in enumerate(piece_refs, 1):
        ref[...] = scratch[here ^ at % pieces]


def join_kernel(*refs):
    size = refs[0].shape[0]
    for at, ref in enumerate(refs[:-1]):
        refs[-1][at * size : (at + 1) * size, :] = ref[...]


def temporal_kernel(own, period, block, *refs):
    weight_refs, output_refs, (proj_ref, heads_ref) = refs[:2], refs[2:4], refs[-2:]
    groups = proj_ref.shape[1] // block
    row_refs, update_refs = refs[4 : -2 - 2 * groups], refs[-2 - 2 * groups : -2]
    rows = jnp.concatenate([ref[...] for ref in row_refs], axis=0)
    depth = weight_refs[0].shape[0]
    for core in range(2):
        proj_ref[core * depth : (core + 1) * depth, :] = dot(weight_refs[core][...], rows, 1, 1)
    heads = 2 * depth // (3 * HD)
    key_patch = lax.broadcasted_iota(jnp.int32, (block, block), 0) % period
    query_patch = lax.broadcasted_iota(jnp.int32, (block, block), 1) % period
    mask = key_patch == query_patch
    weights = joined(output_refs)
    for group in range(groups):
        cols = slice(group * block, (group + 1) * block)

        def part(head, at):
            start = (head * 3 + at) * HD
            return proj_ref[start : start + HD, cols]

        scores = []
        for head in range(heads):
            keys, query = part(head, 1).astype(BF16).T, part(head, 0).astype(BF16)
            scores.append(jnp.where(mask, dot(keys, query), -1e30))
        soft = soften(jnp.concatenate(scores, axis=1))
        for head in range(heads):
            mixed = mix(part(head, 2), soft[:, head * block : (head + 1) * block])
            heads_ref[head * HD : (head + 1) * HD, cols] = mixed
        mixed = heads_ref[:, cols].astype(BF16).T
        if own:
            kept, sent = halves(mixed, period)
            parts = dot(kept, weights), sent
        else:
            parts = halves(dot(mixed, weights), period)
        for ref, half in zip(update_refs[2 * group : 2 * group + 2], parts):
            ref[...] = half.astype(ref.dtype)


def sum_kernel(groups, *refs):
    piece_refs = refs[2 + 2 * groups :]
    period = piece_refs[0].shape[0] // 2
    for at, update in enumerate(total_updates(groups, refs[:2], refs[2:])):
        update = update.astype(BF16)
        for piece, ref in enumerate(piece_refs):
            rows = update[piece * period : (piece + 1) * period]
            ref[at * period : (at + 1) * period, :] = rows


def result_kernel(pieces, mod_ref, kept_ref, other_ref, *refs):
    piece_refs, out_ref = refs[:-1], refs[-1]
    period = kept_ref.shape[1]
    here = lax.axis_index("frame")
    for at, ref in enumerate(piece_refs, 1):
        there = here // 2 ^ at % len(piece_refs)
        for half, middle_ref in enumerate((kept_ref, other_ref)):
            update = ref[half * period : (half + 1) * period, :].astype(F32)
            middle = middle_ref[there].astype(F32)
            out_ref[2 * there + (here % 2 ^ half)] = (middle + mod_ref[5:6, :] * update).astype(
                BF16
            )


def call(body, operands, outs, scratch=(), limit=24):
    return pl.pallas_call(
        body,
        out_shape=outs,
        in_specs=[pl.BlockSpec(memory_space=pltpu.VMEM)] * len(operands),
        out_specs=[pl.BlockSpec(memory_space=pltpu.VMEM)] * len(outs),
        scratch_shapes=list(scratch),
        compiler_params=pltpu.CompilerParams(vmem_limit_bytes=limit * MIB),
        cost_estimate=pl.CostEstimate(flops=1, bytes_accessed=1, transcendentals=0),
    )(*operands)


def swap(value, axis, offset):
    size = lax.axis_size(axis)
    return lax.ppermute(value, axis, [(at, at ^ offset) for at in range(size)])


def after(value, *others):
    return lax.optimization_barrier((value, *others))[0]


def across(value):
    size = lax.axis_size("patch")
    return [swap(value, "patch", at) if at else value for at in range(0, size, 2)]


def both_cores(blocks):
    return [part for block in blocks for part in (block, swap(block, "patch", 1))]


def swap_diagonal(value, offset):
    frames, size = lax.axis_size("frame"), lax.axis_size("patch")
    pairs = [
        (frame * size + at, (frame ^ 1) * size + (at ^ offset))
        for frame in range(frames)
        for at in range(size)
    ]
    return lax.ppermute(value, ("frame", "patch"), pairs)


def per_device(tokens, modulation, spatial_qkv, spatial_out, temporal_qkv, temporal_out):
    _, rows, width = tokens.shape
    shard = spatial_out.shape[0]
    count, frames = lax.axis_size("patch"), lax.axis_size("frame")
    period = rows // frames
    pieces, groups = frames // 2, count // 2
    shape = jax.ShapeDtypeStruct

    def with_sister(weights, *others):
        return [weights, swap(after(weights, *others), "patch", 1)]

    def exchange_frames(parts):
        sent = [swap(part, "frame", 2 * at) for at, part in enumerate(parts[:-1], 1)]
        return [*sent, parts[-1]]

    def return_updates(own, far):
        same = [swap(part, "patch", 2 * at) for at, part in enumerate(far[::2], 1)]
        diagonal = [swap_diagonal(part, 2 * at) for at, part in enumerate(far[1::2], 1)]
        return [own[0], *same, own[1], *diagonal]

    def halves_shape(dtype):
        return shape((rows // 2, width), dtype)

    own_shapes = [halves_shape(F32), shape((rows // 2, 2 * shard), BF16)]
    far_shapes = [halves_shape(BF16)] * (2 * groups - 2)
    piece_shapes = [shape((2 * period, width), BF16)] * pieces

    sister = swap(tokens, "patch", 1)
    far = across(tokens)[1:]
    (near,) = call(
        near_kernel,
        (modulation, spatial_qkv, tokens, sister),
        [shape((3 * shard, 2 * rows), F32)],
    )
    (shared,) = call(
        functools.partial(share_kernel, period), (after(tokens, sister),), [halves_shape(BF16)]
    )
    paired = swap(shared, "frame", 1)
    out_pair = with_sister(spatial_out, near)
    far = both_cores([after(block, near, paired) for block in far])
    temporal_pair = with_sister(temporal_qkv, *far)

    kept, sent = call(
        functools.partial(spatial_kernel, count),
        (modulation, spatial_qkv, near, *far),
        [shape((shard, groups * rows), BF16)] * 2,
        [pltpu.VMEM((3 * shard, (count - 2) * rows), F32), pltpu.VMEM((shard, count * rows), F32)],
    )
    parts = call(
        functools.partial(partial_kernel, period),
        (kept, swap(sent, "patch", 1), *out_pair),
        own_shapes + far_shapes,
    )
    late_pair = with_sister(temporal_out, parts[0])
    updates = return_updates((parts[0], swap(parts[1], "frame", 1)), parts[2:])
    middle, middle_sent, *parts = call(
        functools.partial(middle_kernel, pieces, groups),
        (modulation, tokens, paired, *out_pair, *updates),
        [shape((pieces, period, width), BF16)] * 2 + piece_shapes,
        [pltpu.VMEM((pieces, 2 * period, width), BF16)],
    )
    arrived = exchange_frames(parts)
    (segment,) = call(join_kernel, arrived, [shape((rows, width), BF16)])
    segments = across(segment)

    def attend_frames(own, segments, shapes):
        columns = len(segments) * rows
        return call(
            functools.partial(temporal_kernel, own, period, rows),
            (*temporal_pair, *late_pair, *segments),
            shapes,
            [pltpu.VMEM((6 * shard, columns), F32), pltpu.VMEM((2 * shard, columns), F32)],
        )

    kept, sent = attend_frames(True, [segment], own_shapes)
    received = swap(sent, "frame", 1)
    middle_other = swap(after(middle_sent, segment), "frame", 1)
    others = [after(block, received) for block in segments[1:]]
    far_parts = attend_frames(False, others, far_shapes)
    updates = return_updates((kept, received), far_parts)
    parts = call(
        functools.partial(sum_kernel, groups),
        (*late_pair, *updates),
        piece_shapes,
    )
    (result,) = call(
        functools.partial(result_kernel, pieces),
        (modulation, middle, middle_other, *exchange_frames(parts)),
        [shape((frames, period, width), BF16)],
    )
    return result.reshape(1, rows, width)


def solution(mesh):
    in_specs = (
        P("frame", "patch", None),
        P(),
        P("patch", None),
        P("patch", None),
        P("patch", None),
        P("patch", None),
    )
    out_specs = P("frame", "patch", None)
    return jax.shard_map(
        per_device, mesh=mesh, in_specs=in_specs, out_specs=out_specs, check_vma=False
    )
```

```python
import functools

import jax
import jax.numpy as jnp
from jax import lax
from jax.experimental import pallas as pl
from jax.experimental.pallas import tpu as pltpu
from jax.sharding import PartitionSpec as P

HD = 72
MIB = 1 << 20
LOG2E = 1.4426950408889634
F32 = jnp.float32
BF16 = jnp.bfloat16


def norm_rows(values, shift, scale):
    average = jnp.mean(values, axis=-1, keepdims=True)
    centred = values - average
    variance = jnp.mean(centred * centred, axis=-1, keepdims=True)
    normed = centred * lax.rsqrt(variance + 1e-06)
    return (normed * (1.0 + scale) + shift).astype(BF16)


def dot(left, right, left_dim=1, right_dim=0):
    return lax.dot_general(
        left, right, (((left_dim,), (right_dim,)), ((), ())), preferred_element_type=F32
    )


def soften(scores):
    top = jnp.max(scores, axis=0, keepdims=True)
    return jnp.exp2((scores - top) * (HD**-0.5 * LOG2E)).astype(BF16)


def mix(values, weights):
    ones = jnp.ones((8, values.shape[1]), F32)
    mixed = dot(jnp.concatenate([values, ones], axis=0).astype(BF16), weights)
    return mixed[:HD] * (1.0 / mixed[HD : HD + 1])


def project(mod_ref, weight_ref, token_refs, proj_ref):
    shift, scale = mod_ref[0:1, :], mod_ref[1:2, :]
    block = token_refs[0].shape[1]
    for at in range(0, len(token_refs), 2):
        rows = [norm_rows(ref[0].astype(F32), shift, scale) for ref in token_refs[at : at + 2]]
        rows = jnp.concatenate(rows, axis=0)
        proj_ref[:, at * block : (at + 2) * block] = dot(weight_ref[...], rows, 1, 1)


def near_kernel(mod_ref, weight_ref, own_ref, sister_ref, proj_ref):
    project(mod_ref, weight_ref, (own_ref, sister_ref), proj_ref)


def spatial_kernel(count, mod_ref, weight_ref, near_ref, *refs):
    token_refs, (kept_ref, sent_ref, far_ref, heads_ref) = refs[: count - 2], refs[count - 2 :]
    block = token_refs[0].shape[1]
    heads = weight_ref.shape[0] // (3 * HD)
    project(mod_ref, weight_ref, token_refs, far_ref)

    def whole(start):
        return jnp.concatenate([ref[start : start + HD, :] for ref in (near_ref, far_ref)], axis=1)

    def score(head, at):
        base = head * 3 * HD
        source, start = (near_ref, 0) if at == 0 else (far_ref, (at - 2) * block)
        query = source[base : base + HD, start : start + 2 * block].astype(BF16)
        return dot(whole(base + HD).astype(BF16).T, query)

    steps = [(head, at) for head in range(heads) for at in range(0, count, 2)]
    scores = score(*steps[0])
    for (head, at), later in zip(steps, [*steps[1:], None]):
        coming = score(*later) if later else None
        rows, cols = slice(head * HD, (head + 1) * HD), slice(at * block, (at + 2) * block)
        heads_ref[rows, cols] = mix(whole(head * 3 * HD + 2 * HD), soften(scores))
        scores = coming
    for at in range(count):
        out_ref = (kept_ref, sent_ref)[at % 2]
        cols = slice(at // 2 * block, (at // 2 + 1) * block)
        out_ref[:, cols] = heads_ref[:, at * block : (at + 1) * block].astype(BF16)


def halves(value, size):
    return [
        jnp.concatenate(
            [value[at : at + size] for at in range(first * size, value.shape[0], 2 * size)], axis=0
        )
        for first in range(2)
    ]


def of_this_half(value, size):
    even, odd = (half.astype(F32) for half in halves(value, size))
    first = lax.axis_index("frame") % 2 == 0
    return jnp.where(first, even, odd), jnp.where(first, odd, even)


def share_kernel(period, token_ref, kept_ref, sent_ref):
    for ref, half in zip((kept_ref, sent_ref), of_this_half(token_ref[0], period)):
        ref[...] = half.astype(BF16)


def joined(refs):
    return jnp.concatenate([ref[...] for ref in refs], axis=0)


def partial_kernel(period, *refs):
    head_refs, weights, out_refs = refs[:2], joined(refs[2:4]), refs[4:]
    block = 2 * out_refs[0].shape[0]
    for at in range(len(out_refs) // 2):
        cols = slice(at * block, (at + 1) * block)
        heads = jnp.concatenate([ref[:, cols] for ref in head_refs], axis=0).T
        if at == 0:
            kept, sent = (half.astype(BF16) for half in of_this_half(heads, period))
            parts = dot(kept, weights), sent
        else:
            parts = of_this_half(dot(heads, weights), period)
        for ref, part in zip(out_refs[2 * at : 2 * at + 2], parts):
            ref[...] = part.astype(ref.dtype)


def paired_kernel(head_ref, *refs):
    refs[-1][...] = dot(head_ref[...], joined(refs[:-1]))


def total_updates(groups, refs):
    return [
        sum(ref[...].astype(F32) for ref in refs[at * groups : (at + 1) * groups])
        for at in range(2)
    ]


def middle_kernel(pieces, groups, mod_ref, own_ref, paired_ref, *refs):
    kept_ref, sent_ref, *piece_refs, scratch = refs[2 * groups :]
    updates = total_updates(groups, refs)
    _, period, width = kept_ref.shape
    inputs = (own_ref[...], paired_ref[...])
    for at, (tokens, middle_ref) in enumerate(zip(inputs, (kept_ref, sent_ref))):
        update = updates[at]
        middle = (tokens.astype(F32) + mod_ref[2:3, :] * update).astype(BF16)
        normed = norm_rows(middle.astype(F32), mod_ref[3:4, :], mod_ref[4:5, :])
        for piece in range(pieces):
            rows = slice(piece * period, (piece + 1) * period)
            middle_ref[piece] = middle[rows]
            scratch[piece, at * period : (at + 1) * period, :] = normed[rows]
    here = lax.axis_index("frame") // 2
    for at, ref in enumerate(piece_refs):
        ref[...] = scratch[here ^ (pieces - 1 - at)]


def join_kernel(*refs):
    size = refs[0].shape[0]
    for at, ref in enumerate(refs[:-1]):
        refs[-1][at * size : (at + 1) * size, :] = ref[...]


def temporal_kernel(own, period, block, *refs):
    weight_refs, output_refs, (proj_ref, heads_ref) = refs[:2], refs[2:4], refs[-2:]
    groups = proj_ref.shape[1] // block
    row_refs, update_refs = refs[4 : -2 - 2 * groups], refs[-2 - 2 * groups : -2]
    rows = jnp.concatenate([ref[...] for ref in row_refs], axis=0)
    depth = weight_refs[0].shape[0]
    for core in range(2):
        proj_ref[core * depth : (core + 1) * depth, :] = dot(weight_refs[core][...], rows, 1, 1)
    heads = 2 * depth // (3 * HD)
    key_patch = lax.broadcasted_iota(jnp.int32, (block, block), 0) % period
    query_patch = lax.broadcasted_iota(jnp.int32, (block, block), 1) % period
    mask = key_patch == query_patch
    weights = joined(output_refs)
    for group in range(groups):
        cols = slice(group * block, (group + 1) * block)

        def part(head, at):
            start = (head * 3 + at) * HD
            return proj_ref[start : start + HD, cols]

        scores = []
        for head in range(heads):
            keys, query = part(head, 1).astype(BF16).T, part(head, 0).astype(BF16)
            scores.append(jnp.where(mask, dot(keys, query), -1e30))
        soft = soften(jnp.concatenate(scores, axis=1))
        for head in range(heads):
            mixed = mix(part(head, 2), soft[:, head * block : (head + 1) * block])
            heads_ref[head * HD : (head + 1) * HD, cols] = mixed
        mixed = heads_ref[:, cols].astype(BF16).T
        if own:
            kept, sent = halves(mixed, period)
            parts = dot(kept, weights), sent
        else:
            parts = halves(dot(mixed, weights), period)
        for ref, half in zip(update_refs[2 * group : 2 * group + 2], parts):
            ref[...] = half.astype(ref.dtype)


def sum_kernel(groups, *refs):
    piece_refs = refs[2 * groups :]
    period = piece_refs[0].shape[0] // 2
    for at, update in enumerate(total_updates(groups, refs)):
        update = update.astype(BF16)
        for piece, ref in enumerate(piece_refs):
            rows = update[piece * period : (piece + 1) * period]
            ref[at * period : (at + 1) * period, :] = rows


def result_kernel(pieces, mod_ref, kept_ref, other_ref, *refs):
    piece_refs, out_ref = refs[:-1], refs[-1]
    period = kept_ref.shape[1]
    here = lax.axis_index("frame")
    for at, ref in enumerate(piece_refs):
        there = here // 2 ^ (pieces - 1 - at)
        for half, middle_ref in enumerate((kept_ref, other_ref)):
            update = ref[half * period : (half + 1) * period, :].astype(F32)
            middle = middle_ref[there].astype(F32)
            out_ref[2 * there + (here % 2 ^ half)] = (middle + mod_ref[5:6, :] * update).astype(
                BF16
            )


def call(body, operands, outs, scratch=(), limit=24):
    return pl.pallas_call(
        body,
        out_shape=outs,
        in_specs=[pl.BlockSpec(memory_space=pltpu.VMEM)] * len(operands),
        out_specs=[pl.BlockSpec(memory_space=pltpu.VMEM)] * len(outs),
        scratch_shapes=list(scratch),
        compiler_params=pltpu.CompilerParams(vmem_limit_bytes=limit * MIB),
        cost_estimate=pl.CostEstimate(flops=1, bytes_accessed=1, transcendentals=0),
    )(*operands)


def swap(value, axis, offset):
    size = lax.axis_size(axis)
    return lax.ppermute(value, axis, [(at, at ^ offset) for at in range(size)])


def after(value, *others):
    return lax.optimization_barrier((value, *others))[0]


def across(value):
    size = lax.axis_size("patch")
    return [swap(value, "patch", at) if at else value for at in range(0, size, 2)]


def both_cores(blocks):
    return [part for block in blocks for part in (block, swap(block, "patch", 1))]


def swap_diagonal(value, offset):
    frames, size = lax.axis_size("frame"), lax.axis_size("patch")
    pairs = [
        (frame * size + at, (frame ^ 1) * size + (at ^ offset))
        for frame in range(frames)
        for at in range(size)
    ]
    return lax.ppermute(value, ("frame", "patch"), pairs)


def per_device(tokens, modulation, spatial_qkv, spatial_out, temporal_qkv, temporal_out):
    _, rows, width = tokens.shape
    shard = spatial_out.shape[0]
    count, frames = lax.axis_size("patch"), lax.axis_size("frame")
    period = rows // frames
    pieces, groups = frames // 2, count // 2
    shape = jax.ShapeDtypeStruct

    def with_sister(weights, *others):
        return [weights, swap(after(weights, *others), "patch", 1)]

    def exchange_frames(parts):
        offsets = reversed(range(pieces))
        return [swap(part, "frame", 2 * at) if at else part for at, part in zip(offsets, parts)]

    def project_paired(sent, weights):
        heads = swap(sent, "frame", 1)
        return call(paired_kernel, (heads, *weights), [halves_shape(F32)])[0]

    def return_updates(own, far):
        same = [swap(part, "patch", 2 * at) for at, part in enumerate(far[::2], 1)]
        diagonal = [swap_diagonal(part, 2 * at) for at, part in enumerate(far[1::2], 1)]
        return [own[0], *same, own[1], *diagonal]

    def halves_shape(dtype):
        return shape((rows // 2, width), dtype)

    own_shapes = [halves_shape(F32), shape((rows // 2, 2 * shard), BF16)]
    far_shapes = [halves_shape(BF16)] * (2 * groups - 2)
    piece_shapes = [shape((2 * period, width), BF16)] * pieces

    sister = swap(tokens, "patch", 1)
    far = across(tokens)[1:]
    (near,) = call(
        near_kernel,
        (modulation, spatial_qkv, tokens, sister),
        [shape((3 * shard, 2 * rows), F32)],
    )
    own_tokens, shared = call(
        functools.partial(share_kernel, period), (after(tokens, sister),), [halves_shape(BF16)] * 2
    )
    paired = swap(shared, "frame", 1)
    out_pair = with_sister(spatial_out, near)
    far = both_cores([after(block, near, paired) for block in far])
    temporal_pair = with_sister(temporal_qkv, *far)

    kept, sent = call(
        functools.partial(spatial_kernel, count),
        (modulation, spatial_qkv, near, *far),
        [shape((shard, groups * rows), BF16)] * 2,
        [pltpu.VMEM((3 * shard, (count - 2) * rows), F32), pltpu.VMEM((shard, count * rows), F32)],
    )
    parts = call(
        functools.partial(partial_kernel, period),
        (kept, swap(sent, "patch", 1), *out_pair),
        own_shapes + far_shapes,
    )
    late_pair = with_sister(temporal_out, parts[0])
    updates = return_updates((parts[0], project_paired(parts[1], out_pair)), parts[2:])
    middle, middle_sent, *parts = call(
        functools.partial(middle_kernel, pieces, groups),
        (modulation, own_tokens, paired, *updates),
        [shape((pieces, period, width), BF16)] * 2 + piece_shapes,
        [pltpu.VMEM((pieces, 2 * period, width), BF16)],
    )
    arrived = exchange_frames(parts)
    (segment,) = call(join_kernel, arrived, [shape((rows, width), BF16)])
    segments = across(segment)

    def attend_frames(own, segments, shapes):
        columns = len(segments) * rows
        return call(
            functools.partial(temporal_kernel, own, period, rows),
            (*temporal_pair, *late_pair, *segments),
            shapes,
            [pltpu.VMEM((6 * shard, columns), F32), pltpu.VMEM((2 * shard, columns), F32)],
        )

    kept, sent = attend_frames(True, [segment], own_shapes)
    received = project_paired(sent, late_pair)
    middle_other = swap(after(middle_sent, segment), "frame", 1)
    others = [after(block, received) for block in segments[1:]]
    far_parts = attend_frames(False, others, far_shapes)
    updates = return_updates((kept, received), far_parts)
    parts = call(
        functools.partial(sum_kernel, groups),
        updates,
        piece_shapes,
    )
    (result,) = call(
        functools.partial(result_kernel, pieces),
        (modulation, middle, middle_other, *exchange_frames(parts)),
        [shape((frames, period, width), BF16)],
    )
    return result.reshape(1, rows, width)


def solution(mesh):
    in_specs = (
        P("frame", "patch", None),
        P(),
        P("patch", None),
        P("patch", None),
        P("patch", None),
        P("patch", None),
    )
    out_specs = P("frame", "patch", None)
    return jax.shard_map(
        per_device, mesh=mesh, in_specs=in_specs, out_specs=out_specs, check_vma=False
    )
```

```python
import functools

import jax
import jax.numpy as jnp
from jax import lax
from jax.experimental import pallas as pl
from jax.experimental.pallas import tpu as pltpu
from jax.sharding import PartitionSpec as P

HD = 72
MIB = 1 << 20
LOG2E = 1.4426950408889634
F32 = jnp.float32
BF16 = jnp.bfloat16


def norm_rows(values, shift, scale):
    average = jnp.mean(values, axis=-1, keepdims=True)
    centred = values - average
    variance = jnp.mean(centred * centred, axis=-1, keepdims=True)
    normed = centred * lax.rsqrt(variance + 1e-06)
    return (normed * (1.0 + scale) + shift).astype(BF16)


def dot(left, right, left_dim=1, right_dim=0):
    return lax.dot_general(
        left, right, (((left_dim,), (right_dim,)), ((), ())), preferred_element_type=F32
    )


def soften(scores):
    top = jnp.max(scores, axis=0, keepdims=True)
    return jnp.exp2((scores - top) * (HD**-0.5 * LOG2E)).astype(BF16)


def mix(values, weights):
    ones = jnp.ones((8, values.shape[1]), F32)
    mixed = dot(jnp.concatenate([values, ones], axis=0).astype(BF16), weights)
    return mixed[:HD] * (1.0 / mixed[HD : HD + 1])


def project(mod_ref, weight_ref, token_refs, proj_ref):
    shift, scale = mod_ref[0:1, :], mod_ref[1:2, :]
    block = token_refs[0].shape[1]
    for at in range(0, len(token_refs), 2):
        rows = [norm_rows(ref[0].astype(F32), shift, scale) for ref in token_refs[at : at + 2]]
        rows = jnp.concatenate(rows, axis=0)
        proj_ref[:, at * block : (at + 2) * block] = dot(weight_ref[...], rows, 1, 1)


def near_kernel(mod_ref, weight_ref, own_ref, sister_ref, proj_ref):
    project(mod_ref, weight_ref, (own_ref, sister_ref), proj_ref)


def attend_patches(near_ref, far_ref, query_ref, heads_ref, kept_ref, sent_ref):
    columns, block = query_ref.shape[1], near_ref.shape[1] // 2

    def whole(start):
        return jnp.concatenate([ref[start : start + HD, :] for ref in (near_ref, far_ref)], axis=1)

    def score(head, at):
        base = head * 3 * HD
        query = query_ref[base : base + HD, at : at + 2 * block].astype(BF16)
        return dot(whole(base + HD).astype(BF16).T, query)

    heads = range(heads_ref.shape[0] // HD)
    steps = [(head, at) for head in heads for at in range(0, columns, 2 * block)]
    scores = score(*steps[0])
    for (head, at), later in zip(steps, [*steps[1:], None]):
        coming = score(*later) if later else None
        rows, cols = slice(head * HD, (head + 1) * HD), slice(at, at + 2 * block)
        heads_ref[rows, cols] = mix(whole(head * 3 * HD + 2 * HD), soften(scores))
        scores = coming
    for at in range(columns // block):
        out_ref = (kept_ref, sent_ref)[at % 2]
        cols = slice(at // 2 * block, (at // 2 + 1) * block)
        out_ref[:, cols] = heads_ref[:, at * block : (at + 1) * block].astype(BF16)


def far_queries_kernel(mod_ref, weight_ref, near_ref, *refs):
    token_refs, (far_ref, kept_ref, sent_ref, heads_ref) = refs[:-4], refs[-4:]
    project(mod_ref, weight_ref, token_refs, far_ref)
    attend_patches(near_ref, far_ref, far_ref, heads_ref, kept_ref, sent_ref)


def near_queries_kernel(near_ref, far_ref, kept_ref, sent_ref, heads_ref):
    attend_patches(near_ref, far_ref, near_ref, heads_ref, kept_ref, sent_ref)


def halves(value, size):
    return [
        jnp.concatenate(
            [value[at : at + size] for at in range(first * size, value.shape[0], 2 * size)], axis=0
        )
        for first in range(2)
    ]


def of_this_half(value, size):
    even, odd = (half.astype(F32) for half in halves(value, size))
    first = lax.axis_index("frame") % 2 == 0
    return jnp.where(first, even, odd), jnp.where(first, odd, even)


def share_kernel(period, token_ref, kept_ref, sent_ref):
    for ref, half in zip((kept_ref, sent_ref), of_this_half(token_ref[0], period)):
        ref[...] = half.astype(BF16)


def joined(refs):
    return jnp.concatenate([ref[...] for ref in refs], axis=0)


def far_partial_kernel(period, *refs):
    head_refs, weights, out_refs = refs[:2], joined(refs[2:4]), refs[4:]
    block = 2 * out_refs[0].shape[0]
    for at in range(len(out_refs) // 2):
        cols = slice(at * block, (at + 1) * block)
        heads = jnp.concatenate([ref[:, cols] for ref in head_refs], axis=0).T
        parts = of_this_half(dot(heads, weights), period)
        for ref, part in zip(out_refs[2 * at : 2 * at + 2], parts):
            ref[...] = part.astype(ref.dtype)


def near_partial_kernel(period, *refs):
    head_refs, weights, (kept_ref, sent_ref) = refs[:2], joined(refs[2:4]), refs[4:]
    kept, sent = of_this_half(joined(head_refs).T, period)
    kept_ref[...] = dot(kept.astype(BF16), weights)
    sent_ref[...] = sent.astype(BF16)


def paired_kernel(head_ref, *refs):
    refs[-1][...] = dot(head_ref[...], joined(refs[:-1]))


def far_sum_kernel(count, *refs):
    for at, ref in enumerate(refs[2 * count :]):
        ref[...] = sum(part[...].astype(F32) for part in refs[at * count : (at + 1) * count])


def total_updates(groups, refs):
    return [
        sum(ref[...].astype(F32) for ref in refs[at * groups : (at + 1) * groups])
        for at in range(2)
    ]


def middle_kernel(pieces, mod_ref, own_ref, paired_ref, *refs):
    kept_ref, sent_ref, *piece_refs, scratch = refs[4:]
    updates = total_updates(2, refs)
    _, period, width = kept_ref.shape
    inputs = (own_ref[...], paired_ref[...])
    for at, (tokens, middle_ref) in enumerate(zip(inputs, (kept_ref, sent_ref))):
        update = updates[at]
        middle = (tokens.astype(F32) + mod_ref[2:3, :] * update).astype(BF16)
        normed = norm_rows(middle.astype(F32), mod_ref[3:4, :], mod_ref[4:5, :])
        for piece in range(pieces):
            rows = slice(piece * period, (piece + 1) * period)
            middle_ref[piece] = middle[rows]
            scratch[piece, at * period : (at + 1) * period, :] = normed[rows]
    here = lax.axis_index("frame") // 2
    for at, ref in enumerate(piece_refs):
        ref[...] = scratch[here ^ (pieces - 1 - at)]


def join_kernel(*refs):
    size = refs[0].shape[0]
    for at, ref in enumerate(refs[:-1]):
        refs[-1][at * size : (at + 1) * size, :] = ref[...]


def temporal_kernel(own, period, block, *refs):
    weight_refs, output_refs, (proj_ref, heads_ref) = refs[:2], refs[2:4], refs[-2:]
    groups = proj_ref.shape[1] // block
    row_refs, update_refs = refs[4 : -2 - 2 * groups], refs[-2 - 2 * groups : -2]
    rows = jnp.concatenate([ref[...] for ref in row_refs], axis=0)
    depth = weight_refs[0].shape[0]
    for core in range(2):
        proj_ref[core * depth : (core + 1) * depth, :] = dot(weight_refs[core][...], rows, 1, 1)
    heads = 2 * depth // (3 * HD)
    key_patch = lax.broadcasted_iota(jnp.int32, (block, block), 0) % period
    query_patch = lax.broadcasted_iota(jnp.int32, (block, block), 1) % period
    mask = key_patch == query_patch
    weights = joined(output_refs)
    for group in range(groups):
        cols = slice(group * block, (group + 1) * block)

        def part(head, at):
            start = (head * 3 + at) * HD
            return proj_ref[start : start + HD, cols]

        scores = []
        for head in range(heads):
            keys, query = part(head, 1).astype(BF16).T, part(head, 0).astype(BF16)
            scores.append(jnp.where(mask, dot(keys, query), -1e30))
        soft = soften(jnp.concatenate(scores, axis=1))
        for head in range(heads):
            mixed = mix(part(head, 2), soft[:, head * block : (head + 1) * block])
            heads_ref[head * HD : (head + 1) * HD, cols] = mixed
        mixed = heads_ref[:, cols].astype(BF16).T
        if own:
            kept, sent = halves(mixed, period)
            parts = dot(kept, weights), sent
        else:
            parts = halves(dot(mixed, weights), period)
        for ref, half in zip(update_refs[2 * group : 2 * group + 2], parts):
            ref[...] = half.astype(ref.dtype)


def sum_kernel(groups, *refs):
    piece_refs = refs[2 * groups :]
    period = piece_refs[0].shape[0] // 2
    for at, update in enumerate(total_updates(groups, refs)):
        update = update.astype(BF16)
        for piece, ref in enumerate(piece_refs):
            rows = update[piece * period : (piece + 1) * period]
            ref[at * period : (at + 1) * period, :] = rows


def result_kernel(pieces, mod_ref, kept_ref, other_ref, *refs):
    piece_refs, out_ref = refs[:-1], refs[-1]
    period = kept_ref.shape[1]
    here = lax.axis_index("frame")
    for at, ref in enumerate(piece_refs):
        there = here // 2 ^ (pieces - 1 - at)
        for half, middle_ref in enumerate((kept_ref, other_ref)):
            update = ref[half * period : (half + 1) * period, :].astype(F32)
            middle = middle_ref[there].astype(F32)
            out_ref[2 * there + (here % 2 ^ half)] = (middle + mod_ref[5:6, :] * update).astype(
                BF16
            )


def call(body, operands, outs, scratch=(), limit=24, flops=1):
    return pl.pallas_call(
        body,
        out_shape=outs,
        in_specs=[pl.BlockSpec(memory_space=pltpu.VMEM)] * len(operands),
        out_specs=[pl.BlockSpec(memory_space=pltpu.VMEM)] * len(outs),
        scratch_shapes=list(scratch),
        compiler_params=pltpu.CompilerParams(vmem_limit_bytes=limit * MIB),
        cost_estimate=pl.CostEstimate(flops=flops, bytes_accessed=1, transcendentals=0),
    )(*operands)


def swap(value, axis, offset):
    size = lax.axis_size(axis)
    return lax.ppermute(value, axis, [(at, at ^ offset) for at in range(size)])


def after(value, *others):
    return lax.optimization_barrier((value, *others))[0]


def across(value):
    size = lax.axis_size("patch")
    return [swap(value, "patch", at) if at else value for at in range(0, size, 2)]


def both_cores(blocks):
    return [part for block in blocks for part in (block, swap(block, "patch", 1))]


def swap_diagonal(value, offset):
    frames, size = lax.axis_size("frame"), lax.axis_size("patch")
    pairs = [
        (frame * size + at, (frame ^ 1) * size + (at ^ offset))
        for frame in range(frames)
        for at in range(size)
    ]
    return lax.ppermute(value, ("frame", "patch"), pairs)


def per_device(tokens, modulation, spatial_qkv, spatial_out, temporal_qkv, temporal_out):
    _, rows, width = tokens.shape
    shard = spatial_out.shape[0]
    count, frames = lax.axis_size("patch"), lax.axis_size("frame")
    period = rows // frames
    pieces, groups = frames // 2, count // 2
    shape = jax.ShapeDtypeStruct

    def with_sister(weights, *others):
        return [weights, swap(after(weights, *others), "patch", 1)]

    def exchange_frames(parts):
        offsets = reversed(range(pieces))
        return [swap(part, "frame", 2 * at) if at else part for at, part in zip(offsets, parts)]

    def project_paired(sent, weights):
        heads = swap(sent, "frame", 1)
        return call(paired_kernel, (heads, *weights), [halves_shape(F32)])[0]

    def return_updates(own, far):
        same = [swap(part, "patch", 2 * at) for at, part in enumerate(far[::2], 1)]
        diagonal = [swap_diagonal(part, 2 * at) for at, part in enumerate(far[1::2], 1)]
        return [own[0], *same, own[1], *diagonal]

    def halves_shape(dtype):
        return shape((rows // 2, width), dtype)

    own_shapes = [halves_shape(F32), shape((rows // 2, 2 * shard), BF16)]
    far_shapes = [halves_shape(BF16)] * (2 * groups - 2)
    piece_shapes = [shape((2 * period, width), BF16)] * pieces

    sister = swap(tokens, "patch", 1)
    far = across(tokens)[1:]
    (near,) = call(
        near_kernel,
        (modulation, spatial_qkv, tokens, sister),
        [shape((3 * shard, 2 * rows), F32)],
    )
    own_tokens, shared = call(
        functools.partial(share_kernel, period), (after(tokens, sister),), [halves_shape(BF16)] * 2
    )
    paired = swap(shared, "frame", 1)
    out_pair = with_sister(spatial_out, near)
    far = both_cores([after(block, near, paired) for block in far])
    temporal_pair = with_sister(temporal_qkv, *far)

    columns = (groups - 1) * rows
    far_proj, kept, sent = call(
        far_queries_kernel,
        (modulation, spatial_qkv, near, *far),
        [shape((3 * shard, 2 * columns), F32)] + [shape((shard, columns), BF16)] * 2,
        [pltpu.VMEM((shard, 2 * columns), F32)],
    )
    far_parts = call(
        functools.partial(far_partial_kernel, period),
        (kept, swap(sent, "patch", 1), *out_pair),
        far_shapes,
    )
    kept, sent = call(
        near_queries_kernel,
        (after(near, far_parts[0]), far_proj),
        [shape((shard, rows), BF16)] * 2,
        [pltpu.VMEM((shard, 2 * rows), F32)],
        flops=1,
    )
    received = swap(sent, "patch", 1)
    own_parts = call(
        functools.partial(near_partial_kernel, period), (kept, received, *out_pair), own_shapes
    )
    late_pair = with_sister(temporal_out, received)
    updates = return_updates((own_parts[0], project_paired(own_parts[1], out_pair)), far_parts)
    sums = call(
        functools.partial(far_sum_kernel, groups - 1),
        (*updates[1:groups], *updates[groups + 1 :]),
        [halves_shape(F32)] * 2,
        flops=4_000_000_000,
    )
    updates = [updates[0], sums[0], updates[groups], sums[1]]
    middle, middle_sent, *parts = call(
        functools.partial(middle_kernel, pieces),
        (modulation, own_tokens, paired, *updates),
        [shape((pieces, period, width), BF16)] * 2 + piece_shapes,
        [pltpu.VMEM((pieces, 2 * period, width), BF16)],
    )
    arrived = exchange_frames(parts)
    (segment,) = call(join_kernel, arrived, [shape((rows, width), BF16)])
    segments = across(segment)

    def attend_frames(own, segments, shapes):
        columns = len(segments) * rows
        return call(
            functools.partial(temporal_kernel, own, period, rows),
            (*temporal_pair, *late_pair, *segments),
            shapes,
            [pltpu.VMEM((6 * shard, columns), F32), pltpu.VMEM((2 * shard, columns), F32)],
        )

    kept, sent = attend_frames(True, [segment], own_shapes)
    received = project_paired(sent, late_pair)
    middle_other = swap(after(middle_sent, segment), "frame", 1)
    others = [after(block, received) for block in segments[1:]]
    far_parts = attend_frames(False, others, far_shapes)
    updates = return_updates((kept, received), far_parts)
    parts = call(
        functools.partial(sum_kernel, groups),
        updates,
        piece_shapes,
    )
    (result,) = call(
        functools.partial(result_kernel, pieces),
        (modulation, middle, middle_other, *exchange_frames(parts)),
        [shape((frames, period, width), BF16)],
    )
    return result.reshape(1, rows, width)


def solution(mesh):
    in_specs = (
        P("frame", "patch", None),
        P(),
        P("patch", None),
        P("patch", None),
        P("patch", None),
        P("patch", None),
    )
    out_specs = P("frame", "patch", None)
    return jax.shard_map(
        per_device, mesh=mesh, in_specs=in_specs, out_specs=out_specs, check_vma=False
    )
```

```python
import functools

import jax
import jax.numpy as jnp
from jax import lax
from jax.experimental import pallas as pl
from jax.experimental.pallas import tpu as pltpu
from jax.sharding import PartitionSpec as P

HD = 72
MIB = 1 << 20
LOG2E = 1.4426950408889634
F32 = jnp.float32
BF16 = jnp.bfloat16


def norm_rows(values, shift, scale):
    average = jnp.mean(values, axis=-1, keepdims=True)
    centred = values - average
    variance = jnp.mean(centred * centred, axis=-1, keepdims=True)
    normed = centred * lax.rsqrt(variance + 1e-06)
    return (normed * (1.0 + scale) + shift).astype(BF16)


def dot(left, right, left_dim=1, right_dim=0):
    return lax.dot_general(
        left, right, (((left_dim,), (right_dim,)), ((), ())), preferred_element_type=F32
    )


def soften(scores):
    top = jnp.max(scores, axis=0, keepdims=True)
    return jnp.exp2((scores - top) * (HD**-0.5 * LOG2E)).astype(BF16)


def mix(values, weights):
    ones = jnp.ones((8, values.shape[1]), F32)
    mixed = dot(jnp.concatenate([values, ones], axis=0).astype(BF16), weights)
    return mixed[:HD] * (1.0 / mixed[HD : HD + 1])


def project(mod_ref, weight_ref, token_refs, proj_ref):
    shift, scale = mod_ref[0:1, :], mod_ref[1:2, :]
    block = token_refs[0].shape[1]
    for at in range(0, len(token_refs), 2):
        rows = [norm_rows(ref[0].astype(F32), shift, scale) for ref in token_refs[at : at + 2]]
        rows = jnp.concatenate(rows, axis=0)
        proj_ref[:, at * block : (at + 2) * block] = dot(weight_ref[...], rows, 1, 1)


def near_kernel(mod_ref, weight_ref, own_ref, sister_ref, proj_ref):
    project(mod_ref, weight_ref, (own_ref, sister_ref), proj_ref)


def spatial_kernel(count, mod_ref, weight_ref, near_ref, *refs):
    token_refs, (kept_ref, sent_ref, far_ref, heads_ref) = refs[: count - 2], refs[count - 2 :]
    block = token_refs[0].shape[1]
    heads = weight_ref.shape[0] // (3 * HD)
    project(mod_ref, weight_ref, token_refs, far_ref)

    def whole(start):
        return jnp.concatenate([ref[start : start + HD, :] for ref in (near_ref, far_ref)], axis=1)

    def score(head, at):
        base = head * 3 * HD
        source, start = (near_ref, 0) if at == 0 else (far_ref, (at - 2) * block)
        query = source[base : base + HD, start : start + 2 * block].astype(BF16)
        return dot(whole(base + HD).astype(BF16).T, query)

    steps = [(head, at) for head in range(heads) for at in range(0, count, 2)]
    scores = score(*steps[0])
    for (head, at), later in zip(steps, [*steps[1:], None]):
        coming = score(*later) if later else None
        rows, cols = slice(head * HD, (head + 1) * HD), slice(at * block, (at + 2) * block)
        heads_ref[rows, cols] = mix(whole(head * 3 * HD + 2 * HD), soften(scores))
        scores = coming
    for at in range(count):
        out_ref = (kept_ref, sent_ref)[at % 2]
        cols = slice(at // 2 * block, (at // 2 + 1) * block)
        out_ref[:, cols] = heads_ref[:, at * block : (at + 1) * block].astype(BF16)


def halves(value, size):
    return [
        jnp.concatenate(
            [value[at : at + size] for at in range(first * size, value.shape[0], 2 * size)], axis=0
        )
        for first in range(2)
    ]


def of_this_half(value, size):
    even, odd = (half.astype(F32) for half in halves(value, size))
    first = lax.axis_index("frame") % 2 == 0
    return jnp.where(first, even, odd), jnp.where(first, odd, even)


def share_kernel(period, token_ref, kept_ref, sent_ref):
    for ref, half in zip((kept_ref, sent_ref), of_this_half(token_ref[0], period)):
        ref[...] = half.astype(BF16)


def joined(refs):
    return jnp.concatenate([ref[...] for ref in refs], axis=0)


def partial_kernel(period, *refs):
    head_refs, weights, out_refs = refs[:2], joined(refs[2:4]), refs[4:]
    block = 2 * out_refs[0].shape[0]
    for at in range(len(out_refs) // 2):
        cols = slice(at * block, (at + 1) * block)
        heads = jnp.concatenate([ref[:, cols] for ref in head_refs], axis=0).T
        if at == 0:
            kept, sent = (half.astype(BF16) for half in of_this_half(heads, period))
            parts = dot(kept, weights), sent
        else:
            parts = of_this_half(dot(heads, weights), period)
        for ref, part in zip(out_refs[2 * at : 2 * at + 2], parts):
            ref[...] = part.astype(ref.dtype)


def paired_kernel(head_ref, *refs):
    refs[-1][...] = dot(head_ref[...], joined(refs[:-1]))


def total_updates(groups, refs):
    return [
        sum(ref[...].astype(F32) for ref in refs[at * groups : (at + 1) * groups])
        for at in range(2)
    ]


def middle_kernel(pieces, groups, mod_ref, own_ref, paired_ref, *refs):
    kept_ref, sent_ref, *piece_refs, scratch = refs[2 * groups :]
    updates = total_updates(groups, refs)
    _, period, width = kept_ref.shape
    inputs = (own_ref[...], paired_ref[...])
    for at, (tokens, middle_ref) in enumerate(zip(inputs, (kept_ref, sent_ref))):
        update = updates[at]
        middle = (tokens.astype(F32) + mod_ref[2:3, :] * update).astype(BF16)
        normed = norm_rows(middle.astype(F32), mod_ref[3:4, :], mod_ref[4:5, :])
        for piece in range(pieces):
            rows = slice(piece * period, (piece + 1) * period)
            middle_ref[piece] = middle[rows]
            scratch[piece, at * period : (at + 1) * period, :] = normed[rows]
    here = lax.axis_index("frame") // 2
    for at, ref in enumerate(piece_refs):
        ref[...] = scratch[here ^ (pieces - 1 - at)]


def join_kernel(*refs):
    size = refs[0].shape[0]
    for at, ref in enumerate(refs[:-1]):
        refs[-1][at * size : (at + 1) * size, :] = ref[...]


def temporal_kernel(own, period, block, *refs):
    weight_refs, output_refs, (proj_ref, heads_ref) = refs[:2], refs[2:4], refs[-2:]
    groups = proj_ref.shape[1] // block
    row_refs, update_refs = refs[4 : -2 - 2 * groups], refs[-2 - 2 * groups : -2]
    rows = jnp.concatenate([ref[...] for ref in row_refs], axis=0)
    depth = weight_refs[0].shape[0]
    for core in range(2):
        proj_ref[core * depth : (core + 1) * depth, :] = dot(weight_refs[core][...], rows, 1, 1)
    heads = 2 * depth // (3 * HD)
    key_patch = lax.broadcasted_iota(jnp.int32, (block, block), 0) % period
    query_patch = lax.broadcasted_iota(jnp.int32, (block, block), 1) % period
    mask = key_patch == query_patch
    weights = joined(output_refs)
    for group in range(groups):
        cols = slice(group * block, (group + 1) * block)

        def part(head, at):
            start = (head * 3 + at) * HD
            return proj_ref[start : start + HD, cols]

        scores = []
        for head in range(heads):
            keys, query = part(head, 1).astype(BF16).T, part(head, 0).astype(BF16)
            scores.append(jnp.where(mask, dot(keys, query), -1e30))
        soft = soften(jnp.concatenate(scores, axis=1))
        for head in range(heads):
            mixed = mix(part(head, 2), soft[:, head * block : (head + 1) * block])
            heads_ref[head * HD : (head + 1) * HD, cols] = mixed
        mixed = heads_ref[:, cols].astype(BF16).T
        if own:
            kept, sent = halves(mixed, period)
            parts = dot(kept, weights), sent
        else:
            parts = halves(dot(mixed, weights), period)
        for ref, half in zip(update_refs[2 * group : 2 * group + 2], parts):
            ref[...] = half.astype(ref.dtype)


def sum_kernel(pieces, *refs):
    update = sum(ref[...].astype(F32) for ref in refs[:-pieces]).astype(BF16)
    period = update.shape[0] // pieces
    for at, ref in enumerate(refs[-pieces:]):
        ref[...] = update[at * period : (at + 1) * period]


def result_rows(mod_ref, middle_ref, piece_refs):
    here = lax.axis_index("frame") // 2
    for at, ref in enumerate(piece_refs):
        there = here ^ (len(piece_refs) - 1 - at)
        update = ref[...].astype(F32)
        yield there, (middle_ref[there].astype(F32) + mod_ref[5:6, :] * update).astype(BF16)


def first_result_kernel(mod_ref, middle_ref, *refs):
    for there, rows in result_rows(mod_ref, middle_ref, refs[:-1]):
        refs[-1][there] = rows


def result_kernel(mod_ref, middle_ref, done_ref, *refs):
    half = lax.axis_index("frame") % 2
    for there in range(done_ref.shape[0]):
        refs[-1][2 * there + half] = done_ref[there]
    for there, rows in result_rows(mod_ref, middle_ref, refs[:-1]):
        refs[-1][2 * there + (1 - half)] = rows


def call(body, operands, outs, scratch=(), limit=24, flops=1):
    return pl.pallas_call(
        body,
        out_shape=outs,
        in_specs=[pl.BlockSpec(memory_space=pltpu.VMEM)] * len(operands),
        out_specs=[pl.BlockSpec(memory_space=pltpu.VMEM)] * len(outs),
        scratch_shapes=list(scratch),
        compiler_params=pltpu.CompilerParams(vmem_limit_bytes=limit * MIB),
        cost_estimate=pl.CostEstimate(flops=flops, bytes_accessed=1, transcendentals=0),
    )(*operands)


def swap(value, axis, offset):
    size = lax.axis_size(axis)
    return lax.ppermute(value, axis, [(at, at ^ offset) for at in range(size)])


def after(value, *others):
    return lax.optimization_barrier((value, *others))[0]


def across(value):
    size = lax.axis_size("patch")
    return [swap(value, "patch", at) if at else value for at in range(0, size, 2)]


def both_cores(blocks):
    return [part for block in blocks for part in (block, swap(block, "patch", 1))]


def swap_diagonal(value, offset):
    frames, size = lax.axis_size("frame"), lax.axis_size("patch")
    pairs = [
        (frame * size + at, (frame ^ 1) * size + (at ^ offset))
        for frame in range(frames)
        for at in range(size)
    ]
    return lax.ppermute(value, ("frame", "patch"), pairs)


def per_device(tokens, modulation, spatial_qkv, spatial_out, temporal_qkv, temporal_out):
    _, rows, width = tokens.shape
    shard = spatial_out.shape[0]
    count, frames = lax.axis_size("patch"), lax.axis_size("frame")
    period = rows // frames
    pieces, groups = frames // 2, count // 2
    shape = jax.ShapeDtypeStruct

    def with_sister(weights, *others):
        return [weights, swap(after(weights, *others), "patch", 1)]

    def exchange_frames(parts):
        offsets = reversed(range(pieces))
        return [swap(part, "frame", 2 * at) if at else part for at, part in zip(offsets, parts)]

    def project_paired(sent, weights):
        heads = swap(sent, "frame", 1)
        return call(paired_kernel, (heads, *weights), [halves_shape(F32)])[0]

    def return_updates(own, far):
        same = [swap(part, "patch", 2 * at) for at, part in enumerate(far[::2], 1)]
        diagonal = [swap_diagonal(part, 2 * at) for at, part in enumerate(far[1::2], 1)]
        return [own[0], *same, own[1], *diagonal]

    def halves_shape(dtype):
        return shape((rows // 2, width), dtype)

    own_shapes = [halves_shape(F32), shape((rows // 2, 2 * shard), BF16)]
    far_shapes = [halves_shape(BF16)] * (2 * groups - 2)
    piece_shapes = [shape((2 * period, width), BF16)] * pieces

    sister = swap(tokens, "patch", 1)
    far = across(tokens)[1:]
    (near,) = call(
        near_kernel,
        (modulation, spatial_qkv, tokens, sister),
        [shape((3 * shard, 2 * rows), F32)],
    )
    own_tokens, shared = call(
        functools.partial(share_kernel, period), (after(tokens, sister),), [halves_shape(BF16)] * 2
    )
    paired = swap(shared, "frame", 1)
    out_pair = with_sister(spatial_out, near)
    far = both_cores([after(block, near, paired) for block in far])
    temporal_pair = with_sister(temporal_qkv, *far)

    kept, sent = call(
        functools.partial(spatial_kernel, count),
        (modulation, spatial_qkv, near, *far),
        [shape((shard, groups * rows), BF16)] * 2,
        [pltpu.VMEM((3 * shard, (count - 2) * rows), F32), pltpu.VMEM((shard, count * rows), F32)],
    )
    parts = call(
        functools.partial(partial_kernel, period),
        (kept, swap(sent, "patch", 1), *out_pair),
        own_shapes + far_shapes,
    )
    late_pair = with_sister(temporal_out, parts[0])
    updates = return_updates((parts[0], project_paired(parts[1], out_pair)), parts[2:])
    middle, middle_sent, *parts = call(
        functools.partial(middle_kernel, pieces, groups),
        (modulation, own_tokens, paired, *updates),
        [shape((pieces, period, width), BF16)] * 2 + piece_shapes,
        [pltpu.VMEM((pieces, 2 * period, width), BF16)],
    )
    arrived = exchange_frames(parts)
    (segment,) = call(join_kernel, arrived, [shape((rows, width), BF16)])
    segments = across(segment)

    def attend_frames(own, segments, shapes):
        columns = len(segments) * rows
        return call(
            functools.partial(temporal_kernel, own, period, rows),
            (*temporal_pair, *late_pair, *segments),
            shapes,
            [pltpu.VMEM((6 * shard, columns), F32), pltpu.VMEM((2 * shard, columns), F32)],
        )

    kept, sent = attend_frames(True, [segment], own_shapes)
    received = project_paired(sent, late_pair)
    middle_other = swap(after(middle_sent, segment), "frame", 1)
    others = [after(block, received) for block in segments[1:]]
    far_parts = attend_frames(False, others, far_shapes)
    updates = return_updates((kept, received), far_parts)
    piece_shapes = [shape((period, width), BF16)] * pieces
    first, second = (
        exchange_frames(call(functools.partial(sum_kernel, pieces), part, piece_shapes))
        for part in (updates[:groups], updates[groups:])
    )
    (done,) = call(
        first_result_kernel,
        (modulation, middle, *first),
        [shape((pieces, period, width), BF16)],
        flops=4_000_000_000,
    )
    (result,) = call(
        result_kernel,
        (modulation, middle_other, done, *second),
        [shape((frames, period, width), BF16)],
    )
    return result.reshape(1, rows, width)


def solution(mesh):
    in_specs = (
        P("frame", "patch", None),
        P(),
        P("patch", None),
        P("patch", None),
        P("patch", None),
        P("patch", None),
    )
    out_specs = P("frame", "patch", None)
    return jax.shard_map(
        per_device, mesh=mesh, in_specs=in_specs, out_specs=out_specs, check_vma=False
    )
```

```python
import functools

import jax
import jax.numpy as jnp
from jax import lax
from jax.experimental import pallas as pl
from jax.experimental.pallas import tpu as pltpu
from jax.sharding import PartitionSpec as P

HD = 72
MIB = 1 << 20
LOG2E = 1.4426950408889634
F32 = jnp.float32
BF16 = jnp.bfloat16


def norm_rows(values, shift, scale):
    average = jnp.mean(values, axis=-1, keepdims=True)
    centred = values - average
    variance = jnp.mean(centred * centred, axis=-1, keepdims=True)
    normed = centred * lax.rsqrt(variance + 1e-06)
    return (normed * (1.0 + scale) + shift).astype(BF16)


def dot(left, right, left_dim=1, right_dim=0):
    return lax.dot_general(
        left, right, (((left_dim,), (right_dim,)), ((), ())), preferred_element_type=F32
    )


def soften(scores):
    top = jnp.max(scores, axis=0, keepdims=True)
    return jnp.exp2((scores - top) * (HD**-0.5 * LOG2E)).astype(BF16)


def mix(values, weights):
    ones = jnp.ones((8, values.shape[1]), F32)
    mixed = dot(jnp.concatenate([values, ones], axis=0).astype(BF16), weights)
    return mixed[:HD] * (1.0 / mixed[HD : HD + 1])


def project(mod_ref, weight_ref, token_refs, proj_ref):
    shift, scale = mod_ref[0:1, :], mod_ref[1:2, :]
    block = token_refs[0].shape[1]
    for at in range(0, len(token_refs), 2):
        rows = [norm_rows(ref[0].astype(F32), shift, scale) for ref in token_refs[at : at + 2]]
        rows = jnp.concatenate(rows, axis=0)
        proj_ref[:, at * block : (at + 2) * block] = dot(weight_ref[...], rows, 1, 1)


def near_kernel(mod_ref, weight_ref, own_ref, sister_ref, proj_ref):
    project(mod_ref, weight_ref, (own_ref, sister_ref), proj_ref)


def attend_patches(near_ref, far_ref, query_ref, heads_ref, kept_ref, sent_ref):
    columns, block = query_ref.shape[1], near_ref.shape[1] // 2

    def whole(start):
        return jnp.concatenate([ref[start : start + HD, :] for ref in (near_ref, far_ref)], axis=1)

    def score(head, at):
        base = head * 3 * HD
        query = query_ref[base : base + HD, at : at + 2 * block].astype(BF16)
        return dot(whole(base + HD).astype(BF16).T, query)

    heads = range(heads_ref.shape[0] // HD)
    steps = [(head, at) for head in heads for at in range(0, columns, 2 * block)]
    scores = score(*steps[0])
    for (head, at), later in zip(steps, [*steps[1:], None]):
        coming = score(*later) if later else None
        rows, cols = slice(head * HD, (head + 1) * HD), slice(at, at + 2 * block)
        heads_ref[rows, cols] = mix(whole(head * 3 * HD + 2 * HD), soften(scores))
        scores = coming
    for at in range(columns // block):
        out_ref = (kept_ref, sent_ref)[at % 2]
        cols = slice(at // 2 * block, (at // 2 + 1) * block)
        out_ref[:, cols] = heads_ref[:, at * block : (at + 1) * block].astype(BF16)


def far_queries_kernel(mod_ref, weight_ref, near_ref, *refs):
    token_refs, (far_ref, kept_ref, sent_ref, heads_ref) = refs[:-4], refs[-4:]
    project(mod_ref, weight_ref, token_refs, far_ref)
    attend_patches(near_ref, far_ref, far_ref, heads_ref, kept_ref, sent_ref)


def near_queries_kernel(near_ref, far_ref, kept_ref, sent_ref, heads_ref):
    attend_patches(near_ref, far_ref, near_ref, heads_ref, kept_ref, sent_ref)


def halves(value, size):
    return [
        jnp.concatenate(
            [value[at : at + size] for at in range(first * size, value.shape[0], 2 * size)], axis=0
        )
        for first in range(2)
    ]


def of_this_half(value, size):
    even, odd = (half.astype(F32) for half in halves(value, size))
    first = lax.axis_index("frame") % 2 == 0
    return jnp.where(first, even, odd), jnp.where(first, odd, even)


def share_kernel(period, token_ref, kept_ref, sent_ref):
    for ref, half in zip((kept_ref, sent_ref), of_this_half(token_ref[0], period)):
        ref[...] = half.astype(BF16)


def joined(refs):
    return jnp.concatenate([ref[...] for ref in refs], axis=0)


def far_partial_kernel(period, *refs):
    head_refs, weights, out_refs = refs[:2], joined(refs[2:4]), refs[4:]
    block = 2 * out_refs[0].shape[0]
    for at in range(len(out_refs) // 2):
        cols = slice(at * block, (at + 1) * block)
        heads = jnp.concatenate([ref[:, cols] for ref in head_refs], axis=0).T
        parts = of_this_half(dot(heads, weights), period)
        for ref, part in zip(out_refs[2 * at : 2 * at + 2], parts):
            ref[...] = part.astype(ref.dtype)


def near_partial_kernel(period, *refs):
    head_refs, weights, (kept_ref, sent_ref) = refs[:2], joined(refs[2:4]), refs[4:]
    kept, sent = of_this_half(joined(head_refs).T, period)
    kept_ref[...] = dot(kept.astype(BF16), weights)
    sent_ref[...] = sent.astype(BF16)


def paired_kernel(head_ref, *refs):
    refs[-1][...] = dot(head_ref[...], joined(refs[:-1]))


def far_sum_kernel(count, *refs):
    for at, ref in enumerate(refs[2 * count :]):
        ref[...] = sum(part[...].astype(F32) for part in refs[at * count : (at + 1) * count])


def total_updates(groups, refs):
    return [
        sum(ref[...].astype(F32) for ref in refs[at * groups : (at + 1) * groups])
        for at in range(2)
    ]


def middle_kernel(pieces, mod_ref, own_ref, paired_ref, *refs):
    kept_ref, sent_ref, *piece_refs, scratch = refs[4:]
    updates = total_updates(2, refs)
    _, period, width = kept_ref.shape
    inputs = (own_ref[...], paired_ref[...])
    for at, (tokens, middle_ref) in enumerate(zip(inputs, (kept_ref, sent_ref))):
        update = updates[at]
        middle = (tokens.astype(F32) + mod_ref[2:3, :] * update).astype(BF16)
        normed = norm_rows(middle.astype(F32), mod_ref[3:4, :], mod_ref[4:5, :])
        for piece in range(pieces):
            rows = slice(piece * period, (piece + 1) * period)
            middle_ref[piece] = middle[rows]
            scratch[piece, at * period : (at + 1) * period, :] = normed[rows]
    here = lax.axis_index("frame") // 2
    for at, ref in enumerate(piece_refs):
        ref[...] = scratch[here ^ (pieces - 1 - at)]


def join_kernel(*refs):
    size = refs[0].shape[0]
    for at, ref in enumerate(refs[:-1]):
        refs[-1][at * size : (at + 1) * size, :] = ref[...]


def temporal_kernel(own, period, block, *refs):
    weight_refs, output_refs, (proj_ref, heads_ref) = refs[:2], refs[2:4], refs[-2:]
    groups = proj_ref.shape[1] // block
    row_refs, update_refs = refs[4 : -2 - 2 * groups], refs[-2 - 2 * groups : -2]
    rows = jnp.concatenate([ref[...] for ref in row_refs], axis=0)
    depth = weight_refs[0].shape[0]
    for core in range(2):
        proj_ref[core * depth : (core + 1) * depth, :] = dot(weight_refs[core][...], rows, 1, 1)
    heads = 2 * depth // (3 * HD)
    key_patch = lax.broadcasted_iota(jnp.int32, (block, block), 0) % period
    query_patch = lax.broadcasted_iota(jnp.int32, (block, block), 1) % period
    mask = key_patch == query_patch
    weights = joined(output_refs)
    for group in range(groups):
        cols = slice(group * block, (group + 1) * block)

        def part(head, at):
            start = (head * 3 + at) * HD
            return proj_ref[start : start + HD, cols]

        scores = []
        for head in range(heads):
            keys, query = part(head, 1).astype(BF16).T, part(head, 0).astype(BF16)
            scores.append(jnp.where(mask, dot(keys, query), -1e30))
        soft = soften(jnp.concatenate(scores, axis=1))
        for head in range(heads):
            mixed = mix(part(head, 2), soft[:, head * block : (head + 1) * block])
            heads_ref[head * HD : (head + 1) * HD, cols] = mixed
        mixed = heads_ref[:, cols].astype(BF16).T
        if own:
            kept, sent = halves(mixed, period)
            parts = dot(kept, weights), sent
        else:
            parts = halves(dot(mixed, weights), period)
        for ref, half in zip(update_refs[2 * group : 2 * group + 2], parts):
            ref[...] = half.astype(ref.dtype)


def sum_kernel(groups, *refs):
    piece_refs = refs[2 * groups :]
    period = piece_refs[0].shape[0] // 2
    for at, update in enumerate(total_updates(groups, refs)):
        update = update.astype(BF16)
        for piece, ref in enumerate(piece_refs):
            rows = update[piece * period : (piece + 1) * period]
            ref[at * period : (at + 1) * period, :] = rows


def result_kernel(pieces, mod_ref, kept_ref, other_ref, *refs):
    piece_refs, out_ref = refs[:-1], refs[-1]
    period = kept_ref.shape[1]
    here = lax.axis_index("frame")
    for at, ref in enumerate(piece_refs):
        there = here // 2 ^ (pieces - 1 - at)
        for half, middle_ref in enumerate((kept_ref, other_ref)):
            update = ref[half * period : (half + 1) * period, :].astype(F32)
            middle = middle_ref[there].astype(F32)
            out_ref[2 * there + (here % 2 ^ half)] = (middle + mod_ref[5:6, :] * update).astype(
                BF16
            )


def call(body, operands, outs, scratch=(), limit=24, flops=1):
    return pl.pallas_call(
        body,
        out_shape=outs,
        in_specs=[pl.BlockSpec(memory_space=pltpu.VMEM)] * len(operands),
        out_specs=[pl.BlockSpec(memory_space=pltpu.VMEM)] * len(outs),
        scratch_shapes=list(scratch),
        compiler_params=pltpu.CompilerParams(vmem_limit_bytes=limit * MIB),
        cost_estimate=pl.CostEstimate(flops=flops, bytes_accessed=1, transcendentals=0),
    )(*operands)


def swap(value, axis, offset):
    size = lax.axis_size(axis)
    return lax.ppermute(value, axis, [(at, at ^ offset) for at in range(size)])


def after(value, *others):
    return lax.optimization_barrier((value, *others))[0]


def across(value):
    size = lax.axis_size("patch")
    return [swap(value, "patch", at) if at else value for at in range(0, size, 2)]


def both_cores(blocks):
    return [part for block in blocks for part in (block, swap(block, "patch", 1))]


def swap_diagonal(value, offset):
    frames, size = lax.axis_size("frame"), lax.axis_size("patch")
    pairs = [
        (frame * size + at, (frame ^ 1) * size + (at ^ offset))
        for frame in range(frames)
        for at in range(size)
    ]
    return lax.ppermute(value, ("frame", "patch"), pairs)


def per_device(tokens, modulation, spatial_qkv, spatial_out, temporal_qkv, temporal_out):
    _, rows, width = tokens.shape
    shard = spatial_out.shape[0]
    count, frames = lax.axis_size("patch"), lax.axis_size("frame")
    period = rows // frames
    pieces, groups = frames // 2, count // 2
    shape = jax.ShapeDtypeStruct

    def with_sister(weights, *others):
        return [weights, swap(after(weights, *others), "patch", 1)]

    def exchange_frames(parts):
        offsets = reversed(range(pieces))
        return [swap(part, "frame", 2 * at) if at else part for at, part in zip(offsets, parts)]

    def project_paired(sent, weights):
        heads = swap(sent, "frame", 1)
        return call(paired_kernel, (heads, *weights), [halves_shape(F32)])[0]

    def return_updates(own, far):
        diagonal = [swap_diagonal(part, 2 * at) for at, part in enumerate(far[1::2], 1)]
        same = [swap(part, "patch", 2 * at) for at, part in enumerate(far[::2], 1)]
        return [own[0], *same, own[1], *diagonal]

    def halves_shape(dtype):
        return shape((rows // 2, width), dtype)

    own_shapes = [halves_shape(F32), shape((rows // 2, 2 * shard), BF16)]
    far_shapes = [halves_shape(BF16)] * (2 * groups - 2)
    piece_shapes = [shape((2 * period, width), BF16)] * pieces

    sister = swap(tokens, "patch", 1)
    far = across(tokens)[1:]
    (near,) = call(
        near_kernel,
        (modulation, spatial_qkv, tokens, sister),
        [shape((3 * shard, 2 * rows), F32)],
    )
    own_tokens, shared = call(
        functools.partial(share_kernel, period), (after(tokens, sister),), [halves_shape(BF16)] * 2
    )
    paired = swap(shared, "frame", 1)
    out_pair = with_sister(spatial_out, near)
    far = both_cores([after(block, near, paired) for block in far])

    columns = (groups - 1) * rows
    far_proj, kept, sent = call(
        far_queries_kernel,
        (modulation, spatial_qkv, near, *far),
        [shape((3 * shard, 2 * columns), F32)] + [shape((shard, columns), BF16)] * 2,
        [pltpu.VMEM((shard, 2 * columns), F32)],
    )
    far_parts = call(
        functools.partial(far_partial_kernel, period),
        (kept, swap(sent, "patch", 1), *out_pair),
        far_shapes,
    )
    temporal_pair = with_sister(temporal_qkv, far_parts[0])
    kept, sent = call(
        near_queries_kernel,
        (after(near, far_parts[0]), far_proj),
        [shape((shard, rows), BF16)] * 2,
        [pltpu.VMEM((shard, 2 * rows), F32)],
        flops=1,
    )
    received = swap(sent, "patch", 1)
    own_parts = call(
        functools.partial(near_partial_kernel, period), (kept, received, *out_pair), own_shapes
    )
    late_pair = with_sister(temporal_out, received)
    updates = return_updates((own_parts[0], project_paired(own_parts[1], out_pair)), far_parts)
    sums = call(
        functools.partial(far_sum_kernel, groups - 1),
        (*updates[1:groups], *updates[groups + 1 :]),
        [halves_shape(F32)] * 2,
        flops=4_000_000_000,
    )
    updates = [updates[0], sums[0], updates[groups], sums[1]]
    middle, middle_sent, *parts = call(
        functools.partial(middle_kernel, pieces),
        (modulation, own_tokens, paired, *updates),
        [shape((pieces, period, width), BF16)] * 2 + piece_shapes,
        [pltpu.VMEM((pieces, 2 * period, width), BF16)],
    )
    arrived = exchange_frames(parts)
    (segment,) = call(join_kernel, arrived, [shape((rows, width), BF16)])
    segments = across(segment)

    def attend_frames(own, segments, shapes):
        columns = len(segments) * rows
        return call(
            functools.partial(temporal_kernel, own, period, rows),
            (*temporal_pair, *late_pair, *segments),
            shapes,
            [pltpu.VMEM((6 * shard, columns), F32), pltpu.VMEM((2 * shard, columns), F32)],
        )

    kept, sent = attend_frames(True, [segment], own_shapes)
    received = project_paired(sent, late_pair)
    middle_other = swap(after(middle_sent, segment), "frame", 1)
    others = [after(block, received) for block in segments[1:]]
    far_parts = attend_frames(False, others, far_shapes)
    updates = return_updates((kept, received), far_parts)
    parts = call(
        functools.partial(sum_kernel, groups),
        updates,
        piece_shapes,
    )
    (result,) = call(
        functools.partial(result_kernel, pieces),
        (modulation, middle, middle_other, *exchange_frames(parts)),
        [shape((frames, period, width), BF16)],
    )
    return result.reshape(1, rows, width)


def solution(mesh):
    in_specs = (
        P("frame", "patch", None),
        P(),
        P("patch", None),
        P("patch", None),
        P("patch", None),
        P("patch", None),
    )
    out_specs = P("frame", "patch", None)
    return jax.shard_map(
        per_device, mesh=mesh, in_specs=in_specs, out_specs=out_specs, check_vma=False
    )
```

```python
import functools

import jax
import jax.numpy as jnp
from jax import lax
from jax.experimental import pallas as pl
from jax.experimental.pallas import tpu as pltpu
from jax.sharding import PartitionSpec as P

HD = 72
MIB = 1 << 20
LOG2E = 1.4426950408889634
F32 = jnp.float32
BF16 = jnp.bfloat16


def norm_rows(values, shift, scale):
    average = jnp.mean(values, axis=-1, keepdims=True)
    centred = values - average
    variance = jnp.mean(centred * centred, axis=-1, keepdims=True)
    normed = centred * lax.rsqrt(variance + 1e-06)
    return (normed * (1.0 + scale) + shift).astype(BF16)


def dot(left, right, left_dim=1, right_dim=0):
    return lax.dot_general(
        left, right, (((left_dim,), (right_dim,)), ((), ())), preferred_element_type=F32
    )


def soften(scores):
    top = jnp.max(scores, axis=0, keepdims=True)
    return jnp.exp2((scores - top) * (HD**-0.5 * LOG2E)).astype(BF16)


def mix(values, weights):
    ones = jnp.ones((8, values.shape[1]), F32)
    mixed = dot(jnp.concatenate([values, ones], axis=0).astype(BF16), weights)
    return mixed[:HD] * (1.0 / mixed[HD : HD + 1])


def project(mod_ref, weight_ref, token_refs, proj_ref):
    shift, scale = mod_ref[0:1, :], mod_ref[1:2, :]
    block = token_refs[0].shape[1]
    for at in range(0, len(token_refs), 2):
        rows = [norm_rows(ref[0].astype(F32), shift, scale) for ref in token_refs[at : at + 2]]
        rows = jnp.concatenate(rows, axis=0)
        proj_ref[:, at * block : (at + 2) * block] = dot(weight_ref[...], rows, 1, 1)


def near_kernel(mod_ref, weight_ref, own_ref, sister_ref, proj_ref):
    project(mod_ref, weight_ref, (own_ref, sister_ref), proj_ref)


def spatial_kernel(count, mod_ref, weight_ref, near_ref, *refs):
    token_refs, (kept_ref, sent_ref, far_ref, heads_ref) = refs[: count - 2], refs[count - 2 :]
    block = token_refs[0].shape[1]
    heads = weight_ref.shape[0] // (3 * HD)
    project(mod_ref, weight_ref, token_refs, far_ref)

    def whole(start):
        return jnp.concatenate([ref[start : start + HD, :] for ref in (near_ref, far_ref)], axis=1)

    def score(head, at):
        base = head * 3 * HD
        source, start = (near_ref, 0) if at == 0 else (far_ref, (at - 2) * block)
        query = source[base : base + HD, start : start + 2 * block].astype(BF16)
        return dot(whole(base + HD).astype(BF16).T, query)

    steps = [(head, at) for head in range(heads) for at in range(0, count, 2)]
    scores = score(*steps[0])
    for (head, at), later in zip(steps, [*steps[1:], None]):
        coming = score(*later) if later else None
        rows, cols = slice(head * HD, (head + 1) * HD), slice(at * block, (at + 2) * block)
        heads_ref[rows, cols] = mix(whole(head * 3 * HD + 2 * HD), soften(scores))
        scores = coming
    for at in range(count):
        out_ref = (kept_ref, sent_ref)[at % 2]
        cols = slice(at // 2 * block, (at // 2 + 1) * block)
        out_ref[:, cols] = heads_ref[:, at * block : (at + 1) * block].astype(BF16)


def halves(value, size):
    return [
        jnp.concatenate(
            [value[at : at + size] for at in range(first * size, value.shape[0], 2 * size)], axis=0
        )
        for first in range(2)
    ]


def of_this_half(value, size):
    even, odd = (half.astype(F32) for half in halves(value, size))
    first = lax.axis_index("frame") % 2 == 0
    return jnp.where(first, even, odd), jnp.where(first, odd, even)


def share_kernel(period, token_ref, kept_ref, sent_ref):
    for ref, half in zip((kept_ref, sent_ref), of_this_half(token_ref[0], period)):
        ref[...] = half.astype(BF16)


def joined(refs):
    return jnp.concatenate([ref[...] for ref in refs], axis=0)


def partial_kernel(period, *refs):
    head_refs, weights, out_refs = refs[:2], joined(refs[2:4]), refs[4:]
    block = 2 * out_refs[0].shape[0]
    for at in range(len(out_refs) // 2):
        cols = slice(at * block, (at + 1) * block)
        heads = jnp.concatenate([ref[:, cols] for ref in head_refs], axis=0).T
        if at == 0:
            kept, sent = (half.astype(BF16) for half in of_this_half(heads, period))
            parts = dot(kept, weights), sent
        else:
            parts = of_this_half(dot(heads, weights), period)
        for ref, part in zip(out_refs[2 * at : 2 * at + 2], parts):
            ref[...] = part.astype(ref.dtype)


def paired_kernel(head_ref, *refs):
    refs[-1][...] = dot(head_ref[...], joined(refs[:-1]))


def total_updates(groups, refs):
    return [
        sum(ref[...].astype(F32) for ref in refs[at * groups : (at + 1) * groups])
        for at in range(2)
    ]


def middle_kernel(pieces, groups, mod_ref, own_ref, paired_ref, *refs):
    kept_ref, sent_ref, *piece_refs, scratch = refs[2 * groups :]
    updates = total_updates(groups, refs)
    _, period, width = kept_ref.shape
    inputs = (own_ref[...], paired_ref[...])
    for at, (tokens, middle_ref) in enumerate(zip(inputs, (kept_ref, sent_ref))):
        update = updates[at]
        middle = (tokens.astype(F32) + mod_ref[2:3, :] * update).astype(BF16)
        normed = norm_rows(middle.astype(F32), mod_ref[3:4, :], mod_ref[4:5, :])
        for piece in range(pieces):
            rows = slice(piece * period, (piece + 1) * period)
            middle_ref[piece] = middle[rows]
            scratch[piece, at * period : (at + 1) * period, :] = normed[rows]
    here = lax.axis_index("frame") // 2
    for at, ref in enumerate(piece_refs):
        ref[...] = scratch[here ^ (pieces - 1 - at)]


def join_kernel(*refs):
    size = refs[0].shape[0]
    for at, ref in enumerate(refs[:-1]):
        refs[-1][at * size : (at + 1) * size, :] = ref[...]


def temporal_kernel(own, period, block, *refs):
    weight_refs, output_refs, (proj_ref, heads_ref) = refs[:2], refs[2:4], refs[-2:]
    groups = proj_ref.shape[1] // block
    row_refs, update_refs = refs[4 : -2 - 2 * groups], refs[-2 - 2 * groups : -2]
    rows = jnp.concatenate([ref[...] for ref in row_refs], axis=0)
    depth = weight_refs[0].shape[0]
    for core in range(2):
        proj_ref[core * depth : (core + 1) * depth, :] = dot(weight_refs[core][...], rows, 1, 1)
    heads = 2 * depth // (3 * HD)
    key_patch = lax.broadcasted_iota(jnp.int32, (block, block), 0) % period
    query_patch = lax.broadcasted_iota(jnp.int32, (block, block), 1) % period
    mask = key_patch == query_patch
    weights = joined(output_refs)
    for group in range(groups):
        cols = slice(group * block, (group + 1) * block)

        def part(head, at):
            start = (head * 3 + at) * HD
            return proj_ref[start : start + HD, cols]

        scores = []
        for head in range(heads):
            keys, query = part(head, 1).astype(BF16).T, part(head, 0).astype(BF16)
            scores.append(jnp.where(mask, dot(keys, query), -1e30))
        soft = soften(jnp.concatenate(scores, axis=1))
        for head in range(heads):
            mixed = mix(part(head, 2), soft[:, head * block : (head + 1) * block])
            heads_ref[head * HD : (head + 1) * HD, cols] = mixed
        mixed = heads_ref[:, cols].astype(BF16).T
        if own:
            kept, sent = halves(mixed, period)
            parts = dot(kept, weights), sent
        else:
            parts = halves(dot(mixed, weights), period)
        for ref, half in zip(update_refs[2 * group : 2 * group + 2], parts):
            ref[...] = half.astype(ref.dtype)


def sum_kernel(groups, *refs):
    piece_refs = refs[2 * groups :]
    period = piece_refs[0].shape[0] // 2
    for at, update in enumerate(total_updates(groups, refs)):
        update = update.astype(BF16)
        for piece, ref in enumerate(piece_refs):
            rows = update[piece * period : (piece + 1) * period]
            ref[at * period : (at + 1) * period, :] = rows


def result_kernel(pieces, mod_ref, kept_ref, other_ref, *refs):
    piece_refs, out_ref = refs[:-1], refs[-1]
    period = kept_ref.shape[1]
    here = lax.axis_index("frame")
    for at, ref in enumerate(piece_refs):
        there = here // 2 ^ (pieces - 1 - at)
        for half, middle_ref in enumerate((kept_ref, other_ref)):
            update = ref[half * period : (half + 1) * period, :].astype(F32)
            middle = middle_ref[there].astype(F32)
            out_ref[2 * there + (here % 2 ^ half)] = (middle + mod_ref[5:6, :] * update).astype(
                BF16
            )


def call(body, operands, outs, scratch=(), limit=24, flops=1):
    return pl.pallas_call(
        body,
        out_shape=outs,
        in_specs=[pl.BlockSpec(memory_space=pltpu.VMEM)] * len(operands),
        out_specs=[pl.BlockSpec(memory_space=pltpu.VMEM)] * len(outs),
        scratch_shapes=list(scratch),
        compiler_params=pltpu.CompilerParams(vmem_limit_bytes=limit * MIB),
        cost_estimate=pl.CostEstimate(flops=flops, bytes_accessed=1, transcendentals=0),
    )(*operands)


def swap(value, axis, offset):
    size = lax.axis_size(axis)
    return lax.ppermute(value, axis, [(at, at ^ offset) for at in range(size)])


def after(value, *others):
    return lax.optimization_barrier((value, *others))[0]


def across(value):
    size = lax.axis_size("patch")
    return [swap(value, "patch", at) if at else value for at in range(0, size, 2)]


def both_cores(blocks):
    return [part for block in blocks for part in (block, swap(block, "patch", 1))]


def swap_diagonal(value, offset):
    frames, size = lax.axis_size("frame"), lax.axis_size("patch")
    pairs = [
        (frame * size + at, (frame ^ 1) * size + (at ^ offset))
        for frame in range(frames)
        for at in range(size)
    ]
    return lax.ppermute(value, ("frame", "patch"), pairs)


def per_device(tokens, modulation, spatial_qkv, spatial_out, temporal_qkv, temporal_out):
    _, rows, width = tokens.shape
    shard = spatial_out.shape[0]
    count, frames = lax.axis_size("patch"), lax.axis_size("frame")
    period = rows // frames
    pieces, groups = frames // 2, count // 2
    shape = jax.ShapeDtypeStruct

    def with_sister(weights, *others):
        return [weights, swap(after(weights, *others), "patch", 1)]

    def exchange_frames(parts):
        offsets = reversed(range(pieces))
        return [swap(part, "frame", 2 * at) if at else part for at, part in zip(offsets, parts)]

    def project_paired(sent, weights):
        heads = swap(sent, "frame", 1)
        return call(paired_kernel, (heads, *weights), [halves_shape(F32)], flops=1_000_000_000)[0]

    def return_updates(own, far):
        same = [swap(part, "patch", 2 * at) for at, part in enumerate(far[::2], 1)]
        diagonal = [swap_diagonal(part, 2 * at) for at, part in enumerate(far[1::2], 1)]
        return [own[0], *same, own[1], *diagonal]

    def halves_shape(dtype):
        return shape((rows // 2, width), dtype)

    own_shapes = [halves_shape(F32), shape((rows // 2, 2 * shard), BF16)]
    far_shapes = [halves_shape(BF16)] * (2 * groups - 2)
    piece_shapes = [shape((2 * period, width), BF16)] * pieces

    sister = swap(tokens, "patch", 1)
    far = across(tokens)[1:]
    (near,) = call(
        near_kernel,
        (modulation, spatial_qkv, tokens, sister),
        [shape((3 * shard, 2 * rows), F32)],
    )
    own_tokens, shared = call(
        functools.partial(share_kernel, period), (after(tokens, sister),), [halves_shape(BF16)] * 2
    )
    paired = swap(shared, "frame", 1)
    out_pair = with_sister(spatial_out, near)
    far = both_cores([after(block, near, paired) for block in far])
    temporal_pair = with_sister(temporal_qkv, *far)

    kept, sent = call(
        functools.partial(spatial_kernel, count),
        (modulation, spatial_qkv, near, *far),
        [shape((shard, groups * rows), BF16)] * 2,
        [pltpu.VMEM((3 * shard, (count - 2) * rows), F32), pltpu.VMEM((shard, count * rows), F32)],
    )
    parts = call(
        functools.partial(partial_kernel, period),
        (kept, swap(sent, "patch", 1), *out_pair),
        own_shapes + far_shapes,
    )
    late_pair = with_sister(temporal_out, parts[0])
    updates = return_updates((parts[0], project_paired(parts[1], out_pair)), parts[2:])
    middle, middle_sent, *parts = call(
        functools.partial(middle_kernel, pieces, groups),
        (modulation, own_tokens, paired, *updates),
        [shape((pieces, period, width), BF16)] * 2 + piece_shapes,
        [pltpu.VMEM((pieces, 2 * period, width), BF16)],
    )
    arrived = exchange_frames(parts)
    (segment,) = call(join_kernel, arrived, [shape((rows, width), BF16)])
    segments = across(segment)

    def attend_frames(own, segments, shapes):
        columns = len(segments) * rows
        return call(
            functools.partial(temporal_kernel, own, period, rows),
            (*temporal_pair, *late_pair, *segments),
            shapes,
            [pltpu.VMEM((6 * shard, columns), F32), pltpu.VMEM((2 * shard, columns), F32)],
        )

    kept, sent = attend_frames(True, [segment], own_shapes)
    received = project_paired(sent, late_pair)
    middle_other = swap(after(middle_sent, segment), "frame", 1)
    others = [after(block, received) for block in segments[1:]]
    far_parts = attend_frames(False, others, far_shapes)
    updates = return_updates((kept, received), far_parts)
    parts = call(
        functools.partial(sum_kernel, groups),
        updates,
        piece_shapes,
    )
    (result,) = call(
        functools.partial(result_kernel, pieces),
        (modulation, middle, middle_other, *exchange_frames(parts)),
        [shape((frames, period, width), BF16)],
    )
    return result.reshape(1, rows, width)


def solution(mesh):
    in_specs = (
        P("frame", "patch", None),
        P(),
        P("patch", None),
        P("patch", None),
        P("patch", None),
        P("patch", None),
    )
    out_specs = P("frame", "patch", None)
    return jax.shard_map(
        per_device, mesh=mesh, in_specs=in_specs, out_specs=out_specs, check_vma=False
    )
```

```python
import functools

import jax
import jax.numpy as jnp
from jax import lax
from jax.experimental import pallas as pl
from jax.experimental.pallas import tpu as pltpu
from jax.sharding import PartitionSpec as P

HD = 72
MIB = 1 << 20
LOG2E = 1.4426950408889634
F32 = jnp.float32
BF16 = jnp.bfloat16


def norm_rows(values, shift, scale):
    average = jnp.mean(values, axis=-1, keepdims=True)
    centred = values - average
    variance = jnp.mean(centred * centred, axis=-1, keepdims=True)
    normed = centred * lax.rsqrt(variance + 1e-06)
    return (normed * (1.0 + scale) + shift).astype(BF16)


def dot(left, right, left_dim=1, right_dim=0):
    return lax.dot_general(
        left, right, (((left_dim,), (right_dim,)), ((), ())), preferred_element_type=F32
    )


def soften(scores):
    top = jnp.max(scores, axis=0, keepdims=True)
    return jnp.exp2((scores - top) * (HD**-0.5 * LOG2E)).astype(BF16)


def mix(values, weights):
    ones = jnp.ones((8, values.shape[1]), F32)
    mixed = dot(jnp.concatenate([values, ones], axis=0).astype(BF16), weights)
    return mixed[:HD] * (1.0 / mixed[HD : HD + 1])


def project(mod_ref, weight_ref, token_refs, proj_ref):
    shift, scale = mod_ref[0:1, :], mod_ref[1:2, :]
    block = token_refs[0].shape[1]
    for at in range(0, len(token_refs), 2):
        rows = [norm_rows(ref[0].astype(F32), shift, scale) for ref in token_refs[at : at + 2]]
        rows = jnp.concatenate(rows, axis=0)
        proj_ref[:, at * block : (at + 2) * block] = dot(weight_ref[...], rows, 1, 1)


def near_kernel(mod_ref, weight_ref, own_ref, sister_ref, proj_ref):
    project(mod_ref, weight_ref, (own_ref, sister_ref), proj_ref)


def attend_patches(near_ref, far_ref, query_ref, heads_ref, kept_ref, sent_ref):
    columns, block = query_ref.shape[1], near_ref.shape[1] // 2

    def whole(start):
        return jnp.concatenate([ref[start : start + HD, :] for ref in (near_ref, far_ref)], axis=1)

    def score(head, at):
        base = head * 3 * HD
        query = query_ref[base : base + HD, at : at + 2 * block].astype(BF16)
        return dot(whole(base + HD).astype(BF16).T, query)

    heads = range(heads_ref.shape[0] // HD)
    steps = [(head, at) for head in heads for at in range(0, columns, 2 * block)]
    scores = score(*steps[0])
    for (head, at), later in zip(steps, [*steps[1:], None]):
        coming = score(*later) if later else None
        rows, cols = slice(head * HD, (head + 1) * HD), slice(at, at + 2 * block)
        heads_ref[rows, cols] = mix(whole(head * 3 * HD + 2 * HD), soften(scores))
        scores = coming
    for at in range(columns // block):
        out_ref = (kept_ref, sent_ref)[at % 2]
        cols = slice(at // 2 * block, (at // 2 + 1) * block)
        out_ref[:, cols] = heads_ref[:, at * block : (at + 1) * block].astype(BF16)


def far_queries_kernel(mod_ref, weight_ref, near_ref, *refs):
    token_refs, (far_ref, kept_ref, sent_ref, heads_ref) = refs[:-4], refs[-4:]
    project(mod_ref, weight_ref, token_refs, far_ref)
    attend_patches(near_ref, far_ref, far_ref, heads_ref, kept_ref, sent_ref)


def near_queries_kernel(near_ref, far_ref, kept_ref, sent_ref, heads_ref):
    attend_patches(near_ref, far_ref, near_ref, heads_ref, kept_ref, sent_ref)


def halves(value, size):
    return [
        jnp.concatenate(
            [value[at : at + size] for at in range(first * size, value.shape[0], 2 * size)], axis=0
        )
        for first in range(2)
    ]


def of_this_half(value, size):
    even, odd = (half.astype(F32) for half in halves(value, size))
    first = lax.axis_index("frame") % 2 == 0
    return jnp.where(first, even, odd), jnp.where(first, odd, even)


def share_kernel(period, token_ref, kept_ref, sent_ref):
    for ref, half in zip((kept_ref, sent_ref), of_this_half(token_ref[0], period)):
        ref[...] = half.astype(BF16)


def joined(refs):
    return jnp.concatenate([ref[...] for ref in refs], axis=0)


def far_partial_kernel(period, *refs):
    head_refs, weights, out_refs = refs[:2], joined(refs[2:4]), refs[4:]
    block = 2 * out_refs[0].shape[0]
    for at in range(len(out_refs) // 2):
        cols = slice(at * block, (at + 1) * block)
        heads = jnp.concatenate([ref[:, cols] for ref in head_refs], axis=0).T
        parts = of_this_half(dot(heads, weights), period)
        for ref, part in zip(out_refs[2 * at : 2 * at + 2], parts):
            ref[...] = part.astype(ref.dtype)


def near_partial_kernel(period, *refs):
    head_refs, weights, (kept_ref, sent_ref) = refs[:2], joined(refs[2:4]), refs[4:]
    kept, sent = of_this_half(joined(head_refs).T, period)
    kept_ref[...] = dot(kept.astype(BF16), weights)
    sent_ref[...] = sent.astype(BF16)


def paired_kernel(head_ref, *refs):
    refs[-1][...] = dot(head_ref[...], joined(refs[:-1]))


def far_sum_kernel(count, *refs):
    for at, ref in enumerate(refs[2 * count :]):
        ref[...] = sum(part[...].astype(F32) for part in refs[at * count : (at + 1) * count])


def total_updates(groups, refs):
    return [
        sum(ref[...].astype(F32) for ref in refs[at * groups : (at + 1) * groups])
        for at in range(2)
    ]


def middle_kernel(pieces, mod_ref, own_ref, paired_ref, *refs):
    kept_ref, sent_ref, *piece_refs, scratch = refs[4:]
    updates = total_updates(2, refs)
    _, period, width = kept_ref.shape
    inputs = (own_ref[...], paired_ref[...])
    for at, (tokens, middle_ref) in enumerate(zip(inputs, (kept_ref, sent_ref))):
        update = updates[at]
        middle = (tokens.astype(F32) + mod_ref[2:3, :] * update).astype(BF16)
        normed = norm_rows(middle.astype(F32), mod_ref[3:4, :], mod_ref[4:5, :])
        for piece in range(pieces):
            rows = slice(piece * period, (piece + 1) * period)
            middle_ref[piece] = middle[rows]
            scratch[piece, at * period : (at + 1) * period, :] = normed[rows]
    here = lax.axis_index("frame") // 2
    for at, ref in enumerate(piece_refs):
        ref[...] = scratch[here ^ (pieces - 1 - at)]


def join_kernel(*refs):
    size = refs[0].shape[0]
    for at, ref in enumerate(refs[:-1]):
        refs[-1][at * size : (at + 1) * size, :] = ref[...]


def temporal_kernel(own, period, block, *refs):
    weight_refs, output_refs, (proj_ref, heads_ref) = refs[:2], refs[2:4], refs[-2:]
    groups = proj_ref.shape[1] // block
    row_refs, update_refs = refs[4 : -2 - 2 * groups], refs[-2 - 2 * groups : -2]
    rows = jnp.concatenate([ref[...] for ref in row_refs], axis=0)
    depth = weight_refs[0].shape[0]
    for core in range(2):
        proj_ref[core * depth : (core + 1) * depth, :] = dot(weight_refs[core][...], rows, 1, 1)
    heads = 2 * depth // (3 * HD)
    key_patch = lax.broadcasted_iota(jnp.int32, (block, block), 0) % period
    query_patch = lax.broadcasted_iota(jnp.int32, (block, block), 1) % period
    mask = key_patch == query_patch
    weights = joined(output_refs)
    for group in range(groups):
        cols = slice(group * block, (group + 1) * block)

        def part(head, at):
            start = (head * 3 + at) * HD
            return proj_ref[start : start + HD, cols]

        scores = []
        for head in range(heads):
            keys, query = part(head, 1).astype(BF16).T, part(head, 0).astype(BF16)
            scores.append(jnp.where(mask, dot(keys, query), -1e30))
        soft = soften(jnp.concatenate(scores, axis=1))
        for head in range(heads):
            mixed = mix(part(head, 2), soft[:, head * block : (head + 1) * block])
            heads_ref[head * HD : (head + 1) * HD, cols] = mixed
        mixed = heads_ref[:, cols].astype(BF16).T
        if own:
            kept, sent = halves(mixed, period)
            parts = dot(kept, weights), sent
        else:
            parts = halves(dot(mixed, weights), period)
        for ref, half in zip(update_refs[2 * group : 2 * group + 2], parts):
            ref[...] = half.astype(ref.dtype)


def sum_kernel(groups, *refs):
    piece_refs = refs[2 * groups :]
    period = piece_refs[0].shape[0] // 2
    for at, update in enumerate(total_updates(groups, refs)):
        update = update.astype(BF16)
        for piece, ref in enumerate(piece_refs):
            rows = update[piece * period : (piece + 1) * period]
            ref[at * period : (at + 1) * period, :] = rows


def result_kernel(pieces, mod_ref, kept_ref, other_ref, *refs):
    piece_refs, out_ref = refs[:-1], refs[-1]
    period = kept_ref.shape[1]
    here = lax.axis_index("frame")
    for at, ref in enumerate(piece_refs):
        there = here // 2 ^ (pieces - 1 - at)
        for half, middle_ref in enumerate((kept_ref, other_ref)):
            update = ref[half * period : (half + 1) * period, :].astype(F32)
            middle = middle_ref[there].astype(F32)
            out_ref[2 * there + (here % 2 ^ half)] = (middle + mod_ref[5:6, :] * update).astype(
                BF16
            )


def call(body, operands, outs, scratch=(), limit=24, flops=1):
    return pl.pallas_call(
        body,
        out_shape=outs,
        in_specs=[pl.BlockSpec(memory_space=pltpu.VMEM)] * len(operands),
        out_specs=[pl.BlockSpec(memory_space=pltpu.VMEM)] * len(outs),
        scratch_shapes=list(scratch),
        compiler_params=pltpu.CompilerParams(vmem_limit_bytes=limit * MIB),
        cost_estimate=pl.CostEstimate(flops=flops, bytes_accessed=1, transcendentals=0),
    )(*operands)


def swap(value, axis, offset):
    size = lax.axis_size(axis)
    return lax.ppermute(value, axis, [(at, at ^ offset) for at in range(size)])


def after(value, *others):
    return lax.optimization_barrier((value, *others))[0]


def across(value):
    size = lax.axis_size("patch")
    return [swap(value, "patch", at) if at else value for at in range(0, size, 2)]


def both_cores(blocks):
    return [part for block in blocks for part in (block, swap(block, "patch", 1))]


def swap_diagonal(value, offset):
    frames, size = lax.axis_size("frame"), lax.axis_size("patch")
    pairs = [
        (frame * size + at, (frame ^ 1) * size + (at ^ offset))
        for frame in range(frames)
        for at in range(size)
    ]
    return lax.ppermute(value, ("frame", "patch"), pairs)


def per_device(tokens, modulation, spatial_qkv, spatial_out, temporal_qkv, temporal_out):
    _, rows, width = tokens.shape
    shard = spatial_out.shape[0]
    count, frames = lax.axis_size("patch"), lax.axis_size("frame")
    period = rows // frames
    pieces, groups = frames // 2, count // 2
    shape = jax.ShapeDtypeStruct

    def with_sister(weights, *others):
        return [weights, swap(after(weights, *others), "patch", 1)]

    def exchange_frames(parts):
        offsets = reversed(range(pieces))
        return [swap(part, "frame", 2 * at) if at else part for at, part in zip(offsets, parts)]

    def project_paired(sent, weights):
        heads = swap(sent, "frame", 1)
        return call(paired_kernel, (heads, *weights), [halves_shape(F32)])[0]

    def return_updates(own, far):
        diagonal = [swap_diagonal(part, 2 * at) for at, part in enumerate(far[1::2], 1)]
        same = [swap(part, "patch", 2 * at) for at, part in enumerate(far[::2], 1)]
        return [own[0], *same, own[1], *diagonal]

    def halves_shape(dtype):
        return shape((rows // 2, width), dtype)

    own_shapes = [halves_shape(F32), shape((rows // 2, 2 * shard), BF16)]
    far_shapes = [halves_shape(BF16)] * (2 * groups - 2)
    piece_shapes = [shape((2 * period, width), BF16)] * pieces

    sister = swap(tokens, "patch", 1)
    far = across(tokens)[1:]
    (near,) = call(
        near_kernel,
        (modulation, spatial_qkv, tokens, sister),
        [shape((3 * shard, 2 * rows), F32)],
    )
    own_tokens, shared = call(
        functools.partial(share_kernel, period), (after(tokens, sister),), [halves_shape(BF16)] * 2
    )
    paired = swap(shared, "frame", 1)
    far = both_cores([after(block, near, paired) for block in far])
    out_pair = with_sister(spatial_out, *far)

    columns = (groups - 1) * rows
    far_proj, kept, sent = call(
        far_queries_kernel,
        (modulation, spatial_qkv, near, *far),
        [shape((3 * shard, 2 * columns), F32)] + [shape((shard, columns), BF16)] * 2,
        [pltpu.VMEM((shard, 2 * columns), F32)],
    )
    far_parts = call(
        functools.partial(far_partial_kernel, period),
        (kept, swap(sent, "patch", 1), *out_pair),
        far_shapes,
    )
    temporal_pair = with_sister(temporal_qkv, far_parts[0])
    kept, sent = call(
        near_queries_kernel,
        (after(near, far_parts[0]), far_proj),
        [shape((shard, rows), BF16)] * 2,
        [pltpu.VMEM((shard, 2 * rows), F32)],
        flops=1,
    )
    received = swap(sent, "patch", 1)
    own_parts = call(
        functools.partial(near_partial_kernel, period), (kept, received, *out_pair), own_shapes
    )
    late_pair = with_sister(temporal_out, received)
    updates = return_updates((own_parts[0], project_paired(own_parts[1], out_pair)), far_parts)
    sums = call(
        functools.partial(far_sum_kernel, groups - 1),
        (*updates[1:groups], *updates[groups + 1 :]),
        [halves_shape(F32)] * 2,
        flops=4_000_000_000,
    )
    updates = [updates[0], sums[0], updates[groups], sums[1]]
    middle, middle_sent, *parts = call(
        functools.partial(middle_kernel, pieces),
        (modulation, own_tokens, paired, *updates),
        [shape((pieces, period, width), BF16)] * 2 + piece_shapes,
        [pltpu.VMEM((pieces, 2 * period, width), BF16)],
    )
    arrived = exchange_frames(parts)
    (segment,) = call(join_kernel, arrived, [shape((rows, width), BF16)])
    segments = across(segment)

    def attend_frames(own, segments, shapes):
        columns = len(segments) * rows
        return call(
            functools.partial(temporal_kernel, own, period, rows),
            (*temporal_pair, *late_pair, *segments),
            shapes,
            [pltpu.VMEM((6 * shard, columns), F32), pltpu.VMEM((2 * shard, columns), F32)],
        )

    kept, sent = attend_frames(True, [segment], own_shapes)
    received = project_paired(sent, late_pair)
    middle_other = swap(after(middle_sent, segment), "frame", 1)
    others = [after(block, received) for block in segments[1:]]
    far_parts = attend_frames(False, others, far_shapes)
    updates = return_updates((kept, received), far_parts)
    parts = call(
        functools.partial(sum_kernel, groups),
        updates,
        piece_shapes,
    )
    (result,) = call(
        functools.partial(result_kernel, pieces),
        (modulation, middle, middle_other, *exchange_frames(parts)),
        [shape((frames, period, width), BF16)],
    )
    return result.reshape(1, rows, width)


def solution(mesh):
    in_specs = (
        P("frame", "patch", None),
        P(),
        P("patch", None),
        P("patch", None),
        P("patch", None),
        P("patch", None),
    )
    out_specs = P("frame", "patch", None)
    return jax.shard_map(
        per_device, mesh=mesh, in_specs=in_specs, out_specs=out_specs, check_vma=False
    )
```

```python
import functools

import jax
import jax.numpy as jnp
from jax import lax
from jax.experimental import pallas as pl
from jax.experimental.pallas import tpu as pltpu
from jax.sharding import PartitionSpec as P

HD = 72
MIB = 1 << 20
LOG2E = 1.4426950408889634
F32 = jnp.float32
BF16 = jnp.bfloat16


def norm_rows(values, shift, scale):
    average = jnp.mean(values, axis=-1, keepdims=True)
    centred = values - average
    variance = jnp.mean(centred * centred, axis=-1, keepdims=True)
    normed = centred * lax.rsqrt(variance + 1e-06)
    return (normed * (1.0 + shift * 0.0 + scale) + shift).astype(BF16)


def dot(left, right, left_dim=1, right_dim=0):
    return lax.dot_general(
        left, right, (((left_dim,), (right_dim,)), ((), ())), preferred_element_type=F32
    )


def soften(scores):
    top = jnp.max(scores, axis=0, keepdims=True)
    return jnp.exp2((scores - top) * (HD**-0.5 * LOG2E)).astype(BF16)


def mix(values, weights):
    ones = jnp.ones((8, values.shape[1]), F32)
    mixed = dot(jnp.concatenate([values, ones], axis=0).astype(BF16), weights)
    return mixed[:HD] * (1.0 / mixed[HD : HD + 1])


def project(mod_ref, weight_ref, token_refs, proj_ref):
    shift, scale = mod_ref[0:1, :], mod_ref[1:2, :]
    block = token_refs[0].shape[1]
    for at in range(0, len(token_refs), 2):
        rows = [norm_rows(ref[0].astype(F32), shift, scale) for ref in token_refs[at : at + 2]]
        rows = jnp.concatenate(rows, axis=0)
        proj_ref[:, at * block : (at + 2) * block] = dot(weight_ref[...], rows, 1, 1)


def near_kernel(mod_ref, weight_ref, own_ref, sister_ref, proj_ref):
    project(mod_ref, weight_ref, (own_ref, sister_ref), proj_ref)


def spatial_kernel(count, mod_ref, weight_ref, near_ref, *refs):
    token_refs, (kept_ref, sent_ref, far_ref, heads_ref) = refs[: count - 2], refs[count - 2 :]
    block = token_refs[0].shape[1]
    heads = weight_ref.shape[0] // (3 * HD)
    project(mod_ref, weight_ref, token_refs, far_ref)

    def whole(start):
        return jnp.concatenate([ref[start : start + HD, :] for ref in (near_ref, far_ref)], axis=1)

    def score(head, at):
        base = head * 3 * HD
        source, start = (near_ref, 0) if at == 0 else (far_ref, (at - 2) * block)
        query = source[base : base + HD, start : start + 2 * block].astype(BF16)
        return dot(whole(base + HD).astype(BF16).T, query)

    steps = [(head, at) for head in range(heads) for at in range(0, count, 2)]
    scores = score(*steps[0])
    for (head, at), later in zip(steps, [*steps[1:], None]):
        coming = score(*later) if later else None
        rows, cols = slice(head * HD, (head + 1) * HD), slice(at * block, (at + 2) * block)
        heads_ref[rows, cols] = mix(whole(head * 3 * HD + 2 * HD), soften(scores))
        scores = coming
    for at in range(count):
        out_ref = (kept_ref, sent_ref)[at % 2]
        cols = slice(at // 2 * block, (at // 2 + 1) * block)
        out_ref[:, cols] = heads_ref[:, at * block : (at + 1) * block].astype(BF16)


def halves(value, size):
    return [
        jnp.concatenate(
            [value[at : at + size] for at in range(first * size, value.shape[0], 2 * size)], axis=0
        )
        for first in range(2)
    ]


def of_this_half(value, size):
    even, odd = (half.astype(F32) for half in halves(value, size))
    first = lax.axis_index("frame") % 2 == 0
    return jnp.where(first, even, odd), jnp.where(first, odd, even)


def share_kernel(period, token_ref, kept_ref, sent_ref):
    for ref, half in zip((kept_ref, sent_ref), of_this_half(token_ref[0], period)):
        ref[...] = half.astype(BF16)


def joined(refs):
    return jnp.concatenate([ref[...] for ref in refs], axis=0)


def partial_kernel(period, *refs):
    head_refs, weights, out_refs = refs[:2], joined(refs[2:4]), refs[4:]
    block = 2 * out_refs[0].shape[0]
    for at in range(len(out_refs) // 2):
        cols = slice(at * block, (at + 1) * block)
        heads = jnp.concatenate([ref[:, cols] for ref in head_refs], axis=0).T
        if at == 0:
            kept, sent = (half.astype(BF16) for half in of_this_half(heads, period))
            parts = dot(kept, weights), sent
        else:
            parts = of_this_half(dot(heads, weights), period)
        for ref, part in zip(out_refs[2 * at : 2 * at + 2], parts):
            ref[...] = part.astype(ref.dtype)


def paired_kernel(head_ref, *refs):
    refs[-1][...] = dot(head_ref[...], joined(refs[:-1]))


def total_updates(groups, refs):
    return [
        sum(ref[...].astype(F32) for ref in refs[at * groups : (at + 1) * groups])
        for at in range(2)
    ]


def middle_kernel(pieces, groups, mod_ref, own_ref, paired_ref, *refs):
    kept_ref, sent_ref, *piece_refs, scratch = refs[2 * groups :]
    updates = total_updates(groups, refs)
    _, period, width = kept_ref.shape
    inputs = (own_ref[...], paired_ref[...])
    for at, (tokens, middle_ref) in enumerate(zip(inputs, (kept_ref, sent_ref))):
        update = updates[at]
        middle = (tokens.astype(F32) + mod_ref[2:3, :] * update).astype(BF16)
        normed = norm_rows(middle.astype(F32), mod_ref[3:4, :], mod_ref[4:5, :])
        for piece in range(pieces):
            rows = slice(piece * period, (piece + 1) * period)
            middle_ref[piece] = middle[rows]
            scratch[piece, at * period : (at + 1) * period, :] = normed[rows]
    here = lax.axis_index("frame") // 2
    for at, ref in enumerate(piece_refs):
        ref[...] = scratch[here ^ (pieces - 1 - at)]


def join_kernel(*refs):
    size = refs[0].shape[0]
    for at, ref in enumerate(refs[:-1]):
        refs[-1][at * size : (at + 1) * size, :] = ref[...]


def temporal_kernel(own, period, block, *refs):
    weight_refs, output_refs, (proj_ref, heads_ref) = refs[:2], refs[2:4], refs[-2:]
    groups = proj_ref.shape[1] // block
    row_refs, update_refs = refs[4 : -2 - 2 * groups], refs[-2 - 2 * groups : -2]
    rows = jnp.concatenate([ref[...] for ref in row_refs], axis=0)
    depth = weight_refs[0].shape[0]
    for core in range(2):
        proj_ref[core * depth : (core + 1) * depth, :] = dot(weight_refs[core][...], rows, 1, 1)
    heads = 2 * depth // (3 * HD)
    key_patch = lax.broadcasted_iota(jnp.int32, (block, block), 0) % period
    query_patch = lax.broadcasted_iota(jnp.int32, (block, block), 1) % period
    mask = key_patch == query_patch
    weights = joined(output_refs)
    for group in range(groups):
        cols = slice(group * block, (group + 1) * block)

        def part(head, at):
            start = (head * 3 + at) * HD
            return proj_ref[start : start + HD, cols]

        scores = []
        for head in range(heads):
            keys, query = part(head, 1).astype(BF16).T, part(head, 0).astype(BF16)
            scores.append(jnp.where(mask, dot(keys, query), -1e30))
        soft = soften(jnp.concatenate(scores, axis=1))
        for head in range(heads):
            mixed = mix(part(head, 2), soft[:, head * block : (head + 1) * block])
            heads_ref[head * HD : (head + 1) * HD, cols] = mixed
        mixed = heads_ref[:, cols].astype(BF16).T
        if own:
            kept, sent = halves(mixed, period)
            parts = dot(kept, weights), sent
        else:
            parts = halves(dot(mixed, weights), period)
        for ref, half in zip(update_refs[2 * group : 2 * group + 2], parts):
            ref[...] = half.astype(ref.dtype)


def sum_kernel(groups, *refs):
    piece_refs = refs[2 * groups :]
    period = piece_refs[0].shape[0] // 2
    for at, update in enumerate(total_updates(groups, refs)):
        update = update.astype(BF16)
        for piece, ref in enumerate(piece_refs):
            rows = update[piece * period : (piece + 1) * period]
            ref[at * period : (at + 1) * period, :] = rows


def result_kernel(pieces, mod_ref, kept_ref, other_ref, *refs):
    piece_refs, out_ref = refs[:-1], refs[-1]
    period = kept_ref.shape[1]
    here = lax.axis_index("frame")
    for at, ref in enumerate(piece_refs):
        there = here // 2 ^ (pieces - 1 - at)
        for half, middle_ref in enumerate((kept_ref, other_ref)):
            update = ref[half * period : (half + 1) * period, :].astype(F32)
            middle = middle_ref[there].astype(F32)
            out_ref[2 * there + (here % 2 ^ half)] = (middle + mod_ref[5:6, :] * update).astype(
                BF16
            )


def call(body, operands, outs, scratch=(), limit=24):
    return pl.pallas_call(
        body,
        out_shape=outs,
        in_specs=[pl.BlockSpec(memory_space=pltpu.VMEM)] * len(operands),
        out_specs=[pl.BlockSpec(memory_space=pltpu.VMEM)] * len(outs),
        scratch_shapes=list(scratch),
        compiler_params=pltpu.CompilerParams(vmem_limit_bytes=limit * MIB),
        cost_estimate=pl.CostEstimate(flops=1, bytes_accessed=1, transcendentals=0),
    )(*operands)


def swap(value, axis, offset):
    size = lax.axis_size(axis)
    return lax.ppermute(value, axis, [(at, at ^ offset) for at in range(size)])


def after(value, *others):
    return lax.optimization_barrier((value, *others))[0]


def across(value):
    size = lax.axis_size("patch")
    return [swap(value, "patch", at) if at else value for at in range(0, size, 2)]


def both_cores(blocks):
    return [part for block in blocks for part in (block, swap(block, "patch", 1))]


def swap_diagonal(value, offset):
    frames, size = lax.axis_size("frame"), lax.axis_size("patch")
    pairs = [
        (frame * size + at, (frame ^ 1) * size + (at ^ offset))
        for frame in range(frames)
        for at in range(size)
    ]
    return lax.ppermute(value, ("frame", "patch"), pairs)


def per_device(tokens, modulation, spatial_qkv, spatial_out, temporal_qkv, temporal_out):
    _, rows, width = tokens.shape
    shard = spatial_out.shape[0]
    count, frames = lax.axis_size("patch"), lax.axis_size("frame")
    period = rows // frames
    pieces, groups = frames // 2, count // 2
    shape = jax.ShapeDtypeStruct

    def with_sister(weights, *others):
        return [weights, swap(after(weights, *others), "patch", 1)]

    def exchange_frames(parts):
        offsets = reversed(range(pieces))
        return [swap(part, "frame", 2 * at) if at else part for at, part in zip(offsets, parts)]

    def project_paired(sent, weights):
        heads = swap(sent, "frame", 1)
        return call(paired_kernel, (heads, *weights), [halves_shape(F32)])[0]

    def return_updates(own, far):
        same = [swap(part, "patch", 2 * at) for at, part in enumerate(far[::2], 1)]
        diagonal = [swap_diagonal(part, 2 * at) for at, part in enumerate(far[1::2], 1)]
        return [own[0], *same, own[1], *diagonal]

    def halves_shape(dtype):
        return shape((rows // 2, width), dtype)

    own_shapes = [halves_shape(F32), shape((rows // 2, 2 * shard), BF16)]
    far_shapes = [halves_shape(BF16)] * (2 * groups - 2)
    piece_shapes = [shape((2 * period, width), BF16)] * pieces

    sister = swap(tokens, "patch", 1)
    far = across(tokens)[1:]
    (near,) = call(
        near_kernel,
        (modulation, spatial_qkv, tokens, sister),
        [shape((3 * shard, 2 * rows), F32)],
    )
    own_tokens, shared = call(
        functools.partial(share_kernel, period), (after(tokens, sister),), [halves_shape(BF16)] * 2
    )
    paired = swap(shared, "frame", 1)
    out_pair = with_sister(spatial_out, near)
    far = both_cores([after(block, near, paired) for block in far])
    temporal_pair = with_sister(temporal_qkv, *far)

    kept, sent = call(
        functools.partial(spatial_kernel, count),
        (modulation, spatial_qkv, near, *far),
        [shape((shard, groups * rows), BF16)] * 2,
        [pltpu.VMEM((3 * shard, (count - 2) * rows), F32), pltpu.VMEM((shard, count * rows), F32)],
    )
    parts = call(
        functools.partial(partial_kernel, period),
        (kept, swap(sent, "patch", 1), *out_pair),
        own_shapes + far_shapes,
    )
    late_pair = with_sister(temporal_out, parts[0])
    updates = return_updates((parts[0], project_paired(parts[1], out_pair)), parts[2:])
    middle, middle_sent, *parts = call(
        functools.partial(middle_kernel, pieces, groups),
        (modulation, own_tokens, paired, *updates),
        [shape((pieces, period, width), BF16)] * 2 + piece_shapes,
        [pltpu.VMEM((pieces, 2 * period, width), BF16)],
    )
    arrived = exchange_frames(parts)
    (segment,) = call(join_kernel, arrived, [shape((rows, width), BF16)])
    segments = across(segment)

    def attend_frames(own, segments, shapes):
        columns = len(segments) * rows
        return call(
            functools.partial(temporal_kernel, own, period, rows),
            (*temporal_pair, *late_pair, *segments),
            shapes,
            [pltpu.VMEM((6 * shard, columns), F32), pltpu.VMEM((2 * shard, columns), F32)],
        )

    kept, sent = attend_frames(True, [segment], own_shapes)
    received = project_paired(sent, late_pair)
    middle_other = swap(after(middle_sent, segment), "frame", 1)
    others = [after(block, received) for block in segments[1:]]
    far_parts = attend_frames(False, others, far_shapes)
    updates = return_updates((kept, received), far_parts)
    parts = call(
        functools.partial(sum_kernel, groups),
        updates,
        piece_shapes,
    )
    (result,) = call(
        functools.partial(result_kernel, pieces),
        (modulation, middle, middle_other, *exchange_frames(parts)),
        [shape((frames, period, width), BF16)],
    )
    return result.reshape(1, rows, width)


def solution(mesh):
    in_specs = (
        P("frame", "patch", None),
        P(),
        P("patch", None),
        P("patch", None),
        P("patch", None),
        P("patch", None),
    )
    out_specs = P("frame", "patch", None)
    return jax.shard_map(
        per_device, mesh=mesh, in_specs=in_specs, out_specs=out_specs, check_vma=False
    )
```

```python
import functools

import jax
import jax.numpy as jnp
from jax import lax
from jax.experimental import pallas as pl
from jax.experimental.pallas import tpu as pltpu
from jax.sharding import PartitionSpec as P

HD = 72
MIB = 1 << 20
LOG2E = 1.4426950408889634
F32 = jnp.float32
BF16 = jnp.bfloat16


def norm_rows(values, shift, scale):
    average = jnp.mean(values, axis=-1, keepdims=True)
    centred = values - average
    variance = jnp.mean(centred * centred, axis=-1, keepdims=True)
    normed = centred * lax.rsqrt(variance + 1e-06)
    return (normed * (1.0 + shift * 0.0 + scale) + shift).astype(BF16)


def dot(left, right, left_dim=1, right_dim=0):
    return lax.dot_general(
        left, right, (((left_dim,), (right_dim,)), ((), ())), preferred_element_type=F32
    )


def soften(scores):
    top = jnp.max(scores, axis=0, keepdims=True)
    return jnp.exp2((scores - top) * (HD**-0.5 * LOG2E)).astype(BF16)


def mix(values, weights):
    ones = jnp.ones((8, values.shape[1]), F32)
    mixed = dot(jnp.concatenate([values, ones], axis=0).astype(BF16), weights)
    return mixed[:HD] * (1.0 / mixed[HD : HD + 1])


def project(mod_ref, weight_ref, token_refs, proj_ref):
    shift, scale = mod_ref[0:1, :], mod_ref[1:2, :]
    block = token_refs[0].shape[1]
    for at in range(0, len(token_refs), 2):
        rows = [norm_rows(ref[0].astype(F32), shift, scale) for ref in token_refs[at : at + 2]]
        rows = jnp.concatenate(rows, axis=0)
        proj_ref[:, at * block : (at + 2) * block] = dot(weight_ref[...], rows, 1, 1)


def near_kernel(mod_ref, weight_ref, own_ref, sister_ref, proj_ref):
    project(mod_ref, weight_ref, (own_ref, sister_ref), proj_ref)


def spatial_kernel(count, mod_ref, weight_ref, near_ref, *refs):
    token_refs, (kept_ref, sent_ref, far_ref, heads_ref) = refs[: count - 2], refs[count - 2 :]
    block = token_refs[0].shape[1]
    heads = weight_ref.shape[0] // (3 * HD)
    project(mod_ref, weight_ref, token_refs, far_ref)

    def whole(start):
        return jnp.concatenate([ref[start : start + HD, :] for ref in (near_ref, far_ref)], axis=1)

    def score(head, at):
        base = head * 3 * HD
        source, start = (near_ref, 0) if at == 0 else (far_ref, (at - 2) * block)
        query = source[base : base + HD, start : start + 2 * block].astype(BF16)
        return dot(whole(base + HD).astype(BF16).T, query)

    steps = [(head, at) for head in range(heads) for at in range(0, count, 2)]
    scores = score(*steps[0])
    for (head, at), later in zip(steps, [*steps[1:], None]):
        coming = score(*later) if later else None
        rows, cols = slice(head * HD, (head + 1) * HD), slice(at * block, (at + 2) * block)
        heads_ref[rows, cols] = mix(whole(head * 3 * HD + 2 * HD), soften(scores))
        scores = coming
    for at in range(count):
        out_ref = (kept_ref, sent_ref)[at % 2]
        cols = slice(at // 2 * block, (at // 2 + 1) * block)
        out_ref[:, cols] = heads_ref[:, at * block : (at + 1) * block].astype(BF16)


def halves(value, size):
    return [
        jnp.concatenate(
            [value[at : at + size] for at in range(first * size, value.shape[0], 2 * size)], axis=0
        )
        for first in range(2)
    ]


def of_this_half(value, size):
    even, odd = (half.astype(F32) for half in halves(value, size))
    first = lax.axis_index("frame") % 2 == 0
    return jnp.where(first, even, odd), jnp.where(first, odd, even)


def share_kernel(period, token_ref, kept_ref, sent_ref):
    for ref, half in zip((kept_ref, sent_ref), of_this_half(token_ref[0], period)):
        ref[...] = half.astype(BF16)


def joined(refs):
    return jnp.concatenate([ref[...] for ref in refs], axis=0)


def partial_kernel(period, *refs):
    head_refs, weights, out_refs = refs[:2], joined(refs[2:4]), refs[4:]
    block = 2 * out_refs[0].shape[0]
    for at in range(len(out_refs) // 2):
        cols = slice(at * block, (at + 1) * block)
        heads = jnp.concatenate([ref[:, cols] for ref in head_refs], axis=0).T
        if at == 0:
            kept, sent = (half.astype(BF16) for half in of_this_half(heads, period))
            parts = dot(kept, weights), sent
        else:
            parts = of_this_half(dot(heads, weights), period)
        for ref, part in zip(out_refs[2 * at : 2 * at + 2], parts):
            ref[...] = part.astype(ref.dtype)


def paired_kernel(head_ref, *refs):
    refs[-1][...] = dot(head_ref[...], joined(refs[:-1]))


def total_updates(groups, refs):
    return [
        sum(ref[...].astype(F32) for ref in refs[at * groups : (at + 1) * groups])
        for at in range(2)
    ]


def middle_kernel(pieces, groups, mod_ref, own_ref, paired_ref, *refs):
    kept_ref, sent_ref, *piece_refs, scratch = refs[2 * groups :]
    updates = total_updates(groups, refs)
    _, period, width = kept_ref.shape
    inputs = (own_ref[...], paired_ref[...])
    for at, (tokens, middle_ref) in enumerate(zip(inputs, (kept_ref, sent_ref))):
        update = updates[at]
        middle = (tokens.astype(F32) + mod_ref[2:3, :] * update).astype(BF16)
        normed = norm_rows(middle.astype(F32), mod_ref[3:4, :], mod_ref[4:5, :])
        for piece in range(pieces):
            rows = slice(piece * period, (piece + 1) * period)
            middle_ref[piece] = middle[rows]
            scratch[piece, at * period : (at + 1) * period, :] = normed[rows]
    here = lax.axis_index("frame") // 2
    for at, ref in enumerate(piece_refs):
        ref[...] = scratch[here ^ (pieces - 1 - at)]


def join_kernel(*refs):
    size = refs[0].shape[0]
    for at, ref in enumerate(refs[:-1]):
        refs[-1][at * size : (at + 1) * size, :] = ref[...]


def temporal_kernel(own, period, block, *refs):
    weight_refs, output_refs, (proj_ref, heads_ref) = refs[:2], refs[2:4], refs[-2:]
    groups = proj_ref.shape[1] // block
    row_refs, update_refs = refs[4 : -2 - 2 * groups], refs[-2 - 2 * groups : -2]
    rows = jnp.concatenate([ref[...] for ref in row_refs], axis=0)
    depth = weight_refs[0].shape[0]
    for core in range(2):
        proj_ref[core * depth : (core + 1) * depth, :] = dot(weight_refs[core][...], rows, 1, 1)
    heads = 2 * depth // (3 * HD)
    key_patch = lax.broadcasted_iota(jnp.int32, (block, block), 0) % period
    query_patch = lax.broadcasted_iota(jnp.int32, (block, block), 1) % period
    mask = key_patch == query_patch
    weights = joined(output_refs)
    for group in range(groups):
        cols = slice(group * block, (group + 1) * block)

        def part(head, at):
            start = (head * 3 + at) * HD
            return proj_ref[start : start + HD, cols]

        scores = []
        for head in range(heads):
            keys, query = part(head, 1).astype(BF16).T, part(head, 0).astype(BF16)
            scores.append(jnp.where(mask, dot(keys, query), -1e30))
        soft = soften(jnp.concatenate(scores, axis=1))
        for head in range(heads):
            mixed = mix(part(head, 2), soft[:, head * block : (head + 1) * block])
            heads_ref[head * HD : (head + 1) * HD, cols] = mixed
        mixed = heads_ref[:, cols].astype(BF16).T
        if own:
            kept, sent = halves(mixed, period)
            parts = dot(kept, weights), sent
        else:
            parts = halves(dot(mixed, weights), period)
        for ref, half in zip(update_refs[2 * group : 2 * group + 2], parts):
            ref[...] = half.astype(ref.dtype)


def sum_kernel(groups, *refs):
    piece_refs = refs[2 * groups :]
    period = piece_refs[0].shape[0] // 2
    for at, update in enumerate(total_updates(groups, refs)):
        update = update.astype(BF16)
        for piece, ref in enumerate(piece_refs):
            rows = update[piece * period : (piece + 1) * period]
            ref[at * period : (at + 1) * period, :] = rows


def result_kernel(pieces, mod_ref, kept_ref, other_ref, *refs):
    piece_refs, out_ref = refs[:-1], refs[-1]
    period = kept_ref.shape[1]
    here = lax.axis_index("frame")
    for at, ref in enumerate(piece_refs):
        there = here // 2 ^ (pieces - 1 - at)
        for half, middle_ref in enumerate((kept_ref, other_ref)):
            update = ref[half * period : (half + 1) * period, :].astype(F32)
            middle = middle_ref[there].astype(F32)
            out_ref[2 * there + (here % 2 ^ half)] = (middle + mod_ref[5:6, :] * update).astype(
                BF16
            )


def call(body, operands, outs, scratch=(), limit=24):
    return pl.pallas_call(
        body,
        out_shape=outs,
        in_specs=[pl.BlockSpec(memory_space=pltpu.VMEM)] * len(operands),
        out_specs=[pl.BlockSpec(memory_space=pltpu.VMEM)] * len(outs),
        scratch_shapes=list(scratch),
        compiler_params=pltpu.CompilerParams(vmem_limit_bytes=limit * MIB),
        cost_estimate=pl.CostEstimate(flops=1, bytes_accessed=1, transcendentals=0),
    )(*operands)


def swap(value, axis, offset):
    size = lax.axis_size(axis)
    return lax.ppermute(value, axis, [(at, at ^ offset) for at in range(size)])


def after(value, *others):
    return lax.optimization_barrier((value, *others))[0]


def across(value):
    size = lax.axis_size("patch")
    return [swap(value, "patch", at) if at else value for at in range(0, size, 2)]


def both_cores(blocks):
    return [part for block in blocks for part in (block, swap(block, "patch", 1))]


def swap_diagonal(value, offset):
    frames, size = lax.axis_size("frame"), lax.axis_size("patch")
    pairs = [
        (frame * size + at, (frame ^ 1) * size + (at ^ offset))
        for frame in range(frames)
        for at in range(size)
    ]
    return lax.ppermute(value, ("frame", "patch"), pairs)


def per_device(tokens, modulation, spatial_qkv, spatial_out, temporal_qkv, temporal_out):
    _, rows, width = tokens.shape
    shard = spatial_out.shape[0]
    count, frames = lax.axis_size("patch"), lax.axis_size("frame")
    period = rows // frames
    pieces, groups = frames // 2, count // 2
    shape = jax.ShapeDtypeStruct

    def with_sister(weights, *others):
        return [weights, swap(after(weights, *others), "patch", 1)]

    def exchange_frames(parts):
        offsets = reversed(range(pieces))
        return [swap(part, "frame", 2 * at) if at else part for at, part in zip(offsets, parts)]

    def project_paired(sent, weights):
        heads = swap(sent, "frame", 1)
        return call(paired_kernel, (heads, *weights), [halves_shape(F32)])[0]

    def return_updates(own, far):
        same = [swap(part, "patch", 2 * at) for at, part in enumerate(far[::2], 1)]
        diagonal = [swap_diagonal(part, 2 * at) for at, part in enumerate(far[1::2], 1)]
        return [own[0], *same, own[1], *diagonal]

    def halves_shape(dtype):
        return shape((rows // 2, width), dtype)

    own_shapes = [halves_shape(F32), shape((rows // 2, 2 * shard), BF16)]
    far_shapes = [halves_shape(BF16)] * (2 * groups - 2)
    piece_shapes = [shape((2 * period, width), BF16)] * pieces

    sister = swap(tokens, "patch", 1)
    far = across(tokens)[1:]
    (near,) = call(
        near_kernel,
        (modulation, spatial_qkv, tokens, sister),
        [shape((3 * shard, 2 * rows), F32)],
    )
    own_tokens, shared = call(
        functools.partial(share_kernel, period), (after(tokens, sister),), [halves_shape(BF16)] * 2
    )
    paired = swap(shared, "frame", 1)
    far = both_cores([after(block, near, paired) for block in far])
    out_pair = with_sister(spatial_out, *far)

    kept, sent = call(
        functools.partial(spatial_kernel, count),
        (modulation, spatial_qkv, near, *far),
        [shape((shard, groups * rows), BF16)] * 2,
        [pltpu.VMEM((3 * shard, (count - 2) * rows), F32), pltpu.VMEM((shard, count * rows), F32)],
    )
    parts = call(
        functools.partial(partial_kernel, period),
        (kept, swap(sent, "patch", 1), *out_pair),
        own_shapes + far_shapes,
    )
    late_pair = with_sister(temporal_out, parts[0])
    temporal_pair = with_sister(temporal_qkv, parts[0])
    updates = return_updates((parts[0], project_paired(parts[1], out_pair)), parts[2:])
    middle, middle_sent, *parts = call(
        functools.partial(middle_kernel, pieces, groups),
        (modulation, own_tokens, paired, *updates),
        [shape((pieces, period, width), BF16)] * 2 + piece_shapes,
        [pltpu.VMEM((pieces, 2 * period, width), BF16)],
    )
    arrived = exchange_frames(parts)
    (segment,) = call(join_kernel, arrived, [shape((rows, width), BF16)])
    segments = across(segment)

    def attend_frames(own, segments, shapes):
        columns = len(segments) * rows
        return call(
            functools.partial(temporal_kernel, own, period, rows),
            (*temporal_pair, *late_pair, *segments),
            shapes,
            [pltpu.VMEM((6 * shard, columns), F32), pltpu.VMEM((2 * shard, columns), F32)],
        )

    kept, sent = attend_frames(True, [segment], own_shapes)
    received = project_paired(sent, late_pair)
    middle_other = swap(after(middle_sent, segment), "frame", 1)
    others = [after(block, received) for block in segments[1:]]
    far_parts = attend_frames(False, others, far_shapes)
    updates = return_updates((kept, received), far_parts)
    parts = call(
        functools.partial(sum_kernel, groups),
        updates,
        piece_shapes,
    )
    (result,) = call(
        functools.partial(result_kernel, pieces),
        (modulation, middle, middle_other, *exchange_frames(parts)),
        [shape((frames, period, width), BF16)],
    )
    return result.reshape(1, rows, width)


def solution(mesh):
    in_specs = (
        P("frame", "patch", None),
        P(),
        P("patch", None),
        P("patch", None),
        P("patch", None),
        P("patch", None),
    )
    out_specs = P("frame", "patch", None)
    return jax.shard_map(
        per_device, mesh=mesh, in_specs=in_specs, out_specs=out_specs, check_vma=False
    )
```

```python
import functools

import jax
import jax.numpy as jnp
from jax import lax
from jax.experimental import pallas as pl
from jax.experimental.pallas import tpu as pltpu
from jax.sharding import PartitionSpec as P

HD = 72
MIB = 1 << 20
LOG2E = 1.4426950408889634
F32 = jnp.float32
BF16 = jnp.bfloat16


def norm_rows(values, shift, scale):
    average = jnp.mean(values, axis=-1, keepdims=True)
    centred = values - average
    variance = jnp.mean(centred * centred, axis=-1, keepdims=True)
    normed = centred * lax.rsqrt(variance + 1e-06)
    return (normed * (1.0 + shift * 0.0 + scale) + shift).astype(BF16)


def dot(left, right, left_dim=1, right_dim=0):
    return lax.dot_general(
        left, right, (((left_dim,), (right_dim,)), ((), ())), preferred_element_type=F32
    )


def soften(scores):
    top = jnp.max(scores, axis=0, keepdims=True)
    return jnp.exp2((scores - top) * (HD**-0.5 * LOG2E)).astype(BF16)


def mix(values, weights):
    ones = jnp.ones((8, values.shape[1]), F32)
    mixed = dot(jnp.concatenate([values, ones], axis=0).astype(BF16), weights)
    return mixed[:HD] * (1.0 / mixed[HD : HD + 1])


def project(mod_ref, weight_ref, token_refs, proj_ref):
    shift, scale = mod_ref[0:1, :], mod_ref[1:2, :]
    block = token_refs[0].shape[1]
    for at in range(0, len(token_refs), 2):
        rows = [norm_rows(ref[0].astype(F32), shift, scale) for ref in token_refs[at : at + 2]]
        rows = jnp.concatenate(rows, axis=0)
        proj_ref[:, at * block : (at + 2) * block] = dot(weight_ref[...], rows, 1, 1)


def near_kernel(mod_ref, weight_ref, own_ref, sister_ref, proj_ref):
    project(mod_ref, weight_ref, (own_ref, sister_ref), proj_ref)


def spatial_kernel(count, mod_ref, weight_ref, near_ref, *refs):
    token_refs, (kept_ref, sent_ref, far_ref, heads_ref) = refs[: count - 2], refs[count - 2 :]
    block = token_refs[0].shape[1]
    heads = weight_ref.shape[0] // (3 * HD)
    project(mod_ref, weight_ref, token_refs, far_ref)

    def whole(start):
        return jnp.concatenate([ref[start : start + HD, :] for ref in (near_ref, far_ref)], axis=1)

    def score(head, at):
        base = head * 3 * HD
        source, start = (near_ref, 0) if at == 0 else (far_ref, (at - 2) * block)
        query = source[base : base + HD, start : start + 2 * block].astype(BF16)
        return dot(whole(base + HD).astype(BF16).T, query)

    steps = [(head, at) for head in range(heads) for at in range(0, count, 2)]
    scores = score(*steps[0])
    for (head, at), later in zip(steps, [*steps[1:], None]):
        coming = score(*later) if later else None
        rows, cols = slice(head * HD, (head + 1) * HD), slice(at * block, (at + 2) * block)
        heads_ref[rows, cols] = mix(whole(head * 3 * HD + 2 * HD), soften(scores))
        scores = coming
    for at in range(count):
        out_ref = (kept_ref, sent_ref)[at % 2]
        cols = slice(at // 2 * block, (at // 2 + 1) * block)
        out_ref[:, cols] = heads_ref[:, at * block : (at + 1) * block].astype(BF16)


def halves(value, size):
    return [
        jnp.concatenate(
            [value[at : at + size] for at in range(first * size, value.shape[0], 2 * size)], axis=0
        )
        for first in range(2)
    ]


def of_this_half(value, size):
    even, odd = (half.astype(F32) for half in halves(value, size))
    first = lax.axis_index("frame") % 2 == 0
    return jnp.where(first, even, odd), jnp.where(first, odd, even)


def share_kernel(period, token_ref, kept_ref, sent_ref):
    for ref, half in zip((kept_ref, sent_ref), of_this_half(token_ref[0], period)):
        ref[...] = half.astype(BF16)


def joined(refs):
    return jnp.concatenate([ref[...] for ref in refs], axis=0)


def partial_kernel(period, *refs):
    head_refs, weights, out_refs = refs[:2], joined(refs[2:4]), refs[4:]
    block = 2 * out_refs[0].shape[0]
    for at in range(len(out_refs) // 2):
        cols = slice(at * block, (at + 1) * block)
        heads = jnp.concatenate([ref[:, cols] for ref in head_refs], axis=0).T
        if at == 0:
            kept, sent = (half.astype(BF16) for half in of_this_half(heads, period))
            parts = dot(kept, weights), sent
        else:
            parts = of_this_half(dot(heads, weights), period)
        for ref, part in zip(out_refs[2 * at : 2 * at + 2], parts):
            ref[...] = part.astype(ref.dtype)


def paired_kernel(head_ref, *refs):
    refs[-1][...] = dot(head_ref[...], joined(refs[:-1]))


def total_updates(groups, refs):
    return [
        sum(ref[...].astype(F32) for ref in refs[at * groups : (at + 1) * groups])
        for at in range(2)
    ]


def middle_kernel(pieces, groups, mod_ref, own_ref, paired_ref, *refs):
    kept_ref, sent_ref, *piece_refs, scratch = refs[2 * groups :]
    updates = total_updates(groups, refs)
    _, period, width = kept_ref.shape
    inputs = (own_ref[...], paired_ref[...])
    for at, (tokens, middle_ref) in enumerate(zip(inputs, (kept_ref, sent_ref))):
        update = updates[at]
        middle = (tokens.astype(F32) + mod_ref[2:3, :] * update).astype(BF16)
        normed = norm_rows(middle.astype(F32), mod_ref[3:4, :], mod_ref[4:5, :])
        for piece in range(pieces):
            rows = slice(piece * period, (piece + 1) * period)
            middle_ref[piece] = middle[rows]
            scratch[piece, at * period : (at + 1) * period, :] = normed[rows]
    here = lax.axis_index("frame") // 2
    for at, ref in enumerate(piece_refs):
        ref[...] = scratch[here ^ (pieces - 1 - at)]


def join_kernel(*refs):
    size = refs[0].shape[0]
    for at, ref in enumerate(refs[:-1]):
        refs[-1][at * size : (at + 1) * size, :] = ref[...]


def temporal_kernel(own, period, block, *refs):
    weight_refs, output_refs, (proj_ref, heads_ref) = refs[:2], refs[2:4], refs[-2:]
    groups = proj_ref.shape[1] // block
    row_refs, update_refs = refs[4 : -2 - 2 * groups], refs[-2 - 2 * groups : -2]
    rows = jnp.concatenate([ref[...] for ref in row_refs], axis=0)
    depth = weight_refs[0].shape[0]
    for core in range(2):
        proj_ref[core * depth : (core + 1) * depth, :] = dot(weight_refs[core][...], rows, 1, 1)
    heads = 2 * depth // (3 * HD)
    key_patch = lax.broadcasted_iota(jnp.int32, (block, block), 0) % period
    query_patch = lax.broadcasted_iota(jnp.int32, (block, block), 1) % period
    mask = key_patch == query_patch
    weights = joined(output_refs)
    for group in range(groups):
        cols = slice(group * block, (group + 1) * block)

        def part(head, at):
            start = (head * 3 + at) * HD
            return proj_ref[start : start + HD, cols]

        scores = []
        for head in range(heads):
            keys, query = part(head, 1).astype(BF16).T, part(head, 0).astype(BF16)
            scores.append(jnp.where(mask, dot(keys, query), -1e30))
        soft = soften(jnp.concatenate(scores, axis=1))
        for head in range(heads):
            mixed = mix(part(head, 2), soft[:, head * block : (head + 1) * block])
            heads_ref[head * HD : (head + 1) * HD, cols] = mixed
        mixed = heads_ref[:, cols].astype(BF16).T
        if own:
            kept, sent = halves(mixed, period)
            parts = dot(kept, weights), sent
        else:
            parts = halves(dot(mixed, weights), period)
        for ref, half in zip(update_refs[2 * group : 2 * group + 2], parts):
            ref[...] = half.astype(ref.dtype)


def sum_kernel(groups, *refs):
    piece_refs = refs[2 * groups :]
    period = piece_refs[0].shape[0] // 2
    for at, update in enumerate(total_updates(groups, refs)):
        update = update.astype(BF16)
        for piece, ref in enumerate(piece_refs):
            rows = update[piece * period : (piece + 1) * period]
            ref[at * period : (at + 1) * period, :] = rows


def result_kernel(pieces, mod_ref, kept_ref, other_ref, *refs):
    piece_refs, out_ref = refs[:-1], refs[-1]
    period = kept_ref.shape[1]
    here = lax.axis_index("frame")
    for at, ref in enumerate(piece_refs):
        there = here // 2 ^ (pieces - 1 - at)
        for half, middle_ref in enumerate((kept_ref, other_ref)):
            update = ref[half * period : (half + 1) * period, :].astype(F32)
            middle = middle_ref[there].astype(F32)
            out_ref[2 * there + (here % 2 ^ half)] = (middle + mod_ref[5:6, :] * update).astype(
                BF16
            )


def call(body, operands, outs, scratch=(), limit=24):
    return pl.pallas_call(
        body,
        out_shape=outs,
        in_specs=[pl.BlockSpec(memory_space=pltpu.VMEM)] * len(operands),
        out_specs=[pl.BlockSpec(memory_space=pltpu.VMEM)] * len(outs),
        scratch_shapes=list(scratch),
        compiler_params=pltpu.CompilerParams(vmem_limit_bytes=limit * MIB),
        cost_estimate=pl.CostEstimate(flops=1, bytes_accessed=1, transcendentals=0),
    )(*operands)


def swap(value, axis, offset):
    size = lax.axis_size(axis)
    return lax.ppermute(value, axis, [(at, at ^ offset) for at in range(size)])


def after(value, *others):
    return lax.optimization_barrier((value, *others))[0]


def across(value):
    size = lax.axis_size("patch")
    return [swap(value, "patch", at) if at else value for at in range(0, size, 2)]


def both_cores(blocks):
    return [part for block in blocks for part in (block, swap(block, "patch", 1))]


def swap_diagonal(value, offset):
    frames, size = lax.axis_size("frame"), lax.axis_size("patch")
    pairs = [
        (frame * size + at, (frame ^ 1) * size + (at ^ offset))
        for frame in range(frames)
        for at in range(size)
    ]
    return lax.ppermute(value, ("frame", "patch"), pairs)


def per_device(tokens, modulation, spatial_qkv, spatial_out, temporal_qkv, temporal_out):
    _, rows, width = tokens.shape
    shard = spatial_out.shape[0]
    count, frames = lax.axis_size("patch"), lax.axis_size("frame")
    period = rows // frames
    pieces, groups = frames // 2, count // 2
    shape = jax.ShapeDtypeStruct

    def with_sister(weights, *others):
        return [weights, swap(after(weights, *others), "patch", 1)]

    def exchange_frames(parts):
        offsets = reversed(range(pieces))
        return [swap(part, "frame", 2 * at) if at else part for at, part in zip(offsets, parts)]

    def project_paired(sent, weights):
        heads = swap(sent, "frame", 1)
        return call(paired_kernel, (heads, *weights), [halves_shape(F32)])[0]

    def return_updates(own, far):
        same = [swap(part, "patch", 2 * at) for at, part in enumerate(far[::2], 1)]
        diagonal = [swap_diagonal(part, 2 * at) for at, part in enumerate(far[1::2], 1)]
        return [own[0], *same, own[1], *diagonal]

    def halves_shape(dtype):
        return shape((rows // 2, width), dtype)

    own_shapes = [halves_shape(F32), shape((rows // 2, 2 * shard), BF16)]
    far_shapes = [halves_shape(BF16)] * (2 * groups - 2)
    piece_shapes = [shape((2 * period, width), BF16)] * pieces

    sister = swap(tokens, "patch", 1)
    far = across(tokens)[1:]
    (near,) = call(
        near_kernel,
        (modulation, spatial_qkv, tokens, sister),
        [shape((3 * shard, 2 * rows), F32)],
    )
    own_tokens, shared = call(
        functools.partial(share_kernel, period), (after(tokens, sister),), [halves_shape(BF16)] * 2
    )
    paired = swap(shared, "frame", 1)
    far = both_cores([after(block, near, paired) for block in far])
    out_pair = with_sister(spatial_out, *far)

    kept, sent = call(
        functools.partial(spatial_kernel, count),
        (modulation, spatial_qkv, near, *far),
        [shape((shard, groups * rows), BF16)] * 2,
        [pltpu.VMEM((3 * shard, (count - 2) * rows), F32), pltpu.VMEM((shard, count * rows), F32)],
    )
    parts = call(
        functools.partial(partial_kernel, period),
        (kept, swap(sent, "patch", 1), *out_pair),
        own_shapes + far_shapes,
    )
    late_pair = with_sister(temporal_out, parts[0])
    updates = return_updates((parts[0], project_paired(parts[1], out_pair)), parts[2:])
    middle, middle_sent, *parts = call(
        functools.partial(middle_kernel, pieces, groups),
        (modulation, own_tokens, paired, *updates),
        [shape((pieces, period, width), BF16)] * 2 + piece_shapes,
        [pltpu.VMEM((pieces, 2 * period, width), BF16)],
    )
    temporal_pair = with_sister(temporal_qkv, middle)
    arrived = exchange_frames(parts)
    (segment,) = call(join_kernel, arrived, [shape((rows, width), BF16)])
    segments = across(segment)

    def attend_frames(own, segments, shapes):
        columns = len(segments) * rows
        return call(
            functools.partial(temporal_kernel, own, period, rows),
            (*temporal_pair, *late_pair, *segments),
            shapes,
            [pltpu.VMEM((6 * shard, columns), F32), pltpu.VMEM((2 * shard, columns), F32)],
        )

    kept, sent = attend_frames(True, [segment], own_shapes)
    received = project_paired(sent, late_pair)
    middle_other = swap(after(middle_sent, segment), "frame", 1)
    others = [after(block, received) for block in segments[1:]]
    far_parts = attend_frames(False, others, far_shapes)
    updates = return_updates((kept, received), far_parts)
    parts = call(
        functools.partial(sum_kernel, groups),
        updates,
        piece_shapes,
    )
    (result,) = call(
        functools.partial(result_kernel, pieces),
        (modulation, middle, middle_other, *exchange_frames(parts)),
        [shape((frames, period, width), BF16)],
    )
    return result.reshape(1, rows, width)


def solution(mesh):
    in_specs = (
        P("frame", "patch", None),
        P(),
        P("patch", None),
        P("patch", None),
        P("patch", None),
        P("patch", None),
    )
    out_specs = P("frame", "patch", None)
    return jax.shard_map(
        per_device, mesh=mesh, in_specs=in_specs, out_specs=out_specs, check_vma=False
    )
```
